32 devices in a mesh: dp: 8 (over z, x), tensor: 4 (over y, core).
Axes of the slice: x: 2, y: 2, z: 4, core: 2. Of those that a mesh axis runs over, the one named last changes fastest.
Arguments:
- inputs: bfloat16 [8, 1024, 512], P('dp'), may hold values from -6 to 6
- memory: bfloat16 [8, 512, 512], P('dp'), may hold values from -6 to 6
- counts: int32 [8], P('dp'), may hold values from 341 to 1024, as said below
- attn_gain: float32 [512], replicated, may hold values from 0.5 to 1.5
- attn_shift: float32 [512], replicated, may hold values from -2 to 2
- w_query: bfloat16 [512, 512], P(None, 'tensor'), may hold values from -0.25 to 0.25
- w_key: bfloat16 [512, 512], P(None, 'tensor'), may hold values from -0.25 to 0.25
- w_value: bfloat16 [512, 512], P(None, 'tensor'), may hold values from -0.25 to 0.25
- w_pos: bfloat16 [512, 512], P(None, 'tensor'), may hold values from -0.25 to 0.25
- bias_u: float32 [8, 64], P('tensor'), may hold values from -4 to 4
- bias_v: float32 [8, 64], P('tensor'), may hold values from -4 to 4
- w_out: bfloat16 [512, 512], P('tensor'), may hold values from -1 to 1
- ffn_gain: float32 [512], replicated, may hold values from 0.5 to 1.5
- ffn_shift: float32 [512], replicated, may hold values from -2 to 2
- w_up: bfloat16 [512, 2048], P(None, 'tensor'), may hold values from -0.25 to 0.25
- up_bias: float32 [2048], P('tensor'), may hold values from -2 to 2
- w_down: bfloat16 [2048, 512], P('tensor'), may hold values from -0.125 to 0.125
- down_bias: float32 [512], replicated, may hold values from -2 to 2
- out_grad: bfloat16 [8, 1024, 512], P('dp'), may hold values from -6 to 6
Outputs:
- output: bfloat16 [8, 1024, 512], P('dp')
- input_grad: bfloat16 [8, 1024, 512], P('dp')
- grad_attn_gain: float32 [512], replicated
- grad_attn_shift: float32 [512], replicated
- grad_w_query: float32 [512, 512], P(None, 'tensor')
- grad_w_key: float32 [512, 512], P(None, 'tensor')
- grad_w_value: float32 [512, 512], P(None, 'tensor')
- grad_w_pos: float32 [512, 512], P(None, 'tensor')
- grad_bias_u: float32 [8, 64], P('tensor')
- grad_bias_v: float32 [8, 64], P('tensor')
- grad_w_out: float32 [512, 512], P('tensor')
- grad_ffn_gain: float32 [512], replicated
- grad_ffn_shift: float32 [512], replicated
- grad_w_up: float32 [512, 2048], P(None, 'tensor')
- grad_up_bias: float32 [2048], P('tensor')
- grad_w_down: float32 [2048, 512], P('tensor')
- grad_down_bias: float32 [512], replicated
The draws below stay inside these ranges and needn't reach their ends.
Inputs may be any that keep to these rules, and one draw needn't show every extreme that they name: Each entry counts the live leading rows of its sequence; one sequence in every draw has all 1024 rows live.
All inputs are finite; a program needn't handle non-finite values.
Results may differ from the reference program's by a relative error of at most 0.024.
Values may be sent and summed in bfloat16 or wider, within the bound.
No kernel may reach another device: no remote copies, remote signals or barrier semaphores. Data moves between devices by JAX's collectives and lax.ppermute only.
A program may use at most 192 MiB of HBM per device.

```python
import jax
import jax.numpy as jnp
from jax import lax

D = 512
HEADS = 8
HEAD = 64
FF = 2048
MEM = 512
SEQ_LEN = 1024
SEQS = 8
N_TENSOR = 4


def draw_counts(key, part):
    key = jax.random.fold_in(key, 7)
    first_key, second_key = jax.random.split(key)
    base = jax.random.randint(first_key, (SEQS,), SEQ_LEN // 3, SEQ_LEN + 1)
    chosen = jax.random.randint(second_key, (), 0, SEQS)
    return jnp.where(jnp.arange(SEQS) == chosen, SEQ_LEN, base).astype(jnp.int32)


def level_of(stream_key, dims, cuts, smallest, high):
    loudness = 1.0
    for dim, parts in cuts:
        steps = jax.random.uniform(jax.random.fold_in(jax.random.fold_in(stream_key, 6), dim), (parts,), jnp.float32, smallest / len(cuts), high / len(cuts))
        loudness = loudness * jnp.repeat(jnp.exp(steps), dims[dim] // parts).reshape((-1,) + (1,) * (len(dims) - 1 - dim))
    return loudness


def bell_draw(own_key, dims, deviation, reach, cuts=(), held_as=jnp.bfloat16):
    drawn = deviation * jax.random.normal(own_key, dims, jnp.float32)
    if cuts:
        drawn = drawn * level_of(own_key, dims, cuts, -0.22, 0.18)
    return jnp.clip(drawn, -reach, reach).astype(held_as)


def setup_inputs(seed: int = 0) -> dict:
    seeds = jax.random.split(jax.random.key(seed), 20)
    return {
        "inputs": bell_draw(seeds[0], (SEQS, SEQ_LEN, D), 1.0, 6.0, ((0, 8),)),
        "memory": bell_draw(seeds[1], (SEQS, MEM, D), 1.0, 6.0, ((0, 8),)),
        "counts": draw_counts(jax.random.fold_in(seeds[19], 71), 0),
        "attn_gain": jnp.clip(1.0 + 0.1 * jax.random.normal(seeds[3], (D,), jnp.float32), 0.5, 1.5),
        "attn_shift": bell_draw(seeds[4], (D,), 0.3, 2.0, (), jnp.float32),
        "w_query": bell_draw(seeds[5], (D, HEADS * HEAD), D ** -0.5, 0.25, ((1, 4),)),
        "w_key": bell_draw(seeds[6], (D, HEADS * HEAD), D ** -0.5, 0.25, ((1, 4),)),
        "w_value": bell_draw(seeds[7], (D, HEADS * HEAD), D ** -0.5, 0.25, ((1, 4),)),
        "w_pos": bell_draw(seeds[8], (D, HEADS * HEAD), D ** -0.5, 0.25, ((1, 4),)),
        "bias_u": bell_draw(seeds[9], (HEADS, HEAD), 1.0, 4.0, ((0, 4),), jnp.float32),
        "bias_v": bell_draw(seeds[10], (HEADS, HEAD), 1.0, 4.0, ((0, 4),), jnp.float32),
        "w_out": bell_draw(seeds[11], (HEADS * HEAD, D), (HEADS * HEAD // 16) ** -0.5, 1.0, ((0, 4),)),
        "ffn_gain": jnp.clip(1.0 + 0.1 * jax.random.normal(seeds[12], (D,), jnp.float32), 0.5, 1.5),
        "ffn_shift": bell_draw(seeds[13], (D,), 0.3, 2.0, (), jnp.float32),
        "w_up": bell_draw(seeds[14], (D, FF), D ** -0.5, 0.25, ((1, 4),)),
        "up_bias": bell_draw(seeds[15], (FF,), 0.3, 2.0, ((0, 4),), jnp.float32),
        "w_down": bell_draw(seeds[16], (FF, D), FF ** -0.5, 0.125, ((0, 4),)),
        "down_bias": bell_draw(seeds[17], (D,), 0.3, 2.0, (), jnp.float32),
        "out_grad": bell_draw(seeds[18], (SEQS, SEQ_LEN, D), 1.0, 6.0, ((0, 8),)),
    }


eps_norm = 1e-05
neg_fill = -1e+30

@jax.custom_vjp
def low(v):
    return lax.optimization_barrier(v.astype(jnp.bfloat16)).astype(jnp.float32)

@jax.custom_vjp
def low_back(v):
    return v

def low_keep(v):
    return (low(v), None)

def low_pass(kept, grad):
    return (grad,)

def back_keep(v):
    return (v, None)

def back_low(kept, grad):
    return (low(grad),)
low.defvjp(low_keep, low_pass)
low_back.defvjp(back_keep, back_low)

def matmul(left, right):
    return jnp.dot(left, right, precision=lax.Precision.HIGHEST)

def layer_norm(rows, gain, shift):
    center = rows - lax.optimization_barrier(jnp.mean(rows, axis=-1, keepdims=True))
    spread = lax.optimization_barrier(jnp.mean(center * center, axis=-1, keepdims=True))
    return center * lax.rsqrt(spread + eps_norm) * gain + shift

def position_table(total, width):
    distance = (total - 1 - jnp.arange(total)).astype(jnp.float32)
    freq_rows = 1.0 / 10000.0 ** (jnp.arange(0, width, 2).astype(jnp.float32) / width)
    phase = distance[:, None] * freq_rows[None, :]
    return jnp.concatenate([jnp.sin(phase), jnp.cos(phase)], axis=1)

def skew_rows(raw, start):
    rows, keys = raw.shape
    padded = jnp.concatenate([raw, jnp.zeros((rows, 1), raw.dtype)], axis=1).reshape(-1)
    padded = jnp.concatenate([padded, jnp.zeros((keys,), raw.dtype)])
    return lax.dynamic_slice_in_dim(padded, start, rows * keys).reshape(rows, keys)

def block_context(query_u, query_v, keys, values, rel_group, count, first, scale):
    rows = query_u.shape[0]
    total = keys.shape[0]
    content = jnp.einsum('bhd,khd->hbk', query_u, keys, precision=lax.Precision.HIGHEST)
    raw = jnp.einsum('bhd,khd->hbk', query_v, rel_group, precision=lax.Precision.HIGHEST)
    start = (SEQ_LEN - 1 - first).astype(jnp.int32)
    shifted = jax.vmap(lambda single: skew_rows(single, start))(raw)
    query_pos = first + jnp.arange(rows).astype(jnp.int32)
    key_pos = jnp.arange(total).astype(jnp.int32)
    allowed = (key_pos[None, :] <= MEM + query_pos[:, None]) & ((key_pos[None, :] < MEM) | (key_pos[None, :] - MEM < count))
    scores = jnp.where(allowed[None], low_back((content + shifted) * scale), neg_fill)
    probs = low(jax.nn.softmax(scores, axis=-1))
    return jnp.einsum('hbk,khd->bhd', probs, values, precision=lax.Precision.HIGHEST)

def forward(inputs, memory, counts, attn_gain, attn_shift, w_query, w_key, w_value, w_pos, bias_u, bias_v, w_out, ffn_gain, ffn_shift, w_up, up_bias, w_down, down_bias):
    groups = N_TENSOR
    local_heads = HEADS // groups
    local_width = local_heads * HEAD
    local_ff = FF // groups
    total = MEM + SEQ_LEN
    block = min(512, SEQ_LEN)
    blocks = SEQ_LEN // block
    scale = HEAD ** (-0.5)
    table = low(position_table(total, D))
    rel_keys = low_back(low(matmul(table, w_pos))).reshape(total, HEADS, HEAD)

    def one_sequence(carry, item):
        seq_rows, mem_rows, count = item
        normed = low(layer_norm(jnp.concatenate([mem_rows, seq_rows], axis=0), attn_gain, attn_shift))
        attn_total = jnp.zeros((SEQ_LEN, D), jnp.float32)
        for group in range(groups):
            col_span = slice(group * local_width, (group + 1) * local_width)
            head_span = slice(group * local_heads, (group + 1) * local_heads)
            normed_copy = low_back(normed)
            query = low_back(low(matmul(normed_copy[MEM:], w_query[:, col_span]))).reshape(SEQ_LEN, local_heads, HEAD)
            keys = low_back(low(matmul(normed_copy, w_key[:, col_span]))).reshape(total, local_heads, HEAD)
            values = low_back(low(matmul(normed_copy, w_value[:, col_span]))).reshape(total, local_heads, HEAD)
            query_u = low(query + bias_u[head_span]).reshape(blocks, block, local_heads, HEAD)
            query_v = low(query + bias_v[head_span]).reshape(blocks, block, local_heads, HEAD)
            rel_group = rel_keys[:, head_span]

            def one_block(block_id):
                block_id = block_id.astype(jnp.int32)
                return block_context(query_u[block_id], query_v[block_id], keys, values, rel_group, count, block_id * block, scale)
            context = lax.map(jax.checkpoint(one_block), jnp.arange(blocks).astype(jnp.int32))
            context = low_back(low(context.reshape(SEQ_LEN, local_width)))
            attn_total = attn_total + low(matmul(context, w_out[col_span, :]))
        hidden = seq_rows + low_back(attn_total)
        normed_two = low(layer_norm(hidden, ffn_gain, ffn_shift))
        ffn_total = jnp.zeros((SEQ_LEN, D), jnp.float32)
        for group in range(groups):
            unit_span = slice(group * local_ff, (group + 1) * local_ff)
            normed_copy = low_back(normed_two)
            pre_act = low_back(matmul(normed_copy, w_up[:, unit_span]) + up_bias[unit_span])
            activ = low(jax.nn.gelu(pre_act, approximate=False))
            ffn_total = ffn_total + low(matmul(activ, w_down[unit_span, :]))
        return (carry, hidden + low_back(ffn_total) + down_bias)
    start_carry = jnp.zeros((), jnp.float32)
    _, result = lax.scan(jax.checkpoint(one_sequence), start_carry, (inputs, memory, counts))
    return result

def reference(inputs, memory, counts, attn_gain, attn_shift, w_query, w_key, w_value, w_pos, bias_u, bias_v, w_out, ffn_gain, ffn_shift, w_up, up_bias, w_down, down_bias, out_grad):
    weights = [item.astype(jnp.float32) for item in (attn_gain, attn_shift, w_query, w_key, w_value, w_pos, bias_u, bias_v, w_out, ffn_gain, ffn_shift, w_up, up_bias, w_down, down_bias)]
    memory_f = memory.astype(jnp.float32)

    def wrapped(rows, *params):
        return forward(rows, memory_f, counts, *params)
    result, pull = jax.vjp(wrapped, inputs.astype(jnp.float32), *weights)
    grads = pull(out_grad.astype(jnp.float32))
    return (result.astype(jnp.bfloat16), grads[0].astype(jnp.bfloat16), grads[1], grads[2], grads[3], grads[4], grads[5], grads[6], grads[7], grads[8], grads[9], grads[10], grads[11], grads[12], grads[13], grads[14], grads[15])
```

```python
import functools

import jax
import jax.numpy as jnp
import numpy as np
from jax import lax
from jax.experimental import pallas as pl
from jax.experimental.pallas import tpu as pltpu
from jax.sharding import PartitionSpec as P

HEAD = 64
BF = jnp.bfloat16
FL = jnp.float32
eps_norm = 1e-05
neg_fill = -1e30
VMEM_LIMIT = 40 * 1024 * 1024


def mm(left, right):
    return lax.dot_general(left, right, (((1,), (0,)), ((), ())), preferred_element_type=FL)


def mm_t(left, right):
    return lax.dot_general(left, right, (((1,), (1,)), ((), ())), preferred_element_type=FL)


def t_mm(left, right):
    return lax.dot_general(left, right, (((0,), (0,)), ((), ())), preferred_element_type=FL)


def norm_parts(rows):
    center = rows - jnp.mean(rows, axis=-1, keepdims=True)
    spread = jnp.mean(center * center, axis=-1, keepdims=True)
    inv = lax.rsqrt(spread + eps_norm)
    return center * inv, inv


def head_lanes(heads):
    lane = lax.broadcasted_iota(jnp.int32, (1, heads * HEAD), 1)
    return [(lane >= h * HEAD) & (lane < (h + 1) * HEAD) for h in range(heads)]


def pick_heads(parts, lanes):
    out = parts[0]
    for part, lane in zip(parts[1:], lanes[1:]):
        out = jnp.where(lane, part, out)
    return out


def make_queries(normed, spots, at, refs, heads):
    wq_ref, wpos_ref, bu_ref, bv_ref, sin_ref, cos_ref, qb_ref, qv_ref = refs
    lanes = head_lanes(heads)
    wide = heads * HEAD
    scale = HEAD ** (-0.5)
    query = mm(normed, wq_ref[...]).astype(BF).astype(FL)
    query_u = (query + bu_ref[...]).astype(BF).astype(FL) * scale
    query_v = (query + bv_ref[...]).astype(BF).astype(FL) * scale
    qv_ref[at, :] = query_v.astype(BF)
    sin = sin_ref[spots, :]
    cos = cos_ref[spots, :]
    half = sin.shape[1]
    for h in range(heads):
        qb_ref[h, at, :wide] = jnp.where(lanes[h], query_u, 0.0).astype(BF)
        coef = mm_t(jnp.where(lanes[h], query_v, 0.0).astype(BF), wpos_ref[...])
        on_sin, on_cos = coef[:, :half], coef[:, half:]
        qb_ref[h, at, wide : wide + half] = (on_sin * sin + on_cos * cos).astype(BF)
        qb_ref[h, at, wide + half :] = (on_cos * sin - on_sin * cos).astype(BF)


def attend(first, block, mem_len, heads, refs):
    count_ref, core_ref, qb_ref, kt_ref, v_ref, wout_ref, probs_ref, ctx_ref, keep_ref, send_ref = refs
    count = count_ref[0]
    core = core_ref[0]
    lanes = head_lanes(heads)
    rows = qb_ref.shape[1]
    for part in range(rows // block):
        at = pl.ds(part * block, block)
        start = first + part * block
        seen = mem_len + start + block
        query_pos = start + lax.broadcasted_iota(jnp.int32, (block, 1), 0)
        limit = jnp.minimum(query_pos, count - 1)
        key_pos = lax.broadcasted_iota(jnp.int32, (block, seen - mem_len), 1)
        allowed = key_pos <= limit
        found = []
        for h in range(heads):
            scores = mm_t(qb_ref[h, at, :], kt_ref[:seen, :])
            scores = jnp.concatenate(
                [scores[:, :mem_len], jnp.where(allowed, scores[:, mem_len:], neg_fill)], axis=1
            )
            expo = jnp.exp(scores - jnp.max(scores, axis=-1, keepdims=True))
            probs = (expo * (1.0 / jnp.sum(expo, axis=-1, keepdims=True))).astype(BF)
            probs_ref[h, at, :seen] = probs
            found.append(mm(probs, v_ref[:seen, :]))
        context = pick_heads(found, lanes).astype(BF)
        ctx_ref[at, :] = context
        share = mm(context, wout_ref[...]).astype(BF)

        @pl.when(core == part)
        def _():
            keep_ref[...] = share

        @pl.when(core != part)
        def _():
            send_ref[...] = share


def front_kernel(
    first, block, heads,
    count_ref, core_ref, x_ref, mem_ref, gain_ref, shift_ref, wq_ref, wk_ref, wv_ref, wpos_ref,
    bu_ref, bv_ref, table_ref, sin_ref, cos_ref, wout_ref,
    normed_ref, kt_ref, v_ref, qb_ref, qv_ref, probs_ref, ctx_ref, keep_ref, send_ref,
):
    mem_len = mem_ref.shape[0]
    total = normed_ref.shape[0]
    wide = heads * HEAD
    weights = jnp.concatenate([wk_ref[...], wv_ref[...]], axis=1)
    for at in range(0, total, block):
        rows = mem_ref[at : at + block, :] if at < mem_len else x_ref[at - mem_len : at - mem_len + block, :]
        unit, _ = norm_parts(rows.astype(FL))
        normed = (unit * gain_ref[...] + shift_ref[...]).astype(BF)
        normed_ref[at : at + block, :] = normed
        pair = mm(normed, weights).astype(BF)
        kt_ref[at : at + block, :wide] = pair[:, :wide]
        kt_ref[at : at + block, wide:] = table_ref[at : at + block, :]
        v_ref[at : at + block, :] = pair[:, wide:]
        if at >= mem_len + first:
            make_queries(
                normed, pl.ds(at - mem_len, block), pl.ds(at - mem_len - first, block),
                (wq_ref, wpos_ref, bu_ref, bv_ref, sin_ref, cos_ref, qb_ref, qv_ref), heads,
            )
    attend(
        first, block, mem_len, heads,
        (count_ref, core_ref, qb_ref, kt_ref, v_ref, wout_ref, probs_ref, ctx_ref, keep_ref, send_ref),
    )


def second_kernel(
    first, block, heads, mem_len,
    count_ref, core_ref, normed_ref, kt_ref, v_ref, wq_ref, wpos_ref, bu_ref, bv_ref, sin_ref, cos_ref, wout_ref,
    qb_ref, qv_ref, probs_ref, ctx_ref, keep_ref, send_ref,
):
    for at in range(0, qb_ref.shape[1], block):
        normed = normed_ref[mem_len + first + at : mem_len + first + at + block, :]
        make_queries(
            normed, pl.ds(first + at, block), pl.ds(at, block),
            (wq_ref, wpos_ref, bu_ref, bv_ref, sin_ref, cos_ref, qb_ref, qv_ref), heads,
        )
    attend(
        first, block, mem_len, heads,
        (count_ref, core_ref, qb_ref, kt_ref, v_ref, wout_ref, probs_ref, ctx_ref, keep_ref, send_ref),
    )


def ordered(core, mine, other, part):
    return jnp.where(core == part, mine, other)


def ffn_kernel(
    first, block, last,
    core_ref, x_ref, mine_ref, other_ref, gain_ref, shift_ref, up_ref, upb_ref, down_ref, g_ref, *rest,
):
    if last:
        up_in, down_in, vec_in, upb_in = rest[:4]
        rest = rest[4:]
    keep_ref, send_ref, keep2_ref, send2_ref, up_out, down_out, vec_out, upb_out = rest
    core = core_ref[0]
    gain = gain_ref[...]
    up_sum = down_sum = None
    vecs = [0.0, 0.0, 0.0]
    upb = 0.0
    for part in range(2):
        at = slice(first + part * block, first + (part + 1) * block)
        attended = ordered(core, mine_ref[...].astype(FL), other_ref[...].astype(FL), part)
        unit, _ = norm_parts(x_ref[at, :].astype(FL) + attended)
        normed = (unit * gain + shift_ref[...]).astype(BF)
        pre = mm(normed, up_ref[...]) + upb_ref[...]
        cdf = 0.5 + 0.5 * lax.erf(pre * np.float32(0.5**0.5))
        activ = (pre * cdf).astype(BF)
        share = mm(activ, down_ref[...]).astype(BF)
        slope = cdf + pre * jnp.exp(-0.5 * pre * pre) * np.float32((2 * np.pi) ** -0.5)
        grads = g_ref[at, :]
        grad_pre = (mm_t(grads, down_ref[...]) * slope).astype(BF)
        back = mm_t(grad_pre, up_ref[...])
        back_b = back.astype(BF)

        @pl.when(core == part)
        def _():
            keep_ref[...] = share
            keep2_ref[...] = back_b

        @pl.when(core != part)
        def _():
            send_ref[...] = share
            send2_ref[...] = back_b

        down_new = t_mm(activ, grads)
        up_new = t_mm(normed, grad_pre)
        down_sum = down_new if part == 0 else down_sum + down_new
        up_sum = up_new if part == 0 else up_sum + up_new
        vecs[0] += jnp.sum(back * unit, axis=0, keepdims=True)
        vecs[1] += jnp.sum(back, axis=0, keepdims=True)
        vecs[2] += jnp.sum(grads.astype(FL), axis=0, keepdims=True)
        upb += jnp.sum(grad_pre.astype(FL), axis=0, keepdims=True)
    if last:
        up_sum = up_sum + up_in[...]
        down_sum = down_sum + down_in[...]
    up_out[...] = up_sum.astype(up_out.dtype)
    down_out[...] = down_sum.astype(down_out.dtype)
    for i, vec in enumerate(vecs):
        vec_out[i : i + 1, :] = vec + (vec_in[i : i + 1, :] if last else 0.0)
    upb_out[...] = upb + (upb_in[...] if last else 0.0)


def back_kernel(
    first, block, heads, mem_len, last,
    core_ref, x_ref, mine_ref, other_ref, gmine_ref, gother_ref, g_ref, fgain_ref, wout_ref, ctx_ref, probs_ref,
    qb_ref, qv_ref, kt_ref, v_ref, wpos_ref, sin_ref, cos_ref, normed_ref, wq_ref, wk_ref, wv_ref, *rest,
):
    if last:
        mem_ref, dk_in, dv_in, dpos_in, dout_in, dq_in, vec_in, bias_in = rest[:8]
        rest = rest[8:]
        gh_ref, keep_ref, send_ref, grads_ref, vec_ref, bias_ref, dk_ref, dv_ref, dpos_ref, dout_ref, dq_ref = rest
        dk_ref[...] = dk_in[...]
        dv_ref[...] = dv_in[...]
    else:
        gh_ref, keep_ref, send_ref, dk_ref, dv_ref, dpos_ref, dout_ref, dq_ref, vec_ref, bias_ref = rest
        dk_ref[...] = jnp.zeros(dk_ref.shape, FL)
        dv_ref[...] = jnp.zeros(dv_ref.shape, FL)
    core = core_ref[0]
    lanes = head_lanes(heads)
    wide = heads * HEAD
    half = sin_ref.shape[1]
    scale = HEAD ** (-0.5)
    rows = 2 * block
    dpos = dout = None
    bias_u = bias_v = 0.0
    for part in range(2):
        at = slice(part * block, (part + 1) * block)
        spots = slice(first + part * block, first + (part + 1) * block)
        seen = mem_len + first + (part + 1) * block
        attended = ordered(core, mine_ref[...].astype(FL), other_ref[...].astype(FL), part)
        unit, inv = norm_parts(x_ref[spots, :].astype(FL) + attended)
        scaled = ordered(core, gmine_ref[...].astype(FL), gother_ref[...].astype(FL), part) * fgain_ref[...]
        flat = jnp.mean(scaled, axis=-1, keepdims=True)
        along = jnp.mean(scaled * unit, axis=-1, keepdims=True)
        grad_hidden = g_ref[spots, :].astype(FL) + inv * (scaled - flat - unit * along)
        gh_ref[at, :] = grad_hidden
        gh = grad_hidden.astype(BF)
        context = ctx_ref[at, :]
        grad_context = mm_t(gh, wout_ref[...]).astype(BF).astype(FL)
        dout_new = t_mm(context, gh)
        dout = dout_new if part == 0 else dout + dout_new
        along_context = grad_context * context.astype(FL)
        sin = sin_ref[spots, :]
        cos = cos_ref[spots, :]
        keys = kt_ref[:seen, :]
        values = v_ref[:seen, :]
        grad_u, grad_v = [], []
        for h in range(heads):
            delta = jnp.sum(jnp.where(lanes[h], along_context, 0.0), axis=-1, keepdims=True)
            own = jnp.where(lanes[h], grad_context, 0.0).astype(BF)
            probs = probs_ref[h, at, :seen]
            grad_score = (probs.astype(FL) * (mm_t(own, values) - delta)).astype(BF)
            dv_ref[:, :seen] += t_mm(own, probs)
            dk_ref[:, :seen] += t_mm(qb_ref[h, at, :wide], grad_score)
            spread = mm(grad_score, keys)
            grad_u.append(spread[:, :wide])
            on_cos, on_sin = spread[:, wide : wide + half], spread[:, wide + half :]
            turned = jnp.concatenate(
                [(on_cos * sin - on_sin * cos).astype(BF), (on_cos * cos + on_sin * sin).astype(BF)], axis=1
            )
            grad_v.append(mm(turned, wpos_ref[...]))
            query_v = jnp.where(lanes[h], qv_ref[at, :].astype(FL), 0.0).astype(BF)
            dpos_new = t_mm(query_v, turned)
            dpos = dpos_new if dpos is None else dpos + dpos_new
        grad_u = pick_heads(grad_u, lanes) * scale
        grad_v = pick_heads(grad_v, lanes) * scale
        bias_u += jnp.sum(grad_u, axis=0, keepdims=True)
        bias_v += jnp.sum(grad_v, axis=0, keepdims=True)
        dq_ref[at, :] = (grad_u + grad_v).astype(BF)
    weights = jnp.concatenate([wq_ref[...], wk_ref[...], wv_ref[...]], axis=1)
    gain_sum = shift_sum = 0.0
    for part in range(2):
        at = slice(part * block, (part + 1) * block)
        spots = slice(first + part * block, first + (part + 1) * block)
        cols = slice(mem_len + first + part * block, mem_len + first + (part + 1) * block)
        grads = jnp.concatenate(
            [dq_ref[at, :], dk_ref[:, cols].T.astype(BF), dv_ref[:, cols].T.astype(BF)], axis=1
        )
        back = mm_t(grads, weights)
        unit, _ = norm_parts(x_ref[spots, :].astype(FL))
        gain_sum += jnp.sum(back * unit, axis=0, keepdims=True)
        shift_sum += jnp.sum(back, axis=0, keepdims=True)
        back_b = back.astype(BF)

        @pl.when(core == part)
        def _():
            keep_ref[...] = back_b

        @pl.when(core != part)
        def _():
            send_ref[...] = back_b

    if last:
        for at in range(0, mem_len, block):
            cols = slice(at, at + block)
            grads = jnp.concatenate([dk_ref[:, cols].T.astype(BF), dv_ref[:, cols].T.astype(BF)], axis=1)
            back = mm_t(grads, weights[:, wide:])
            unit, _ = norm_parts(mem_ref[cols, :].astype(FL))
            gain_sum += jnp.sum(back * unit, axis=0, keepdims=True)
            shift_sum += jnp.sum(back, axis=0, keepdims=True)
        normed = normed_ref[...]
        query_grads = jnp.concatenate([dq_ref[...], dq_in[...]], axis=0)
        grads_ref[:wide, :] = t_mm(query_grads, normed[mem_len:, :]).astype(BF)
        grads_ref[wide : 2 * wide, :] = mm(dk_ref[...].astype(BF), normed).astype(BF)
        grads_ref[2 * wide : 3 * wide, :] = mm(dv_ref[...].astype(BF), normed).astype(BF)
        grads_ref[3 * wide : 4 * wide, :] = (dpos + dpos_in[...]).astype(BF)
        grads_ref[4 * wide : 5 * wide, :] = (dout + dout_in[...]).astype(BF)
        gain_sum += vec_in[0:1, :]
        shift_sum += vec_in[1:2, :]
        bias_u += bias_in[0:1, :]
        bias_v += bias_in[1:2, :]
    dpos_ref[...] = dpos
    dout_ref[...] = dout
    vec_ref[0:1, :] = gain_sum
    vec_ref[1:2, :] = shift_sum
    bias_ref[0:1, :] = bias_u
    bias_ref[1:2, :] = bias_v


def finish_kernel(first, block, core_ref, x_ref, gain_ref, gh_ref, mine_ref, other_ref, out_ref):
    core = core_ref[0]
    for part in range(2):
        at = slice(part * block, (part + 1) * block)
        spots = slice(first + part * block, first + (part + 1) * block)
        unit, inv = norm_parts(x_ref[spots, :].astype(FL))
        scaled = ordered(core, mine_ref[...].astype(FL), other_ref[...].astype(FL), part) * gain_ref[...]
        flat = jnp.mean(scaled, axis=-1, keepdims=True)
        along = jnp.mean(scaled * unit, axis=-1, keepdims=True)
        out_ref[at, :] = (gh_ref[at, :] + inv * (scaled - flat - unit * along)).astype(BF)


def call(kernel, outs, args, scalars, name, flops):
    specs = [pl.BlockSpec(memory_space=pltpu.SMEM)] * scalars
    specs += [pl.BlockSpec(memory_space=pltpu.VMEM)] * (len(args) - scalars)
    shapes = [jax.ShapeDtypeStruct(s, d) for s, d in outs]
    size = sum(a.size * a.dtype.itemsize for a in args) + sum(int(np.prod(s)) * np.dtype(d).itemsize for s, d in outs)
    return pl.pallas_call(
        kernel,
        out_shape=shapes,
        in_specs=specs,
        out_specs=[pl.BlockSpec(memory_space=pltpu.VMEM)] * len(outs),
        compiler_params=pltpu.CompilerParams(vmem_limit_bytes=VMEM_LIMIT),
        cost_estimate=pl.CostEstimate(flops=int(flops), bytes_accessed=int(size), transcendentals=0),
        name=name,
    )(*args)


def rounded_sum(left, right):
    return (left.astype(FL) + right.astype(FL)).astype(BF)


def swap(rows, axis, size, bit):
    return lax.ppermute(rows, axis, [(i, i ^ bit) for i in range(size)])


def tensor_sum(keep, send, n_tensor):
    mine = rounded_sum(keep, swap(send, "tensor", n_tensor, 1))
    bit = 2
    while bit < n_tensor:
        mine = rounded_sum(mine, swap(mine, "tensor", n_tensor, bit))
        bit *= 2
    return mine, swap(mine, "tensor", n_tensor, 1)


def dp_sum(rows, n_dp, order):
    here = lax.axis_index("dp")
    for bit in order:
        size = rows.shape[0] // 2
        high = (here >> bit & 1) == 1
        keep = jnp.where(high, rows[size:], rows[:size])
        send = jnp.where(high, rows[:size], rows[size:])
        rows = rounded_sum(keep, swap(send, "dp", n_dp, 1 << bit))
    for bit in reversed(order):
        high = (here >> bit & 1) == 1
        other = swap(rows, "dp", n_dp, 1 << bit)
        rows = jnp.where(high, jnp.concatenate([other, rows]), jnp.concatenate([rows, other]))
    return rows


def all_sum(rows, axis, size):
    bit = 1
    while bit < size:
        rows = rows + swap(rows, axis, size, bit)
        bit *= 2
    return rows


def per_device(n_dp, n_tensor, *args):
    (inputs, memory, counts, attn_gain, attn_shift, w_query, w_key, w_value, w_pos, bias_u, bias_v, w_out,
     ffn_gain, ffn_shift, w_up, up_bias, w_down, down_bias, out_grad) = args
    _, seq_len, width = inputs.shape
    mem_len = memory.shape[1]
    total = mem_len + seq_len
    wide = w_query.shape[1]
    heads = wide // HEAD
    ff = w_up.shape[1]
    chunk = seq_len // 2
    block = chunk // 2
    late = chunk
    core = (lax.axis_index("tensor") & 1).astype(jnp.int32).reshape(1)
    x, mem, g = inputs[0], memory[0], out_grad[0]
    row = lambda v: v.reshape(1, -1)

    freq = 1.0 / 10000.0 ** (np.arange(0, width, 2, dtype=np.float64) / width)
    key_phase = np.arange(total)[:, None] * freq[None, :]
    table = jnp.asarray(np.concatenate([np.cos(key_phase), np.sin(key_phase)], axis=1).astype(BF))
    row_phase = (np.arange(seq_len) + mem_len)[:, None] * freq[None, :]
    sin = jnp.asarray(np.sin(row_phase).astype(np.float32))
    cos = jnp.asarray(np.cos(row_phase).astype(np.float32))

    part_rows = [((block, width), BF), ((block, width), BF)]
    bu, bv = row(bias_u), row(bias_v)

    def attend_outs(seen):
        return [
            ((heads, chunk, wide + width), BF), ((chunk, wide), BF), ((heads, chunk, seen), BF), ((chunk, wide), BF),
            *part_rows,
        ]

    normed, keys, values, qb_l, qv_l, probs_l, ctx_l, keep, send = call(
        functools.partial(front_kernel, late, block, heads),
        [((total, width), BF), ((total, wide + width), BF), ((total, wide), BF), *attend_outs(total)],
        (counts, core, x, mem, row(attn_gain), row(attn_shift), w_query, w_key, w_value, w_pos, bu, bv, table, sin, cos,
         w_out), 2, "front", 6e9,
    )
    att_l = tensor_sum(keep, send, n_tensor)
    qb_e, qv_e, probs_e, ctx_e, keep, send = call(
        functools.partial(second_kernel, 0, block, heads, mem_len),
        attend_outs(mem_len + chunk),
        (counts, core, normed, keys, values, w_query, w_pos, bu, bv, sin, cos, w_out), 2, "second", 4e9,
    )
    att_e = tensor_sum(keep, send, n_tensor)

    def ffn(first, last, attended, more, name):
        kind = BF if last else FL
        return call(
            functools.partial(ffn_kernel, first, block, last),
            [*part_rows, *part_rows, ((width, ff), kind), ((ff, width), kind), ((3, width), FL), ((1, ff), FL)],
            (core, x, *attended, row(ffn_gain), row(ffn_shift), w_up, row(up_bias), w_down, g, *more), 1, name, 3e9,
        )

    keep, send, keep2, send2, *sums = ffn(late, False, att_l, (), "ffn_late")
    gnt_l = tensor_sum(keep2, send2, n_tensor)
    ffn_l = tensor_sum(keep, send, n_tensor)
    keep, send, keep2, send2, g_up, g_down, ffn_vec, g_up_bias = ffn(0, True, att_e, sums, "ffn_early")
    gnt_e = tensor_sum(keep2, send2, n_tensor)
    ffn_e = tensor_sum(keep, send, n_tensor)

    shared = [((wide, total), FL), ((wide, total), FL), ((wide, width), FL), ((wide, width), FL), ((chunk, wide), BF)]
    small = [((2, width), FL), ((2, wide), FL)]

    def back(first, last, attended, gnt, saved, more, name):
        ctx, probs, qb, qv = saved
        head_outs = [((chunk, width), FL), *part_rows]
        outs = head_outs + ([((5 * wide, width), BF), *small, *shared] if last else [*shared, *small])
        return call(
            functools.partial(back_kernel, first, block, heads, mem_len, last),
            outs,
            (core, x, *attended, *gnt, g, row(ffn_gain), w_out, ctx, probs, qb, qv, keys, values, w_pos, sin, cos,
             normed, w_query, w_key, w_value, *more), 1, name, 8e9,
        )

    gh_l, keep, send, dk, dv, dpos, dout, dq, vec, bias = back(
        late, False, att_l, gnt_l, (ctx_l, probs_l, qb_l, qv_l), (), "back_late"
    )
    part_l = tensor_sum(keep, send, n_tensor)
    gh_e, keep, send, attn_grads, attn_vec, bias = back(
        0, True, att_e, gnt_e, (ctx_e, probs_e, qb_e, qv_e), (mem, dk, dv, dpos, dout, dq, vec, bias), "back_early"
    )[:6]
    part_e = tensor_sum(keep, send, n_tensor)

    steps = list(range((n_dp - 1).bit_length()))
    turned = steps[1:] + steps[:1]
    g_up = dp_sum(g_up, n_dp, steps)
    g_down = dp_sum(g_down, n_dp, turned)
    cut = 5 * wide * 2 // 5
    first_grads = dp_sum(attn_grads[:cut], n_dp, steps)
    second_grads = dp_sum(attn_grads[cut:], n_dp, turned)
    g_query, g_key = first_grads[:wide].T.astype(FL), first_grads[wide:].T.astype(FL)
    g_value, g_pos = second_grads[:wide].T.astype(FL), second_grads[wide : 2 * wide].T.astype(FL)
    g_out = second_grads[2 * wide :].astype(FL)

    vecs = jnp.concatenate([ffn_vec[:2], attn_vec, ffn_vec[2:] * (1.0 / n_tensor)], axis=0)
    own = jnp.concatenate([g_up_bias.reshape(-1, width), jnp.pad(bias.reshape(1, -1), ((0, 0), (0, width - 2 * wide)))])
    small_sum = all_sum(jnp.concatenate([vecs, own]), "dp", n_dp)
    vecs = all_sum(small_sum[:5], "tensor", n_tensor)
    own = small_sum[5:]

    def finish(first, gh, attended, name):
        return call(
            functools.partial(finish_kernel, first, block),
            [((chunk, width), BF)],
            (core, x, row(attn_gain), gh, *attended), 1, name, 1e8,
        )[0]

    input_grad = jnp.concatenate([finish(0, gh_e, part_e, "finish_e"), finish(late, gh_l, part_l, "finish_l")])

    def in_order(pair):
        mine, other = pair
        first_half = core[0] == 0
        return jnp.concatenate([jnp.where(first_half, mine, other), jnp.where(first_half, other, mine)])

    attended = jnp.concatenate([in_order(att_e), in_order(att_l)]).astype(FL)
    added = jnp.concatenate([in_order(ffn_e), in_order(ffn_l)]).astype(FL)
    output = (x.astype(FL) + attended + added + down_bias).astype(BF)
    return (
        output[None],
        input_grad[None],
        vecs[2],
        vecs[3],
        g_query,
        g_key,
        g_value,
        g_pos,
        own[-1, :wide].reshape(heads, HEAD),
        own[-1, wide : 2 * wide].reshape(heads, HEAD),
        g_out,
        vecs[0],
        vecs[1],
        g_up.astype(FL),
        own[: ff // width].reshape(-1),
        g_down.astype(FL),
        vecs[4],
    )


def solution(mesh):
    split, whole = P(None, "tensor"), P()
    return jax.shard_map(
        functools.partial(per_device, mesh.shape["dp"], mesh.shape["tensor"]),
        mesh=mesh,
        in_specs=(
            P("dp", None, None), P("dp", None, None), P("dp"), whole, whole, split, split, split, split,
            P("tensor", None), P("tensor", None), P("tensor", None), whole, whole, split, P("tensor"),
            P("tensor", None), whole, P("dp", None, None),
        ),
        out_specs=(
            P("dp", None, None), P("dp", None, None), whole, whole, split, split, split, split,
            P("tensor", None), P("tensor", None), P("tensor", None), whole, whole, split, P("tensor"),
            P("tensor", None), whole,
        ),
        check_vma=False,
    )
```

```python
import functools

import jax
import jax.numpy as jnp
import numpy as np
from jax import lax
from jax.experimental import pallas as pl
from jax.experimental.pallas import tpu as pltpu
from jax.sharding import PartitionSpec as P

HEAD = 64
BF = jnp.bfloat16
FL = jnp.float32
eps_norm = 1e-05
neg_fill = -1e30
VMEM_LIMIT = 24 * 1024 * 1024
small = 16


def mm(left, right):
    return lax.dot_general(left, right, (((1,), (0,)), ((), ())), preferred_element_type=FL)


def mm_t(left, right):
    return lax.dot_general(left, right, (((1,), (1,)), ((), ())), preferred_element_type=FL)


def t_mm(left, right):
    return lax.dot_general(left, right, (((0,), (0,)), ((), ())), preferred_element_type=FL)


def norm_parts(rows):
    center = rows - jnp.mean(rows, axis=-1, keepdims=True)
    spread = jnp.mean(center * center, axis=-1, keepdims=True)
    inv = lax.rsqrt(spread + eps_norm)
    return center * inv, inv


def norm_back(scaled, unit, inv):
    flat = jnp.mean(scaled, axis=-1, keepdims=True)
    along = jnp.mean(scaled * unit, axis=-1, keepdims=True)
    return inv * (scaled - flat - unit * along)


def head_lanes(wide, h):
    lane = lax.broadcasted_iota(jnp.int32, (1, wide), 1)
    return (lane >= h * HEAD) & (lane < (h + 1) * HEAD)


def col_sum(rows):
    return jnp.sum(rows, axis=0, keepdims=True)


def loop(count, body):
    def step(i, carry):
        body(i)
        return carry

    lax.fori_loop(0, count, step, 0)


def rows_of(i, size):
    return pl.ds(pl.multiple_of(i * size, size), size)


def by_core(core, part, keep_ref, send_ref, rows, at):
    @pl.when(core == part)
    def _():
        keep_ref[at, :] = rows

    @pl.when(core != part)
    def _():
        send_ref[at, :] = rows


def added(left, right):
    return (left.astype(FL) + right.astype(FL)).astype(BF)


def make_queries(normed, spots, at, refs, heads):
    w_ref, wpos_ref, bu, bv, sin_ref, cos_ref, qb_ref, qv_ref = refs
    wide = heads * HEAD
    scale = HEAD ** (-0.5)
    query = mm(normed, w_ref[:, :wide]).astype(BF).astype(FL)
    query_u = (query + bu).astype(BF).astype(FL) * scale
    query_v = (query + bv).astype(BF).astype(FL) * scale
    qv_ref[at, :] = query_v.astype(BF)
    sin = sin_ref[spots, :]
    cos = cos_ref[spots, :]
    half = sin.shape[1]
    for h in range(heads):
        lanes = head_lanes(wide, h)
        qb_ref[h, at, :wide] = jnp.where(lanes, query_u, 0.0).astype(BF)
        coef = mm_t(jnp.where(lanes, query_v, 0.0).astype(BF), wpos_ref[...])
        on_sin, on_cos = coef[:, :half], coef[:, half:]
        qb_ref[h, at, wide : wide + half] = (on_sin * sin + on_cos * cos).astype(BF)
        qb_ref[h, at, wide + half :] = (on_cos * sin - on_sin * cos).astype(BF)


def attend(first, block, mem_len, heads, count, qb_ref, kt_ref, v_ref, probs_ref, ctx_ref, ctx_scr):
    wide = heads * HEAD
    rows = qb_ref.shape[1]
    for part in range(rows // block):
        at = slice(part * block, (part + 1) * block)
        start = first + part * block
        seen = mem_len + start + block

        def one_head(h):
            scores = mm_t(qb_ref[h, at, :], kt_ref[:seen, :])
            query_pos = start + lax.broadcasted_iota(jnp.int32, (block, 1), 0)
            limit = jnp.minimum(query_pos, count - 1)
            key_pos = lax.broadcasted_iota(jnp.int32, (block, seen - mem_len), 1)
            scores = jnp.concatenate(
                [scores[:, :mem_len], jnp.where(key_pos <= limit, scores[:, mem_len:], neg_fill)], axis=1
            )
            expo = jnp.exp(scores - jnp.max(scores, axis=-1, keepdims=True))
            probs = (expo * (1.0 / jnp.sum(expo, axis=-1, keepdims=True))).astype(BF)
            probs_ref[h, at, :seen] = probs
            found = mm(probs, v_ref[:seen, :])
            ctx_scr[...] = jnp.where(head_lanes(wide, h), found, ctx_scr[...])

        loop(heads, one_head)
        ctx_ref[at, :] = ctx_scr[...].astype(BF)


def front_kernel(
    first, block, heads,
    place_ref, count_ref, x_in, mem_in, g_in, wq_in, wk_in, wv_in, wpos_in, wup_in, wdown_in, wout_in,
    shift_in, gain_in, fgain_in, fshift_in, upb_in, downb_in, bu_in, bv_in, table_in, sin_in, cos_in,
    x_ref, mem_ref, g_ref, w_ref, wpos_ref, wup_ref, wdown_ref, wout_ref, gain_ref, fgain_ref, fshift_ref, upb_ref,
    downb_ref, sin_ref, cos_ref, bias_ref, normed_ref, kt_ref, v_ref, qb_ref, qv_ref, probs_ref, ctx_ref,
    shift_ref, bu_ref, bv_ref, ctx_scr, sems,
):
    wide = heads * HEAD
    mem_len = mem_in.shape[0]
    seq_len = x_in.shape[0]
    todo = [
        (mem_in, mem_ref), (gain_in, gain_ref), (shift_in, shift_ref), (wk_in, w_ref.at[:, wide : 2 * wide]),
        (wv_in, w_ref.at[:, 2 * wide :]), (x_in, x_ref), (wq_in, w_ref.at[:, :wide]), (bu_in, bu_ref), (bv_in, bv_ref),
        (wpos_in, wpos_ref), (sin_in, sin_ref), (cos_in, cos_ref), (table_in, kt_ref.at[:, wide:]),
        (wout_in, wout_ref), (wup_in, wup_ref), (wdown_in, wdown_ref), (g_in, g_ref), (fgain_in, fgain_ref),
        (fshift_in, fshift_ref), (upb_in, upb_ref), (downb_in, downb_ref),
    ]
    copies = [pltpu.make_async_copy(src, dst, sems.at[i]) for i, (src, dst) in enumerate(todo)]
    for copy in copies:
        copy.start()
    for copy in copies[:5]:
        copy.wait()

    def project(rows_ref, at, to):
        unit, _ = norm_parts(rows_ref[at, :].astype(FL))
        normed = (unit * gain_ref[...] + shift_ref[...]).astype(BF)
        normed_ref[to, :] = normed
        pair = mm(normed, w_ref[:, wide:]).astype(BF)
        kt_ref[to, :wide] = pair[:, :wide]
        v_ref[to, :] = pair[:, wide:]

    def some_memory(i):
        project(mem_ref, rows_of(i, block), rows_of(i, block))

    def some_rows(i):
        project(x_ref, rows_of(i, block), rows_of(i + mem_len // block, block))

    loop(mem_len // block, some_memory)
    for copy in copies[5:7]:
        copy.wait()
    loop(seq_len // block, some_rows)
    for copy in copies[7:13]:
        copy.wait()
    bias_ref[0:1, :] = jnp.concatenate([bu_ref[h : h + 1, :] for h in range(heads)], axis=1)
    bias_ref[1:2, :] = jnp.concatenate([bv_ref[h : h + 1, :] for h in range(heads)], axis=1)

    def some_queries(i):
        at = rows_of(i, block)
        spots = rows_of(i + first // block, block)
        make_queries(
            normed_ref[rows_of(i + (mem_len + first) // block, block), :], spots, at,
            (w_ref, wpos_ref, bias_ref[0:1, :], bias_ref[1:2, :], sin_ref, cos_ref, qb_ref, qv_ref), heads,
        )

    loop((seq_len - first) // block, some_queries)
    attend(first, block, mem_len, heads, count_ref[0], qb_ref, kt_ref, v_ref, probs_ref, ctx_ref, ctx_scr)
    for copy in copies[13:]:
        copy.wait()


def second_kernel(
    first, block, heads, mem_len,
    count_ref, normed_ref, kt_ref, v_ref, w_ref, wpos_ref, bias_ref, sin_ref, cos_ref,
    qb_ref, qv_ref, probs_ref, ctx_ref, ctx_scr,
):
    def some_queries(i):
        at = rows_of(i, block)
        spots = rows_of(i + first // block, block)
        make_queries(
            normed_ref[rows_of(i + (mem_len + first) // block, block), :], spots, at,
            (w_ref, wpos_ref, bias_ref[0:1, :], bias_ref[1:2, :], sin_ref, cos_ref, qb_ref, qv_ref), heads,
        )

    loop(qb_ref.shape[1] // block, some_queries)
    attend(first, block, mem_len, heads, count_ref[0], qb_ref, kt_ref, v_ref, probs_ref, ctx_ref, ctx_scr)


def ffn_rows_kernel(
    first, block,
    place_ref, x_ref, c0_ref, c1_ref, c2_ref, c3_ref, o0_ref, o1_ref, o2_ref, o3_ref, gain_ref, shift_ref, up_ref,
    upb_ref, down_ref, g_ref,
    hidden_ref, normed_ref, activ_ref, gpre_ref, keep_ref, send_ref, vec_ref, upb_out,
):
    core = place_ref[0]
    vec_ref[...] = jnp.zeros(vec_ref.shape, FL)
    upb_out[...] = jnp.zeros(upb_out.shape, FL)

    def one(i):
        at = rows_of(i, block)
        spots = rows_of(i + first // block, block)
        attended = mm(c0_ref[at, :], o0_ref[...]) + mm(c1_ref[at, :], o1_ref[...])
        attended = attended + (mm(c2_ref[at, :], o2_ref[...]) + mm(c3_ref[at, :], o3_ref[...]))
        hidden = x_ref[spots, :].astype(FL) + attended
        hidden_ref[at, :] = hidden
        unit, _ = norm_parts(hidden)
        normed = (unit * gain_ref[...] + shift_ref[...]).astype(BF)
        normed_ref[at, :] = normed
        pre = mm(normed, up_ref[...]) + upb_ref[...]
        cdf = 0.5 + 0.5 * lax.erf(pre * np.float32(0.5**0.5))
        activ_ref[at, :] = (pre * cdf).astype(BF)
        slope = cdf + pre * jnp.exp(-0.5 * pre * pre) * np.float32((2 * np.pi) ** -0.5)
        grads = g_ref[spots, :]
        grad_pre = (mm_t(grads, down_ref[...]) * slope).astype(BF)
        gpre_ref[at, :] = grad_pre
        back = mm_t(grad_pre, up_ref[...])
        by_core(core, i, keep_ref, send_ref, back.astype(BF), slice(0, block))
        vec_ref[0:1, :] += col_sum(back * unit)
        vec_ref[1:2, :] += col_sum(back)
        vec_ref[2:3, :] += col_sum(grads.astype(FL))
        upb_out[...] += col_sum(grad_pre.astype(FL))

    loop(2, one)


def ffn_late_kernel(
    first, place_ref, activ_ref, gpre_ref, normed_ref, down_ref, g_ref, ctx_in, share_ref, up_out, down_out, ctx_out
):
    ctx_out[...] = ctx_in[...]
    size = activ_ref.shape[0]
    activ = activ_ref[...]
    share_ref[...] = mm(activ, down_ref[...]).astype(BF)
    down_out[...] = t_mm(activ, g_ref[first : first + size, :])
    up_out[...] = t_mm(normed_ref[...], gpre_ref[...])


def ffn_early_kernel(
    first,
    place_ref, activ_ref, gpre_ref, normed_ref, down_ref, g_ref, late_ref, up_in, down_in,
    share_ref, f_keep, f_send,
):
    size = activ_ref.shape[0]
    activ = activ_ref[...]
    up = up_in[...] + t_mm(normed_ref[...], gpre_ref[...])
    by_core(place_ref[1] & 1, 0, f_keep, f_send, up.astype(BF), slice(None))
    down = down_in[...] + t_mm(activ, g_ref[first : first + size, :])
    by_core(place_ref[1] & 1, 1, f_keep, f_send, down.astype(BF), slice(None))
    share_ref[:size, :] = mm(activ, down_ref[...]).astype(BF)
    share_ref[size:, :] = late_ref[...]


def back_rows(
    first, block, heads, mem_len, place_ref, hidden_ref, mine_ref, other_ref, g_ref, fgain_ref, wout_ref, ctx_ref,
    probs_ref, qb_ref, qv_ref, kt_ref, v_ref, wpos_ref, sin_ref, cos_ref,
    gh_ref, dk_ref, dv_ref, dpos_ref, dout_ref, dq_ref, bias_ref, grad_u, grad_v,
):
    core = place_ref[0]
    wide = heads * HEAD
    half = sin_ref.shape[1]
    scale = HEAD ** (-0.5)
    for part in range(2):
        at = slice(part * block, (part + 1) * block)
        spots = slice(first + part * block, first + (part + 1) * block)
        seen = mem_len + first + (part + 1) * block
        unit, inv = norm_parts(hidden_ref[at, :])
        summed = jnp.where(core == part, mine_ref[...].astype(FL), other_ref[...].astype(FL))
        grad_hidden = g_ref[spots, :].astype(FL) + norm_back(summed * fgain_ref[...], unit, inv)
        gh_ref[at, :] = grad_hidden
        gh = grad_hidden.astype(BF)
        context = ctx_ref[at, :]
        grad_context = mm_t(gh, wout_ref[...]).astype(BF).astype(FL)
        dout_ref[...] += t_mm(context, gh)
        along_context = grad_context * context.astype(FL)

        def one_head(h):
            lanes = head_lanes(wide, h)
            delta = jnp.sum(jnp.where(lanes, along_context, 0.0), axis=-1, keepdims=True)
            own = jnp.where(lanes, grad_context, 0.0).astype(BF)
            probs = probs_ref[h, at, :seen]
            grad_score = (probs.astype(FL) * (mm_t(own, v_ref[:seen, :]) - delta)).astype(BF)
            dv_ref[:, :seen] += t_mm(own, probs)
            dk_ref[:, :seen] += t_mm(qb_ref[h, at, :wide], grad_score)
            spread = mm(grad_score, kt_ref[:seen, :])
            grad_u[...] = jnp.where(lanes, spread[:, :wide], grad_u[...])
            sin = sin_ref[spots, :]
            cos = cos_ref[spots, :]
            on_cos, on_sin = spread[:, wide : wide + half], spread[:, wide + half :]
            turned = jnp.concatenate(
                [(on_cos * sin - on_sin * cos).astype(BF), (on_cos * cos + on_sin * sin).astype(BF)], axis=1
            )
            grad_v[...] = jnp.where(lanes, mm(turned, wpos_ref[...]), grad_v[...])
            query_v = jnp.where(lanes, qv_ref[at, :].astype(FL), 0.0).astype(BF)
            dpos_ref[...] += t_mm(query_v, turned)

        loop(heads, one_head)
        bias_ref[0:1, :] += col_sum(grad_u[...]) * scale
        bias_ref[1:2, :] += col_sum(grad_v[...]) * scale
        dq_ref[at, :] = ((grad_u[...] + grad_v[...]) * scale).astype(BF)


def back_share(cols, dq_rows, unit, dk_ref, dv_ref, weights):
    pair = [dk_ref[:, cols].T.astype(BF), dv_ref[:, cols].T.astype(BF)]
    back = mm_t(jnp.concatenate(dq_rows + pair, axis=1), weights)
    return back, col_sum(back * unit), col_sum(back)


def back_late_kernel(
    first, block, heads, mem_len,
    place_ref, hidden_ref, mine_ref, other_ref, g_ref, fgain_ref, wout_ref, ctx_ref, probs_ref, qb_ref, qv_ref, kt_ref,
    v_ref, wpos_ref, sin_ref, cos_ref, x_ref, w_ref,
    gh_ref, dk_ref, dv_ref, dpos_ref, dout_ref, dq_ref, bias_ref, share_ref, vec_ref, grad_u, grad_v,
):
    for ref in (dk_ref, dv_ref, dpos_ref, dout_ref, bias_ref):
        ref[...] = jnp.zeros(ref.shape, FL)
    back_rows(
        first, block, heads, mem_len, place_ref, hidden_ref, mine_ref, other_ref, g_ref, fgain_ref, wout_ref, ctx_ref,
        probs_ref, qb_ref, qv_ref, kt_ref, v_ref, wpos_ref, sin_ref, cos_ref,
        gh_ref, dk_ref, dv_ref, dpos_ref, dout_ref, dq_ref, bias_ref, grad_u, grad_v,
    )
    vec_ref[...] = jnp.zeros(vec_ref.shape, FL)
    for part in range(2):
        at = slice(part * block, (part + 1) * block)
        spots = slice(first + part * block, first + (part + 1) * block)
        cols = slice(mem_len + first + part * block, mem_len + first + (part + 1) * block)
        unit, _ = norm_parts(x_ref[spots, :].astype(FL))
        back, gain_sum, shift_sum = back_share(cols, [dq_ref[at, :]], unit, dk_ref, dv_ref, w_ref[...])
        share_ref[at, :] = back.astype(BF)
        vec_ref[0:1, :] += gain_sum
        vec_ref[1:2, :] += shift_sum


def back_early_kernel(
    first, block, heads, mem_len, n_tensor, size,
    place_ref, hidden_ref, mine_ref, other_ref, g_ref, fgain_ref, wout_ref, ctx_ref, probs_ref, qb_ref, qv_ref, kt_ref,
    v_ref, wpos_ref, sin_ref, cos_ref, x_ref, w_ref, mem_ref, normed_ref, dk_in, dv_in, dpos_in, dout_in, dq_in,
    bias_in, late_ref, vec_in, vec_l, vec_e, upb_l, upb_e, ffn_ref,
    gh_ref, keep_ref, send_ref, a_keep, a_send,
    dk_ref, dv_ref, dpos_ref, dout_ref, dq_ref, vec_ref, bias_ref, grad_u, grad_v,
):
    wide = heads * HEAD
    core = place_ref[0]
    for part in range(2):
        at = slice(part * block, (part + 1) * block)
        by_core(core, part, keep_ref, send_ref, late_ref[at, :], slice(block, 2 * block))
        by_core(core, part, keep_ref, send_ref, ffn_ref[at, :], slice(2 * block, 3 * block))
        at = slice((part + 2) * block, (part + 3) * block)
        by_core(core, part, keep_ref, send_ref, ffn_ref[at, :], slice(3 * block, 4 * block))
    for ref, old in ((dk_ref, dk_in), (dv_ref, dv_in), (dpos_ref, dpos_in), (dout_ref, dout_in), (bias_ref, bias_in)):
        ref[...] = old[...]
    back_rows(
        first, block, heads, mem_len, place_ref, hidden_ref, mine_ref, other_ref, g_ref, fgain_ref, wout_ref, ctx_ref,
        probs_ref, qb_ref, qv_ref, kt_ref, v_ref, wpos_ref, sin_ref, cos_ref,
        gh_ref, dk_ref, dv_ref, dpos_ref, dout_ref, dq_ref, bias_ref, grad_u, grad_v,
    )
    normed = normed_ref[...]
    dq_all = jnp.concatenate([dq_ref[...], dq_in[...]], axis=0)
    grads = [
        t_mm(dq_all, normed[mem_len:]),
        mm(dk_ref[...].astype(BF), normed),
        mm(dv_ref[...].astype(BF), normed),
        dpos_ref[...],
        dout_ref[...],
    ]
    grads = jnp.concatenate(grads, axis=0)
    vec_ref[...] = vec_in[...]
    for part in range(2):
        at = slice(part * block, (part + 1) * block)
        spots = slice(first + part * block, first + (part + 1) * block)
        cols = slice(mem_len + first + part * block, mem_len + first + (part + 1) * block)
        unit, _ = norm_parts(x_ref[spots, :].astype(FL))
        back, gain_sum, shift_sum = back_share(cols, [dq_ref[at, :]], unit, dk_ref, dv_ref, w_ref[...])
        by_core(core, part, keep_ref, send_ref, back.astype(BF), slice(0, block))
        vec_ref[0:1, :] += gain_sum
        vec_ref[1:2, :] += shift_sum
    for at in range(0, mem_len, block):
        cols = slice(at, at + block)
        unit, _ = norm_parts(mem_ref[cols, :].astype(FL))
        _, gain_sum, shift_sum = back_share(cols, [], unit, dk_ref, dv_ref, w_ref[:, wide:])
        vec_ref[0:1, :] += gain_sum
        vec_ref[1:2, :] += shift_sum
    width = vec_ref.shape[1]
    wider = jnp.zeros((1, width - wide), FL)
    rows = [vec_ref[...], vec_l[0:2, :] + vec_e[0:2, :], (vec_l[2:3, :] + vec_e[2:3, :]) * (1.0 / n_tensor)]
    rows += [jnp.concatenate([bias_ref[i : i + 1, :], wider], axis=1) for i in range(2)]
    for i in range(upb_l.shape[1] // width):
        cols = slice(i * width, (i + 1) * width)
        rows.append(upb_l[:, cols] + upb_e[:, cols])
    rows.append(jnp.zeros((small - 7 - upb_l.shape[1] // width, width), FL))
    rows = jnp.concatenate(rows, axis=0).astype(BF)
    step = size + small
    for d in range(2 * a_keep.shape[0] // step):
        here = max(0, min(size, 5 * wide - d * size))
        piece = [grads[d * size : d * size + here].astype(BF)] if here else []
        piece += [jnp.zeros((size - here, width), BF)] if here < size else []
        piece = jnp.concatenate([*piece, rows], axis=0)
        per_half = a_keep.shape[0] // step
        at = slice(d % per_half * step, (d % per_half + 1) * step)
        by_core(place_ref[1] & 1, d // per_half, a_keep, a_send, piece, at)


def weights_kernel(wide, bit, place_ref, mine_ref, got_ref, *refs):
    outs, rows_ref = refs[:5], refs[5]
    join(place_ref, bit, mine_ref, got_ref, rows_ref)
    for i in range(4):
        outs[i][...] = rows_ref[i * wide : (i + 1) * wide, :].T
    outs[4][...] = rows_ref[4 * wide : 5 * wide, :]


def small_kernel(heads, n_tensor, *refs):
    mine, outs = refs[0], refs[n_tensor:]
    total = mine[...]
    for other in refs[1:n_tensor]:
        total = total + other[...]
    for i in range(5):
        outs[i][...] = total[i : i + 1, :]
    for k in range(2):
        for h in range(heads):
            outs[5 + k][h : h + 1, :] = mine[5 + k : 6 + k, h * HEAD : (h + 1) * HEAD]
    width = mine.shape[1]
    for i in range(outs[7].shape[1] // width):
        outs[7][:, i * width : (i + 1) * width] = mine[7 + i : 8 + i, :]


def ffn_grads_kernel(place_ref, mine_ref, got_ref, up_ref, down_ref):
    own = (place_ref[1] & 1) == 0
    mine, got = mine_ref[...].astype(FL), got_ref[...].astype(FL)
    up_ref[...] = jnp.where(own, mine, got)
    down_ref[...] = jnp.where(own, got, mine)


def finish_kernel(
    block, place_ref, x_ref, gain_ref, gh_e, gh_l, hidden_e, hidden_l, mine_ref, other_ref, bias_ref, out_ref, grad_ref
):
    core = place_ref[0]

    def some_rows(gh_ref, hidden_ref, first):
        def body(i):
            at = rows_of(i, block)
            spots = rows_of(i + 2 * first, block)

            def summed(group):
                rows = slice(group * block, (group + 1) * block)
                return jnp.where(core == i, mine_ref[rows, :].astype(FL), other_ref[rows, :].astype(FL))

            unit, inv = norm_parts(x_ref[spots, :].astype(FL))
            grad_ref[spots, :] = (gh_ref[at, :] + norm_back(summed(first) * gain_ref[...], unit, inv)).astype(BF)
            out_ref[spots, :] = (hidden_ref[at, :] + summed(first + 2) + bias_ref[...]).astype(BF)

        return body

    loop(2, some_rows(gh_e, hidden_e, 0))
    loop(2, some_rows(gh_l, hidden_l, 1))


def halve(place_ref, bit, total, keep_ref, send_ref):
    size = total.shape[0] // 2
    high = (place_ref[1] >> bit) & 1
    by_core(high, 0, keep_ref, send_ref, total[:size], slice(None))
    by_core(high, 1, keep_ref, send_ref, total[size:], slice(None))


def join(place_ref, bit, mine_ref, got_ref, out_ref):
    size = mine_ref.shape[0]
    high = ((place_ref[1] >> bit) & 1) == 1
    mine, got = mine_ref[...].astype(FL), got_ref[...].astype(FL)
    out_ref[:size, :] = jnp.where(high, got, mine).astype(out_ref.dtype)
    out_ref[size:, :] = jnp.where(high, mine, got).astype(out_ref.dtype)


SMEM = pl.BlockSpec(memory_space=pltpu.SMEM)
SPECS = {s: pl.BlockSpec(memory_space=s) for s in (pltpu.VMEM, pltpu.HBM)}


def call(kernel, outs, args, name, flops, scratch=(), space=pltpu.VMEM, after=(), out_space=None):
    count, extra = len(args), len(after)

    def body(*refs):
        kernel(*refs[:count], *refs[count + extra :])

    specs = [SMEM if a.dtype == jnp.int32 else SPECS[space] for a in args]
    specs += [pl.BlockSpec(memory_space=pl.ANY)] * extra
    if space is pltpu.HBM:
        args = [a if a.dtype == jnp.int32 else pltpu.with_memory_space_constraint(a, space) for a in args]
    return pl.pallas_call(
        body,
        out_shape=[out_space(s, d) if out_space else jax.ShapeDtypeStruct(s, d) for s, d in outs],
        in_specs=specs,
        out_specs=[SPECS[pltpu.VMEM]] * len(outs),
        scratch_shapes=scratch,
        compiler_params=pltpu.CompilerParams(vmem_limit_bytes=VMEM_LIMIT),
        cost_estimate=pl.CostEstimate(flops=1, bytes_accessed=1, transcendentals=0),
        name=name,
    )(*args, *after)


def swap(rows, axis, size, bit):
    return lax.ppermute(rows, axis, [(i, i ^ bit) for i in range(size)])


def work_kernel(jobs, place_ref, *refs):
    ins, outs = refs[: 2 * len(jobs)], list(refs[2 * len(jobs) :])
    for i, (kind, bit) in enumerate(jobs):
        mine, got = ins[2 * i : 2 * i + 2]
        if kind == "halve":
            halve(place_ref, bit, added(mine[...], got[...]), outs.pop(0), outs.pop(0))
        elif kind == "join":
            join(place_ref, bit, mine, got, outs.pop(0))
        elif kind == "sum":
            outs.pop(0)[...] = added(mine[...], got[...])
        else:
            total = mine[...].astype(FL) + got[...].astype(FL)
            size = outs[0].shape[0]
            outs.pop(0)[...] = total[:size].astype(BF)
            outs.pop(0)[...] = total[size:]


def work(place, jobs, name, after=()):
    outs = []
    for kind, _, mine, _ in jobs:
        size, width = mine.shape
        outs += {
            "halve": [((size // 2, width), BF)] * 2,
            "join": [((2 * size, width), BF)],
            "sum": [((size, width), BF)],
            "split": [((size - small, width), BF), ((small, width), FL)],
        }[kind]
    args = [a for job in jobs for a in job[2:]]
    return list(
        call(functools.partial(work_kernel, [job[:2] for job in jobs]), outs, (place, *args), name, 1e6, after=after)
    )


class Chain:
    def __init__(self, keep, send, n_dp):
        self.rows, self.send, self.n_dp, self.done = keep, send, n_dp, 0
        self.steps = (n_dp - 1).bit_length()
        self.start()

    def bit(self):
        return min(self.done, 2 * self.steps - 1 - self.done)

    def start(self):
        self.got = swap(self.send, "dp", self.n_dp, 1 << self.bit())

    def last(self):
        return self.done == 2 * self.steps - 1

    def job(self, end="sum"):
        if self.done < self.steps - 1:
            kind, bit = "halve", self.done + 1
        else:
            kind, bit = (end, 0) if self.done == self.steps - 1 else ("join", self.bit())
        return kind, bit, self.rows, self.got

    def take(self, results):
        kind = self.job()[0]
        self.rows = self.send = results.pop(0)
        if kind == "halve":
            self.send = results.pop(0)
        self.done += 1
        self.start()


def cores(rows, n_tensor):
    return swap(rows, "tensor", n_tensor, 1)


def chips(rows, n_tensor):
    return rows, swap(rows, "tensor", n_tensor, 2)


def copy_kernel(in_ref, out_ref):
    out_ref[...] = in_ref[...]


def per_device(n_dp, n_tensor, *args):
    (inputs, memory, counts, attn_gain, attn_shift, w_query, w_key, w_value, w_pos, bias_u, bias_v, w_out,
     ffn_gain, ffn_shift, w_up, up_bias, w_down, down_bias, out_grad) = args
    _, seq_len, width = inputs.shape
    mem_len = memory.shape[1]
    total = mem_len + seq_len
    wide = w_query.shape[1]
    heads = wide // HEAD
    ff = w_up.shape[1]
    chunk = seq_len // 2
    block = chunk // 2
    late = chunk
    place = jnp.stack([lax.axis_index("tensor") & 1, lax.axis_index("dp")]).astype(jnp.int32)
    x, mem, g = inputs[0], memory[0], out_grad[0]
    row = lambda v: v.reshape(1, -1)

    freq = 1.0 / 10000.0 ** (np.arange(0, width, 2, dtype=np.float64) / width)
    key_phase = np.arange(total)[:, None] * freq[None, :]
    table = jnp.asarray(np.concatenate([np.cos(key_phase), np.sin(key_phase)], axis=1).astype(BF))
    row_phase = (np.arange(seq_len) + mem_len)[:, None] * freq[None, :]
    sin = jnp.asarray(np.sin(row_phase).astype(np.float32))
    cos = jnp.asarray(np.cos(row_phase).astype(np.float32))

    outs_of = [w_out] + [swap(w_out, "tensor", n_tensor, k) for k in range(1, n_tensor)]

    def attend_outs(seen):
        return [((heads, chunk, wide + width), BF), ((chunk, wide), BF), ((heads, chunk, seen), BF), ((chunk, wide), BF)]

    ctx_scr = pltpu.VMEM((block, wide), FL)
    vectors = [row(v) for v in (attn_shift, attn_gain, ffn_gain, ffn_shift, up_bias, down_bias)]
    copied = [
        *[(a.shape, BF) for a in (x, mem, g)], ((width, 3 * wide), BF), *[(a.shape, BF) for a in (w_pos, w_up, w_down, w_out)],
        *[(a.shape, FL) for a in (*vectors[1:], sin, cos)], ((2, wide), FL),
    ]
    found = call(
        functools.partial(front_kernel, late, block, heads),
        [*copied, ((total, width), BF), ((total, wide + width), BF), ((total, wide), BF), *attend_outs(total)],
        (place, counts, x, mem, g, w_query, w_key, w_value, w_pos, w_up, w_down, w_out, *vectors, bias_u, bias_v, table, sin,
         cos), "front", 6e9,
        [pltpu.VMEM((1, width), FL)] + [pltpu.VMEM(bias_u.shape, FL)] * 2 + [ctx_scr, pltpu.SemaphoreType.DMA((21,))],
        pltpu.HBM,
    )
    x, mem, g, weights, w_pos, w_up, w_down, w_out = found[:8]
    attn_gain, ffn_gain, ffn_shift, up_bias, down_bias, sin, cos, biases, normed, keys, values, *saved_l = found[8:]
    ctx_l = [saved_l[-1], cores(saved_l[-1], n_tensor), swap(saved_l[-1], "tensor", n_tensor, 2)]
    saved_e = call(
        functools.partial(second_kernel, 0, block, heads, mem_len),
        attend_outs(mem_len + chunk),
        (counts, normed, keys, values, weights, w_pos, biases, sin, cos), "second", 4e9, [ctx_scr],
    )
    ctx_e = [saved_e[-1], cores(saved_e[-1], n_tensor), swap(saved_e[-1], "tensor", n_tensor, 2)]
    (relay,) = call(copy_kernel, [(ctx_l[2].shape, BF)], (ctx_l[2],), "relay_late", 1e6, after=saved_e[-1:])
    ctx_l.append(cores(relay, n_tensor))

    def ffn_rows(first, ctx, name, after):
        return call(
            functools.partial(ffn_rows_kernel, first, block),
            [((chunk, width), FL), ((chunk, width), BF), ((chunk, ff), BF), ((chunk, ff), BF), ((block, width), BF),
             ((block, width), BF), ((3, width), FL), ((1, ff), FL)],
            (place, x, *ctx, *outs_of, ffn_gain, ffn_shift, w_up, up_bias, w_down, g), name, 2e9, after=after,
        )

    hidden_l, normed_l, activ, gpre, keep_l, send, vec_l, upb_l = ffn_rows(late, ctx_l, "ffn_rows_late", saved_e[-1:])
    gnt_l = cores(send, n_tensor)
    share, up_l, down_l, relay = call(
        functools.partial(ffn_late_kernel, late),
        [((chunk, width), BF), ((width, ff), FL), ((ff, width), FL), ((chunk, wide), BF)],
        (place, activ, gpre, normed_l, w_down, g, ctx_e[2]), "ffn_late", 1e9,
    )
    ctx_e.append(cores(relay, n_tensor))
    (gnt_l,) = work(place, [("sum", 0, keep_l, gnt_l)], "add_late", (share,))
    gnt_l = chips(gnt_l, n_tensor)
    hidden_e, normed_e, activ, gpre, keep_e, send, vec_e, upb_e = ffn_rows(0, ctx_e, "ffn_rows_early", gnt_l[:1])
    gnt_e = cores(send, n_tensor)
    share, f_keep, f_send = call(
        functools.partial(ffn_early_kernel, 0),
        [(x.shape, BF)] + [((chunk, width), BF)] * 2,
        (place, activ, gpre, normed_e, w_down, g, share, up_l, down_l), "ffn_early", 1e9,
    )
    ffn = Chain(f_keep, f_send, n_dp)
    gnt_l, gnt_e = work(place, [("sum", 0, *gnt_l), ("sum", 0, keep_e, gnt_e)], "add_early", (f_keep,))
    gnt_l = (gnt_l, cores(gnt_l, n_tensor))
    gnt_e = chips(gnt_e, n_tensor)

    sums = [((wide, total), FL), ((wide, total), FL), ((wide, width), FL), ((wide, width), FL), ((chunk, wide), BF)]
    turn_scr = [ctx_scr, ctx_scr]

    def back_args(hidden, gnt, saved):
        qb, qv, probs, ctx = saved
        return (place, hidden, *gnt, g, ffn_gain, w_out, ctx, probs, qb, qv, keys, values, w_pos, sin, cos, x, weights)

    gh_l, dk, dv, dpos, dout, dq, bias, part, vec = call(
        functools.partial(back_late_kernel, late, block, heads, mem_len),
        [((chunk, width), FL), *sums, ((2, wide), FL), ((chunk, width), BF), ((2, width), FL)],
        back_args(hidden_l, gnt_l, saved_l), "back_late", 8e9, turn_scr,
    )
    gnt_e, *results = work(place, [("sum", 0, *gnt_e), ffn.job()], "add_middle", (vec,))
    ffn.take(results)
    gnt_e = (gnt_e, cores(gnt_e, n_tensor))
    size = max(16, -(-5 * wide // n_dp // 16) * 16)
    gh_e, keep, send, a_keep, a_send = call(
        functools.partial(back_early_kernel, 0, block, heads, mem_len, n_tensor, size),
        [((chunk, width), FL), *[((seq_len, width), BF)] * 2, *[((n_dp // 2 * (size + small), width), BF)] * 2],
        (*back_args(hidden_e, gnt_e, saved_e), mem, normed, dk, dv, dpos, dout, dq, bias, part, vec, vec_l, vec_e, upb_l,
         upb_e, share),
        "back_early", 6e9, [pltpu.VMEM(s, d) for s, d in (*sums, ((2, width), FL), ((2, wide), FL))] + turn_scr,
    )
    attn = Chain(a_keep, a_send, n_dp)
    send = cores(send, n_tensor)
    rows, *results = work(place, [("sum", 0, keep, send), ffn.job()], "step_ffn")
    ffn.take(results)
    rows = chips(rows, n_tensor)
    count = 0
    while not attn.last():
        chains = [attn] + [c for c in (ffn,) if not c.last()]
        jobs = [attn.job("split")] + [c.job() for c in chains[1:]]
        if attn.done == attn.steps:
            jobs.append(("sum", 0, *rows))
        results = work(place, jobs, f"step_{count}")
        if attn.done == attn.steps:
            rows = results.pop()
            rows = (rows, cores(rows, n_tensor))
        if attn.done == attn.steps - 1:
            totals = results.pop(1)
            totals = [totals] + [swap(totals, "tensor", n_tensor, k) for k in range(1, n_tensor)]
        for c in chains:
            c.take(results)
        count += 1
    vecs = call(
        functools.partial(small_kernel, heads, n_tensor),
        [((1, width), FL)] * 5 + [((heads, HEAD), FL)] * 2 + [((1, ff), FL)], totals, "small", 1e6,
    )
    g_up, g_down = call(
        ffn_grads_kernel, [((width, ff), FL), ((ff, width), FL)], (place, ffn.rows, ffn.got), "ffn_grads", 1e6,
        after=vecs[:1], out_space=pltpu.HBM,
    )
    g_up_there = pltpu.with_memory_space_constraint(g_up, pltpu.HBM)
    output, input_grad = call(
        functools.partial(finish_kernel, block), [(x.shape, BF)] * 2,
        (place, x, attn_gain, gh_e, gh_l, hidden_e, hidden_l, *rows, down_bias), "finish", 1e8, after=(g_up_there,),
        out_space=pltpu.HBM,
    )
    output_there = pltpu.with_memory_space_constraint(output, pltpu.HBM)
    g_query, g_key, g_value, g_pos, g_out = call(
        functools.partial(weights_kernel, wide, attn.bit()),
        [((width, wide), FL)] * 4 + [((wide, width), FL)], (place, attn.rows, attn.got), "weights", 1e6,
        [pltpu.VMEM((n_dp * size, width), FL)], after=(output_there,), out_space=pltpu.HBM,
    )
    return (
        output[None],
        input_grad[None],
        vecs[0].reshape(-1),
        vecs[1].reshape(-1),
        g_query,
        g_key,
        g_value,
        g_pos,
        vecs[5],
        vecs[6],
        g_out,
        vecs[2].reshape(-1),
        vecs[3].reshape(-1),
        g_up,
        vecs[7].reshape(-1),
        g_down,
        vecs[4].reshape(-1),
    )


def solution(mesh):
    split, whole = P(None, "tensor"), P()
    return jax.shard_map(
        functools.partial(per_device, mesh.shape["dp"], mesh.shape["tensor"]),
        mesh=mesh,
        in_specs=(
            P("dp", None, None), P("dp", None, None), P("dp"), whole, whole, split, split, split, split,
            P("tensor", None), P("tensor", None), P("tensor", None), whole, whole, split, P("tensor"),
            P("tensor", None), whole, P("dp", None, None),
        ),
        out_specs=(
            P("dp", None, None), P("dp", None, None), whole, whole, split, split, split, split,
            P("tensor", None), P("tensor", None), P("tensor", None), whole, whole, split, P("tensor"),
            P("tensor", None), whole,
        ),
        check_vma=False,
    )
```

```python
import functools

import jax
import jax.numpy as jnp
import numpy as np
from jax import lax
from jax.experimental import pallas as pl
from jax.experimental.pallas import tpu as pltpu
from jax.sharding import PartitionSpec as P

HEAD = 64
BF = jnp.bfloat16
FL = jnp.float32
eps_norm = 1e-05
neg_fill = -1e30
VMEM_LIMIT = 24 * 1024 * 1024
small = 16
UNROLL = [2, 2, 2]


def mm(left, right):
    return lax.dot_general(left, right, (((1,), (0,)), ((), ())), preferred_element_type=FL)


def mm_t(left, right):
    return lax.dot_general(left, right, (((1,), (1,)), ((), ())), preferred_element_type=FL)


def t_mm(left, right):
    return lax.dot_general(left, right, (((0,), (0,)), ((), ())), preferred_element_type=FL)


def norm_parts(rows):
    center = rows - jnp.mean(rows, axis=-1, keepdims=True)
    spread = jnp.mean(center * center, axis=-1, keepdims=True)
    inv = lax.rsqrt(spread + eps_norm)
    return center * inv, inv


def norm_back(scaled, unit, inv):
    flat = jnp.mean(scaled, axis=-1, keepdims=True)
    along = jnp.mean(scaled * unit, axis=-1, keepdims=True)
    return inv * (scaled - flat - unit * along)


def head_lanes(wide, h):
    lane = lax.broadcasted_iota(jnp.int32, (1, wide), 1)
    return (lane >= h * HEAD) & (lane < (h + 1) * HEAD)


def col_sum(rows):
    return jnp.sum(rows, axis=0, keepdims=True)


def loop(count, body, unroll=1):
    def step(i, carry):
        body(i)
        return carry

    lax.fori_loop(0, count, step, 0, unroll=unroll)


def rows_of(i, size):
    return pl.ds(pl.multiple_of(i * size, size), size)


def by_core(core, part, keep_ref, send_ref, rows, at):
    @pl.when(core == part)
    def _():
        keep_ref[at, :] = rows

    @pl.when(core != part)
    def _():
        send_ref[at, :] = rows


def added(left, right):
    return (left.astype(FL) + right.astype(FL)).astype(BF)


def make_queries(normed, spots, at, refs, heads):
    w_ref, wpos_ref, bu, bv, sin_ref, cos_ref, qb_ref, qv_ref = refs
    wide = heads * HEAD
    scale = HEAD ** (-0.5)
    query = mm(normed, w_ref[:, :wide]).astype(BF).astype(FL)
    query_u = (query + bu).astype(BF).astype(FL) * scale
    query_v = (query + bv).astype(BF).astype(FL) * scale
    qv_ref[at, :] = query_v.astype(BF)
    sin = sin_ref[spots, :]
    cos = cos_ref[spots, :]
    half = sin.shape[1]
    for h in range(heads):
        lanes = head_lanes(wide, h)
        qb_ref[h, at, :wide] = jnp.where(lanes, query_u, 0.0).astype(BF)
        coef = mm_t(jnp.where(lanes, query_v, 0.0).astype(BF), wpos_ref[...])
        on_sin, on_cos = coef[:, :half], coef[:, half:]
        qb_ref[h, at, wide : wide + half] = (on_sin * sin + on_cos * cos).astype(BF)
        qb_ref[h, at, wide + half :] = (on_cos * sin - on_sin * cos).astype(BF)


def attend(first, block, mem_len, heads, count, qb_ref, kt_ref, v_ref, probs_ref, ctx_ref, ctx_scr):
    wide = heads * HEAD
    rows = qb_ref.shape[1]
    for part in range(rows // block):
        at = slice(part * block, (part + 1) * block)
        start = first + part * block
        seen = mem_len + start + block

        def one_head(h):
            scores = mm_t(qb_ref[h, at, :], kt_ref[:seen, :])
            query_pos = start + lax.broadcasted_iota(jnp.int32, (block, 1), 0)
            limit = jnp.minimum(query_pos, count - 1)
            key_pos = lax.broadcasted_iota(jnp.int32, (block, seen - mem_len), 1)
            scores = jnp.concatenate(
                [scores[:, :mem_len], jnp.where(key_pos <= limit, scores[:, mem_len:], neg_fill)], axis=1
            )
            expo = jnp.exp(scores - jnp.max(scores, axis=-1, keepdims=True))
            probs = (expo * (1.0 / jnp.sum(expo, axis=-1, keepdims=True))).astype(BF)
            probs_ref[h, at, :seen] = probs
            found = mm(probs, v_ref[:seen, :])
            ctx_scr[...] = jnp.where(head_lanes(wide, h), found, ctx_scr[...])

        loop(heads, one_head, UNROLL[2])
        ctx_ref[at, :] = ctx_scr[...].astype(BF)


def front_kernel(
    first, block, heads,
    place_ref, count_ref, x_in, mem_in, g_in, wq_in, wk_in, wv_in, wpos_in, wup_in, wdown_in, wout_in,
    shift_in, gain_in, fgain_in, fshift_in, upb_in, downb_in, bu_in, bv_in, table_in, sin_in, cos_in,
    x_ref, mem_ref, g_ref, w_ref, wpos_ref, wup_ref, wdown_ref, wout_ref, gain_ref, fgain_ref, fshift_ref, upb_ref,
    downb_ref, sin_ref, cos_ref, bias_ref, normed_ref, kt_ref, v_ref, qb_ref, qv_ref, probs_ref, ctx_ref,
    shift_ref, bu_ref, bv_ref, ctx_scr, sems,
):
    wide = heads * HEAD
    mem_len = mem_in.shape[0]
    seq_len = x_in.shape[0]
    todo = [
        (mem_in, mem_ref), (gain_in, gain_ref), (shift_in, shift_ref), (wk_in, w_ref.at[:, wide : 2 * wide]),
        (wv_in, w_ref.at[:, 2 * wide :]), (x_in, x_ref), (wq_in, w_ref.at[:, :wide]), (bu_in, bu_ref), (bv_in, bv_ref),
        (wpos_in, wpos_ref), (sin_in, sin_ref), (cos_in, cos_ref), (table_in, kt_ref.at[:, wide:]),
        (wout_in, wout_ref), (wup_in, wup_ref), (wdown_in, wdown_ref), (g_in, g_ref), (fgain_in, fgain_ref),
        (fshift_in, fshift_ref), (upb_in, upb_ref), (downb_in, downb_ref),
    ]
    copies = [pltpu.make_async_copy(src, dst, sems.at[i]) for i, (src, dst) in enumerate(todo)]
    for copy in copies:
        copy.start()
    for copy in copies[:5]:
        copy.wait()

    def project(rows_ref, at, to):
        unit, _ = norm_parts(rows_ref[at, :].astype(FL))
        normed = (unit * gain_ref[...] + shift_ref[...]).astype(BF)
        normed_ref[to, :] = normed
        pair = mm(normed, w_ref[:, wide:]).astype(BF)
        kt_ref[to, :wide] = pair[:, :wide]
        v_ref[to, :] = pair[:, wide:]

    def some_memory(i):
        project(mem_ref, rows_of(i, block), rows_of(i, block))

    def some_rows(i):
        project(x_ref, rows_of(i, block), rows_of(i + mem_len // block, block))

    loop(mem_len // block, some_memory, UNROLL[0])
    for copy in copies[5:7]:
        copy.wait()
    loop(seq_len // block, some_rows, UNROLL[0])
    for copy in copies[7:13]:
        copy.wait()
    bias_ref[0:1, :] = jnp.concatenate([bu_ref[h : h + 1, :] for h in range(heads)], axis=1)
    bias_ref[1:2, :] = jnp.concatenate([bv_ref[h : h + 1, :] for h in range(heads)], axis=1)

    def some_queries(i):
        at = rows_of(i, block)
        spots = rows_of(i + first // block, block)
        make_queries(
            normed_ref[rows_of(i + (mem_len + first) // block, block), :], spots, at,
            (w_ref, wpos_ref, bias_ref[0:1, :], bias_ref[1:2, :], sin_ref, cos_ref, qb_ref, qv_ref), heads,
        )

    loop((seq_len - first) // block, some_queries, UNROLL[1])
    attend(first, block, mem_len, heads, count_ref[0], qb_ref, kt_ref, v_ref, probs_ref, ctx_ref, ctx_scr)
    for copy in copies[13:]:
        copy.wait()


def second_kernel(
    first, block, heads, mem_len,
    count_ref, normed_ref, kt_ref, v_ref, w_ref, wpos_ref, bias_ref, sin_ref, cos_ref,
    qb_ref, qv_ref, probs_ref, ctx_ref, ctx_scr,
):
    def some_queries(i):
        at = rows_of(i, block)
        spots = rows_of(i + first // block, block)
        make_queries(
            normed_ref[rows_of(i + (mem_len + first) // block, block), :], spots, at,
            (w_ref, wpos_ref, bias_ref[0:1, :], bias_ref[1:2, :], sin_ref, cos_ref, qb_ref, qv_ref), heads,
        )

    loop(qb_ref.shape[1] // block, some_queries, UNROLL[1])
    attend(first, block, mem_len, heads, count_ref[0], qb_ref, kt_ref, v_ref, probs_ref, ctx_ref, ctx_scr)


def ffn_rows_kernel(
    first, block,
    place_ref, x_ref, c0_ref, c1_ref, c2_ref, c3_ref, o0_ref, o1_ref, o2_ref, o3_ref, gain_ref, shift_ref, up_ref,
    upb_ref, down_ref, g_ref,
    hidden_ref, normed_ref, activ_ref, gpre_ref, upb_out,
):
    upb_out[...] = jnp.zeros(upb_out.shape, FL)

    def one(i):
        at = rows_of(i, block)
        spots = rows_of(i + first // block, block)
        attended = mm(c0_ref[at, :], o0_ref[...]) + mm(c1_ref[at, :], o1_ref[...])
        attended = attended + (mm(c2_ref[at, :], o2_ref[...]) + mm(c3_ref[at, :], o3_ref[...]))
        hidden = x_ref[spots, :].astype(FL) + attended
        hidden_ref[at, :] = hidden
        unit, _ = norm_parts(hidden)
        normed = (unit * gain_ref[...] + shift_ref[...]).astype(BF)
        normed_ref[at, :] = normed
        pre = mm(normed, up_ref[...]) + upb_ref[...]
        cdf = 0.5 + 0.5 * lax.erf(pre * np.float32(0.5**0.5))
        activ_ref[at, :] = (pre * cdf).astype(BF)
        slope = cdf + pre * jnp.exp(-0.5 * pre * pre) * np.float32((2 * np.pi) ** -0.5)
        grads = g_ref[spots, :]
        grad_pre = (mm_t(grads, down_ref[...]) * slope).astype(BF)
        gpre_ref[at, :] = grad_pre
        upb_out[...] += col_sum(grad_pre.astype(FL))

    loop(2, one, 2)


def ffn_back_kernel(block, place_ref, gpre_ref, up_ref, ctx_in, keep_ref, send_ref, back_ref, ctx_out):
    ctx_out[...] = ctx_in[...]
    core = place_ref[0]

    def one(i):
        at = rows_of(i, block)
        back = mm_t(gpre_ref[at, :], up_ref[...])
        back_ref[at, :] = back
        by_core(core, i, keep_ref, send_ref, back.astype(BF), slice(0, block))

    loop(2, one, 2)


def ffn_sums(first, back_ref, hidden_ref, g_ref, vec_ref):
    size = back_ref.shape[0]
    back = back_ref[...]
    unit, _ = norm_parts(hidden_ref[...])
    vec_ref[0:1, :] = col_sum(back * unit)
    vec_ref[1:2, :] = col_sum(back)
    vec_ref[2:3, :] = col_sum(g_ref[first : first + size, :].astype(FL))


def ffn_late_kernel(
    first, place_ref, activ_ref, gpre_ref, normed_ref, down_ref, g_ref, back_ref, hidden_ref,
    share_ref, up_out, down_out, vec_ref,
):
    size = activ_ref.shape[0]
    activ = activ_ref[...]
    share_ref[...] = mm(activ, down_ref[...]).astype(BF)
    down_out[...] = t_mm(activ, g_ref[first : first + size, :])
    up_out[...] = t_mm(normed_ref[...], gpre_ref[...])
    ffn_sums(first, back_ref, hidden_ref, g_ref, vec_ref)


def ffn_early_kernel(
    first,
    place_ref, activ_ref, gpre_ref, normed_ref, down_ref, g_ref, back_ref, hidden_ref, late_ref, up_in, down_in, sum_ref,
    got_ref,
    share_ref, up_keep, up_send, down_keep, down_send, sum_out, vec_ref,
):
    sum_out[...] = added(sum_ref[...], got_ref[...])
    size = activ_ref.shape[0]
    activ = activ_ref[...]
    up = up_in[...] + t_mm(normed_ref[...], gpre_ref[...])
    halve(place_ref, 0, up.astype(BF), up_keep, up_send)
    down = down_in[...] + t_mm(activ, g_ref[first : first + size, :])
    halve(place_ref, 1, down.astype(BF), down_keep, down_send)
    share_ref[:size, :] = mm(activ, down_ref[...]).astype(BF)
    share_ref[size:, :] = late_ref[...]
    ffn_sums(first, back_ref, hidden_ref, g_ref, vec_ref)


def back_rows(
    first, block, heads, mem_len, place_ref, hidden_ref, mine_ref, other_ref, g_ref, fgain_ref, wout_ref, ctx_ref,
    probs_ref, qb_ref, qv_ref, kt_ref, v_ref, wpos_ref, sin_ref, cos_ref,
    gh_ref, dk_ref, dv_ref, dpos_ref, dout_ref, dq_ref, bias_ref, grad_u, grad_v,
):
    core = place_ref[0]
    wide = heads * HEAD
    half = sin_ref.shape[1]
    scale = HEAD ** (-0.5)
    for part in range(2):
        at = slice(part * block, (part + 1) * block)
        spots = slice(first + part * block, first + (part + 1) * block)
        seen = mem_len + first + (part + 1) * block
        unit, inv = norm_parts(hidden_ref[at, :])
        summed = jnp.where(core == part, mine_ref[...].astype(FL), other_ref[...].astype(FL))
        grad_hidden = g_ref[spots, :].astype(FL) + norm_back(summed * fgain_ref[...], unit, inv)
        gh_ref[at, :] = grad_hidden
        gh = grad_hidden.astype(BF)
        context = ctx_ref[at, :]
        grad_context = mm_t(gh, wout_ref[...]).astype(BF).astype(FL)
        dout_ref[...] += t_mm(context, gh)
        along_context = grad_context * context.astype(FL)

        def one_head(h):
            lanes = head_lanes(wide, h)
            delta = jnp.sum(jnp.where(lanes, along_context, 0.0), axis=-1, keepdims=True)
            own = jnp.where(lanes, grad_context, 0.0).astype(BF)
            probs = probs_ref[h, at, :seen]
            grad_score = (probs.astype(FL) * (mm_t(own, v_ref[:seen, :]) - delta)).astype(BF)
            dv_ref[:, :seen] += t_mm(own, probs)
            dk_ref[:, :seen] += t_mm(qb_ref[h, at, :wide], grad_score)
            spread = mm(grad_score, kt_ref[:seen, :])
            grad_u[...] = jnp.where(lanes, spread[:, :wide], grad_u[...])
            sin = sin_ref[spots, :]
            cos = cos_ref[spots, :]
            on_cos, on_sin = spread[:, wide : wide + half], spread[:, wide + half :]
            turned = jnp.concatenate(
                [(on_cos * sin - on_sin * cos).astype(BF), (on_cos * cos + on_sin * sin).astype(BF)], axis=1
            )
            grad_v[...] = jnp.where(lanes, mm(turned, wpos_ref[...]), grad_v[...])
            query_v = jnp.where(lanes, qv_ref[at, :].astype(FL), 0.0).astype(BF)
            dpos_ref[...] += t_mm(query_v, turned)

        loop(heads, one_head, 2)
        bias_ref[0:1, :] += col_sum(grad_u[...]) * scale
        bias_ref[1:2, :] += col_sum(grad_v[...]) * scale
        dq_ref[at, :] = ((grad_u[...] + grad_v[...]) * scale).astype(BF)


def back_share(cols, dq_rows, unit, dk_ref, dv_ref, weights):
    pair = [dk_ref[:, cols].T.astype(BF), dv_ref[:, cols].T.astype(BF)]
    back = mm_t(jnp.concatenate(dq_rows + pair, axis=1), weights)
    return back, col_sum(back * unit), col_sum(back)


def back_late_kernel(
    first, block, heads, mem_len,
    place_ref, hidden_ref, mine_ref, other_ref, g_ref, fgain_ref, wout_ref, ctx_ref, probs_ref, qb_ref, qv_ref, kt_ref,
    v_ref, wpos_ref, sin_ref, cos_ref, x_ref, w_ref,
    gh_ref, dk_ref, dv_ref, dpos_ref, dout_ref, dq_ref, bias_ref, share_ref, vec_ref, grad_u, grad_v,
):
    for ref in (dk_ref, dv_ref, dpos_ref, dout_ref, bias_ref):
        ref[...] = jnp.zeros(ref.shape, FL)
    back_rows(
        first, block, heads, mem_len, place_ref, hidden_ref, mine_ref, other_ref, g_ref, fgain_ref, wout_ref, ctx_ref,
        probs_ref, qb_ref, qv_ref, kt_ref, v_ref, wpos_ref, sin_ref, cos_ref,
        gh_ref, dk_ref, dv_ref, dpos_ref, dout_ref, dq_ref, bias_ref, grad_u, grad_v,
    )
    vec_ref[...] = jnp.zeros(vec_ref.shape, FL)
    for part in range(2):
        at = slice(part * block, (part + 1) * block)
        spots = slice(first + part * block, first + (part + 1) * block)
        cols = slice(mem_len + first + part * block, mem_len + first + (part + 1) * block)
        unit, _ = norm_parts(x_ref[spots, :].astype(FL))
        back, gain_sum, shift_sum = back_share(cols, [dq_ref[at, :]], unit, dk_ref, dv_ref, w_ref[...])
        share_ref[at, :] = back.astype(BF)
        vec_ref[0:1, :] += gain_sum
        vec_ref[1:2, :] += shift_sum


def back_early_kernel(
    first, block, heads, mem_len,
    place_ref, hidden_ref, mine_ref, other_ref, g_ref, fgain_ref, wout_ref, ctx_ref, probs_ref, qb_ref, qv_ref, kt_ref,
    v_ref, wpos_ref, sin_ref, cos_ref, dk_in, dv_in, dpos_in, dout_in, bias_in,
    gh_ref, dk_ref, dv_ref, dpos_ref, dout_ref, dq_ref, bias_ref, grad_u, grad_v,
):
    for ref, old in ((dk_ref, dk_in), (dv_ref, dv_in), (dpos_ref, dpos_in), (dout_ref, dout_in), (bias_ref, bias_in)):
        ref[...] = old[...]
    back_rows(
        first, block, heads, mem_len, place_ref, hidden_ref, mine_ref, other_ref, g_ref, fgain_ref, wout_ref, ctx_ref,
        probs_ref, qb_ref, qv_ref, kt_ref, v_ref, wpos_ref, sin_ref, cos_ref,
        gh_ref, dk_ref, dv_ref, dpos_ref, dout_ref, dq_ref, bias_ref, grad_u, grad_v,
    )


def back_end_kernel(
    first, block, heads, mem_len, n_tensor, size,
    place_ref, x_ref, w_ref, mem_ref, normed_ref, dk_ref, dv_ref, dpos_ref, dout_ref, dq_ref, bias_ref, dq_in, late_ref,
    vec_in, vec_l, vec_e, upb_l, upb_e, ffn_ref, up_keep,
    up_got, down_keep, down_got,
    keep_ref, send_ref, a_keep, a_send, f_ref, vec_ref,
):
    half = up_keep.shape[0]
    f_ref[:half, :] = added(up_keep[...], up_got[...])
    f_ref[half:, :] = added(down_keep[...], down_got[...])
    wide = heads * HEAD
    core = place_ref[0]
    for part in range(2):
        at = slice(part * block, (part + 1) * block)
        by_core(core, part, keep_ref, send_ref, late_ref[at, :], slice(block, 2 * block))
        by_core(core, part, keep_ref, send_ref, ffn_ref[at, :], slice(2 * block, 3 * block))
        at = slice((part + 2) * block, (part + 3) * block)
        by_core(core, part, keep_ref, send_ref, ffn_ref[at, :], slice(3 * block, 4 * block))
    normed = normed_ref[...]
    dq_all = jnp.concatenate([dq_ref[...], dq_in[...]], axis=0)
    grads = [
        t_mm(dq_all, normed[mem_len:]),
        mm(dk_ref[...].astype(BF), normed),
        mm(dv_ref[...].astype(BF), normed),
        dpos_ref[...],
        dout_ref[...],
    ]
    grads = jnp.concatenate(grads, axis=0)
    vec_ref[...] = vec_in[...]
    for part in range(2):
        at = slice(part * block, (part + 1) * block)
        spots = slice(first + part * block, first + (part + 1) * block)
        cols = slice(mem_len + first + part * block, mem_len + first + (part + 1) * block)
        unit, _ = norm_parts(x_ref[spots, :].astype(FL))
        back, gain_sum, shift_sum = back_share(cols, [dq_ref[at, :]], unit, dk_ref, dv_ref, w_ref[...])
        by_core(core, part, keep_ref, send_ref, back.astype(BF), slice(0, block))
        vec_ref[0:1, :] += gain_sum
        vec_ref[1:2, :] += shift_sum
    for at in range(0, mem_len, block):
        cols = slice(at, at + block)
        unit, _ = norm_parts(mem_ref[cols, :].astype(FL))
        _, gain_sum, shift_sum = back_share(cols, [], unit, dk_ref, dv_ref, w_ref[:, wide:])
        vec_ref[0:1, :] += gain_sum
        vec_ref[1:2, :] += shift_sum
    width = vec_ref.shape[1]
    wider = jnp.zeros((1, width - wide), FL)
    rows = [vec_ref[...], vec_l[0:2, :] + vec_e[0:2, :], (vec_l[2:3, :] + vec_e[2:3, :]) * (1.0 / n_tensor)]
    rows += [jnp.concatenate([bias_ref[i : i + 1, :], wider], axis=1) for i in range(2)]
    for i in range(upb_l.shape[1] // width):
        cols = slice(i * width, (i + 1) * width)
        rows.append(upb_l[:, cols] + upb_e[:, cols])
    rows.append(jnp.zeros((small - 7 - upb_l.shape[1] // width, width), FL))
    rows = jnp.concatenate(rows, axis=0).astype(BF)
    step = size + small
    for d in range(2 * a_keep.shape[0] // step):
        here = max(0, min(size, 5 * wide - d * size))
        piece = [grads[d * size : d * size + here].astype(BF)] if here else []
        piece += [jnp.zeros((size - here, width), BF)] if here < size else []
        piece = jnp.concatenate([*piece, rows], axis=0)
        per_half = a_keep.shape[0] // step
        at = slice(d % per_half * step, (d % per_half + 1) * step)
        by_core(place_ref[1] & 1, d // per_half, a_keep, a_send, piece, at)


def weights_kernel(wide, bit, place_ref, mine_ref, got_ref, *refs):
    outs, rows_ref = refs[:5], refs[5]
    join(place_ref, bit, mine_ref, got_ref, rows_ref)
    for i in range(4):
        outs[i][...] = rows_ref[i * wide : (i + 1) * wide, :].T
    outs[4][...] = rows_ref[4 * wide : 5 * wide, :]


def small_kernel(heads, n_tensor, *refs):
    mine, outs = refs[0], refs[n_tensor:]
    total = mine[...]
    for other in refs[1:n_tensor]:
        total = total + other[...]
    for i in range(5):
        outs[i][...] = total[i : i + 1, :]
    for k in range(2):
        for h in range(heads):
            outs[5 + k][h : h + 1, :] = mine[5 + k : 6 + k, h * HEAD : (h + 1) * HEAD]
    width = mine.shape[1]
    for i in range(outs[7].shape[1] // width):
        outs[7][:, i * width : (i + 1) * width] = mine[7 + i : 8 + i, :]


def ffn_grads_kernel(up_rows, down_rows, up_ref, down_ref):
    up_ref[...] = up_rows[...].astype(FL)
    down_ref[...] = down_rows[...].astype(FL)


def finish_kernel(
    block, place_ref, x_ref, gain_ref, gh_e, gh_l, hidden_e, hidden_l, mine_ref, other_ref, bias_ref, out_ref, grad_ref
):
    core = place_ref[0]

    def some_rows(gh_ref, hidden_ref, first):
        def body(i):
            at = rows_of(i, block)
            spots = rows_of(i + 2 * first, block)

            def summed(group):
                rows = slice(group * block, (group + 1) * block)
                return jnp.where(core == i, mine_ref[rows, :].astype(FL), other_ref[rows, :].astype(FL))

            unit, inv = norm_parts(x_ref[spots, :].astype(FL))
            grad_ref[spots, :] = (gh_ref[at, :] + norm_back(summed(first) * gain_ref[...], unit, inv)).astype(BF)
            out_ref[spots, :] = (hidden_ref[at, :] + summed(first + 2) + bias_ref[...]).astype(BF)

        return body

    loop(2, some_rows(gh_e, hidden_e, 0))
    loop(2, some_rows(gh_l, hidden_l, 1))


def halve(place_ref, bit, total, keep_ref, send_ref):
    size = total.shape[0] // 2
    high = (place_ref[1] >> bit) & 1
    by_core(high, 0, keep_ref, send_ref, total[:size], slice(None))
    by_core(high, 1, keep_ref, send_ref, total[size:], slice(None))


def join(place_ref, bit, mine_ref, got_ref, out_ref):
    size = mine_ref.shape[0]
    high = ((place_ref[1] >> bit) & 1) == 1
    mine, got = mine_ref[...].astype(FL), got_ref[...].astype(FL)
    out_ref[:size, :] = jnp.where(high, got, mine).astype(out_ref.dtype)
    out_ref[size:, :] = jnp.where(high, mine, got).astype(out_ref.dtype)


SMEM = pl.BlockSpec(memory_space=pltpu.SMEM)
SPECS = {s: pl.BlockSpec(memory_space=s) for s in (pltpu.VMEM, pltpu.HBM)}


def call(kernel, outs, args, name, flops, scratch=(), space=pltpu.VMEM, after=(), out_space=None):
    count, extra = len(args), len(after)

    def body(*refs):
        kernel(*refs[:count], *refs[count + extra :])

    specs = [SMEM if a.dtype == jnp.int32 else SPECS[space] for a in args]
    specs += [pl.BlockSpec(memory_space=pl.ANY)] * extra
    if space is pltpu.HBM:
        args = [a if a.dtype == jnp.int32 else pltpu.with_memory_space_constraint(a, space) for a in args]
    return pl.pallas_call(
        body,
        out_shape=[out_space(s, d) if out_space else jax.ShapeDtypeStruct(s, d) for s, d in outs],
        in_specs=specs,
        out_specs=[SPECS[pltpu.VMEM]] * len(outs),
        scratch_shapes=scratch,
        compiler_params=pltpu.CompilerParams(vmem_limit_bytes=VMEM_LIMIT),
        cost_estimate=pl.CostEstimate(flops=1, bytes_accessed=1, transcendentals=0),
        name=name,
    )(*args, *after)


def swap(rows, axis, size, bit):
    return lax.ppermute(rows, axis, [(i, i ^ bit) for i in range(size)])


def work_kernel(jobs, place_ref, *refs):
    ins, outs = refs[: 2 * len(jobs)], list(refs[2 * len(jobs) :])
    for i, (kind, bit) in enumerate(jobs):
        mine, got = ins[2 * i : 2 * i + 2]
        if kind == "halve":
            halve(place_ref, bit, added(mine[...], got[...]), outs.pop(0), outs.pop(0))
        elif kind == "join":
            join(place_ref, bit, mine, got, outs.pop(0))
        elif kind == "sum":
            outs.pop(0)[...] = added(mine[...], got[...])
        else:
            total = mine[...].astype(FL) + got[...].astype(FL)
            size = outs[0].shape[0]
            for part in (total[:size], total[size:]):
                out = outs.pop(0)
                out[...] = part.astype(out.dtype)


def work(place, jobs, name, after=()):
    outs = []
    for kind, _, mine, _ in jobs:
        size, width = mine.shape
        outs += {
            "halve": [((size // 2, width), BF)] * 2,
            "two": [((size // 2, width), BF)] * 2,
            "join": [((2 * size, width), BF)],
            "sum": [((size, width), BF)],
            "split": [((size - small, width), BF), ((small, width), FL)],
        }[kind]
    args = [a for job in jobs for a in job[2:]]
    return list(
        call(functools.partial(work_kernel, [job[:2] for job in jobs]), outs, (place, *args), name, 1e6, after=after)
    )


class Chain:
    def __init__(self, rows, send, bits, n_dp, end="sum"):
        self.rows, self.send, self.bits, self.n_dp, self.end, self.done = rows, send, bits, n_dp, end, 0
        self.start()

    def bit(self):
        return self.bits[min(self.done, 2 * len(self.bits) - 2 - self.done)]

    def start(self):
        self.got = swap(self.send, "dp", self.n_dp, 1 << self.bit())

    def left(self):
        return 2 * len(self.bits) - 2 - self.done

    def job(self):
        last = len(self.bits) - 1
        if self.done < last - 1:
            kind, bit = "halve", self.bits[self.done + 1]
        elif self.done <= last:
            kind, bit = (self.end if self.done == last else "sum"), 0
        else:
            kind, bit = "join", self.bit()
        return kind, bit, self.rows, self.got

    def take(self, results):
        kind = self.job()[0]
        self.rows = self.send = results.pop(0)
        if kind == "halve":
            self.send = results.pop(0)
        self.done += 1
        if self.left() >= 0:
            self.start()


def cores(rows, n_tensor):
    return swap(rows, "tensor", n_tensor, 1)


def other_chips(rows, n_tensor):
    return swap(rows, "tensor", n_tensor, 2)


def chips(rows, n_tensor):
    return rows, other_chips(rows, n_tensor)


def copy_kernel(in_ref, out_ref):
    out_ref[...] = in_ref[...]


def per_device(n_dp, n_tensor, *args):
    (inputs, memory, counts, attn_gain, attn_shift, w_query, w_key, w_value, w_pos, bias_u, bias_v, w_out,
     ffn_gain, ffn_shift, w_up, up_bias, w_down, down_bias, out_grad) = args
    _, seq_len, width = inputs.shape
    mem_len = memory.shape[1]
    total = mem_len + seq_len
    wide = w_query.shape[1]
    heads = wide // HEAD
    ff = w_up.shape[1]
    chunk = seq_len // 2
    block = chunk // 2
    late = chunk
    place = jnp.stack([lax.axis_index("tensor") & 1, lax.axis_index("dp")]).astype(jnp.int32)
    x, mem, g = inputs[0], memory[0], out_grad[0]
    row = lambda v: v.reshape(1, -1)

    freq = 1.0 / 10000.0 ** (np.arange(0, width, 2, dtype=np.float64) / width)
    key_phase = np.arange(total)[:, None] * freq[None, :]
    table = jnp.asarray(np.concatenate([np.cos(key_phase), np.sin(key_phase)], axis=1).astype(BF))
    row_phase = (np.arange(seq_len) + mem_len)[:, None] * freq[None, :]
    sin = jnp.asarray(np.sin(row_phase).astype(np.float32))
    cos = jnp.asarray(np.cos(row_phase).astype(np.float32))

    outs_of = [w_out] + [swap(w_out, "tensor", n_tensor, k) for k in range(1, n_tensor)]

    def attend_outs(seen):
        return [((heads, chunk, wide + width), BF), ((chunk, wide), BF), ((heads, chunk, seen), BF), ((chunk, wide), BF)]

    ctx_scr = pltpu.VMEM((block, wide), FL)
    vectors = [row(v) for v in (attn_shift, attn_gain, ffn_gain, ffn_shift, up_bias, down_bias)]
    copied = [
        *[(a.shape, BF) for a in (x, mem, g)], ((width, 3 * wide), BF), *[(a.shape, BF) for a in (w_pos, w_up, w_down, w_out)],
        *[(a.shape, FL) for a in (*vectors[1:], sin, cos)], ((2, wide), FL),
    ]
    found = call(
        functools.partial(front_kernel, late, block, heads),
        [*copied, ((total, width), BF), ((total, wide + width), BF), ((total, wide), BF), *attend_outs(total)],
        (place, counts, x, mem, g, w_query, w_key, w_value, w_pos, w_up, w_down, w_out, *vectors, bias_u, bias_v, table, sin,
         cos), "front", 6e9,
        [pltpu.VMEM((1, width), FL)] + [pltpu.VMEM(bias_u.shape, FL)] * 2 + [ctx_scr, pltpu.SemaphoreType.DMA((21,))],
        pltpu.HBM,
    )
    x, mem, g, weights, w_pos, w_up, w_down, w_out = found[:8]
    attn_gain, ffn_gain, ffn_shift, up_bias, down_bias, sin, cos, biases, normed, keys, values, *saved_l = found[8:]
    ctx_l = [saved_l[-1], cores(saved_l[-1], n_tensor), swap(saved_l[-1], "tensor", n_tensor, 2)]
    saved_e = call(
        functools.partial(second_kernel, 0, block, heads, mem_len),
        attend_outs(mem_len + chunk),
        (counts, normed, keys, values, weights, w_pos, biases, sin, cos), "second", 4e9, [ctx_scr],
    )
    ctx_e = [saved_e[-1], cores(saved_e[-1], n_tensor), swap(saved_e[-1], "tensor", n_tensor, 2)]
    (relay,) = call(copy_kernel, [(ctx_l[2].shape, BF)], (ctx_l[2],), "relay_late", 1e6, after=saved_e[-1:])
    ctx_l.append(cores(relay, n_tensor))

    def ffn_rows(first, ctx, name, after):
        return call(
            functools.partial(ffn_rows_kernel, first, block),
            [((chunk, width), FL), ((chunk, width), BF), ((chunk, ff), BF), ((chunk, ff), BF), ((1, ff), FL)],
            (place, x, *ctx, *outs_of, ffn_gain, ffn_shift, w_up, up_bias, w_down, g), name, 2e9, after=after,
        )

    def ffn_back(gpre, relayed, name):
        return call(
            functools.partial(ffn_back_kernel, block),
            [((block, width), BF)] * 2 + [((chunk, width), FL), ((chunk, wide), BF)], (place, gpre, w_up, relayed), name, 1e9,
        )

    hidden_l, normed_l, activ, gpre, upb_l = ffn_rows(late, ctx_l, "ffn_rows_late", saved_e[-1:])
    keep_l, send, back, relay = ffn_back(gpre, ctx_e[2], "ffn_back_late")
    gnt_l = cores(send, n_tensor)
    ctx_e.append(cores(relay, n_tensor))
    share, up_l, down_l, vec_l = call(
        functools.partial(ffn_late_kernel, late),
        [((chunk, width), BF), ((width, ff), FL), ((ff, width), FL), ((3, width), FL)],
        (place, activ, gpre, normed_l, w_down, g, back, hidden_l), "ffn_late", 1e9,
    )
    (gnt_l,) = work(place, [("sum", 0, keep_l, gnt_l)], "add_late", (share,))
    gnt_l = chips(gnt_l, n_tensor)
    hidden_e, normed_e, activ, gpre, upb_e = ffn_rows(0, ctx_e, "ffn_rows_early", gnt_l[:1])
    keep_e, send, back, _ = ffn_back(gpre, saved_e[-1], "ffn_back_early")
    gnt_e = cores(send, n_tensor)
    share, *halves, gnt_l, vec_e = call(
        functools.partial(ffn_early_kernel, 0),
        [(x.shape, BF)] + [((width // 2, ff), BF)] * 2 + [((ff // 2, width), BF)] * 2 + [((block, width), BF), ((3, width), FL)],
        (place, activ, gpre, normed_e, w_down, g, back, hidden_e, share, up_l, down_l, *gnt_l), "ffn_early", 1e9,
    )
    gnt_l = (gnt_l, cores(gnt_l, n_tensor))
    up_keep, up_send, down_keep, down_send = halves
    up_got = swap(up_send, "dp", n_dp, 1)
    down_got = swap(down_send, "dp", n_dp, 2)
    (gnt_e,) = work(place, [("sum", 0, keep_e, gnt_e)], "add_early", (up_keep,))
    gnt_e = chips(gnt_e, n_tensor)

    sums = [((wide, total), FL), ((wide, total), FL), ((wide, width), FL), ((wide, width), FL), ((chunk, wide), BF)]
    turn_scr = [ctx_scr, ctx_scr]

    def back_args(hidden, gnt, saved):
        qb, qv, probs, ctx = saved
        return (place, hidden, *gnt, g, ffn_gain, w_out, ctx, probs, qb, qv, keys, values, w_pos, sin, cos, x, weights)

    gh_l, dk, dv, dpos, dout, dq, bias, part, vec = call(
        functools.partial(back_late_kernel, late, block, heads, mem_len),
        [((chunk, width), FL), *sums, ((2, wide), FL), ((chunk, width), BF), ((2, width), FL)],
        back_args(hidden_l, gnt_l, saved_l), "back_late", 8e9, turn_scr,
    )
    gnt_e, up_keep, up_send, down_keep, down_send = work(
        place, [("sum", 0, *gnt_e), ("halve", 1, up_keep, up_got), ("halve", 0, down_keep, down_got)], "add_middle", (vec,)
    )
    up_got = swap(up_send, "dp", n_dp, 2)
    down_got = swap(down_send, "dp", n_dp, 1)
    gnt_e = (gnt_e, cores(gnt_e, n_tensor))
    groups = n_dp // 2
    size = max(16, -(-5 * wide // groups // 16) * 16)
    gh_e, dk, dv, dpos, dout, dq_e, bias = call(
        functools.partial(back_early_kernel, 0, block, heads, mem_len),
        [((chunk, width), FL), *sums, ((2, wide), FL)],
        (*back_args(hidden_e, gnt_e, saved_e)[:-2], dk, dv, dpos, dout, bias), "back_early", 6e9, turn_scr,
    )
    keep, send, a_keep, a_send, f_rows = call(
        functools.partial(back_end_kernel, 0, block, heads, mem_len, n_tensor, size),
        [*[((seq_len, width), BF)] * 2, *[((groups // 2 * (size + small), width), BF)] * 2, ((chunk // 2, width), BF)],
        (place, x, weights, mem, normed, dk, dv, dpos, dout, dq_e, bias, dq, part, vec, vec_l, vec_e, upb_l, upb_e, share,
         up_keep, up_got, down_keep, down_got),
        "back_end", 6e9, [pltpu.VMEM((2, width), FL)],
    )
    bits = list(range((n_dp - 1).bit_length()))
    attn = Chain(a_keep, a_send, bits, n_dp, "split")
    if len(bits) > 3:
        f_rows, f_send = work(place, [("halve", 2, f_rows, jnp.zeros_like(f_rows))], "halve_ffn")
    else:
        f_send = f_rows
    ffn = Chain(f_rows, f_send, bits[2:], n_dp, "two" if len(bits) == 3 else "sum")
    rows = (keep, cores(send, n_tensor))
    count, stage = 0, 0
    while attn.left() > 0:
        jobs = [attn.job()]
        if stage == 0:
            jobs.append(ffn.job())
        elif stage < 3:
            jobs += [("join", 2 - stage, up, up_got), ("join", stage - 1, down, down_got)]
        if count == 0 or attn.left() == 1:
            jobs.append(("sum", 0, *rows))
        results = work(place, jobs, f"step_{count}")
        if attn.job()[0] == "split":
            totals = results.pop(1)
            totals = [totals] + [swap(totals, "tensor", n_tensor, k) for k in range(1, n_tensor)]
        if count == 0 or attn.left() == 1:
            rows = results.pop()
            rows = (rows, (other_chips if count == 0 else cores)(rows, n_tensor))
        attn.take(results)
        if stage == 0 and ffn.left() > 0:
            ffn.take(results)
        elif stage < 3:
            up, down = results if len(results) == 2 else (results[0][: chunk // 4], results[0][chunk // 4 :])
            if stage < 2:
                up_got, down_got = swap(up, "dp", n_dp, 2 >> stage), swap(down, "dp", n_dp, 1 << stage)
            stage += 1
        count += 1
    output, input_grad = call(
        functools.partial(finish_kernel, block), [(x.shape, BF)] * 2,
        (place, x, attn_gain, gh_e, gh_l, hidden_e, hidden_l, *rows, down_bias), "finish", 1e8,
        out_space=pltpu.HBM,
    )
    output_there = pltpu.with_memory_space_constraint(output, pltpu.HBM)
    vecs = call(
        functools.partial(small_kernel, heads, n_tensor),
        [((1, width), FL)] * 5 + [((heads, HEAD), FL)] * 2 + [((1, ff), FL)], totals, "small", 1e6, after=(output_there,),
    )
    g_up, g_down = call(
        ffn_grads_kernel, [((width, ff), FL), ((ff, width), FL)], (up, down), "ffn_grads", 1e6,
        out_space=pltpu.HBM, after=vecs[5:6],
    )
    g_up_there = pltpu.with_memory_space_constraint(g_up, pltpu.HBM)
    g_query, g_key, g_value, g_pos, g_out = call(
        functools.partial(weights_kernel, wide, attn.bit()),
        [((width, wide), FL)] * 4 + [((wide, width), FL)], (place, attn.rows, attn.got), "weights", 1e6,
        [pltpu.VMEM((groups * size, width), FL)], after=(g_up_there,), out_space=pltpu.HBM,
    )
    return (
        output[None],
        input_grad[None],
        vecs[0].reshape(-1),
        vecs[1].reshape(-1),
        g_query,
        g_key,
        g_value,
        g_pos,
        vecs[5],
        vecs[6],
        g_out,
        vecs[2].reshape(-1),
        vecs[3].reshape(-1),
        g_up,
        vecs[7].reshape(-1),
        g_down,
        vecs[4].reshape(-1),
    )


def solution(mesh):
    split, whole = P(None, "tensor"), P()
    return jax.shard_map(
        functools.partial(per_device, mesh.shape["dp"], mesh.shape["tensor"]),
        mesh=mesh,
        in_specs=(
            P("dp", None, None), P("dp", None, None), P("dp"), whole, whole, split, split, split, split,
            P("tensor", None), P("tensor", None), P("tensor", None), whole, whole, split, P("tensor"),
            P("tensor", None), whole, P("dp", None, None),
        ),
        out_specs=(
            P("dp", None, None), P("dp", None, None), whole, whole, split, split, split, split,
            P("tensor", None), P("tensor", None), P("tensor", None), whole, whole, split, P("tensor"),
            P("tensor", None), whole,
        ),
        check_vma=False,
    )
```

```python
import functools

import jax
import jax.numpy as jnp
import numpy as np
from jax import lax
from jax.experimental import pallas as pl
from jax.experimental.pallas import tpu as pltpu
from jax.sharding import PartitionSpec as P

HEAD = 64
BF = jnp.bfloat16
FL = jnp.float32
eps_norm = 1e-05
neg_fill = -1e30
VMEM_LIMIT = 24 * 1024 * 1024
small = 16
UNROLL = [2, 2, 2]
STEP_COST = 5e9


def mm(left, right):
    return lax.dot_general(left, right, (((1,), (0,)), ((), ())), preferred_element_type=FL)


def mm_t(left, right):
    return lax.dot_general(left, right, (((1,), (1,)), ((), ())), preferred_element_type=FL)


def t_mm(left, right):
    return lax.dot_general(left, right, (((0,), (0,)), ((), ())), preferred_element_type=FL)


def norm_parts(rows):
    center = rows - jnp.mean(rows, axis=-1, keepdims=True)
    spread = jnp.mean(center * center, axis=-1, keepdims=True)
    inv = lax.rsqrt(spread + eps_norm)
    return center * inv, inv


def norm_back(scaled, unit, inv):
    flat = jnp.mean(scaled, axis=-1, keepdims=True)
    along = jnp.mean(scaled * unit, axis=-1, keepdims=True)
    return inv * (scaled - flat - unit * along)


def head_lanes(wide, h):
    lane = lax.broadcasted_iota(jnp.int32, (1, wide), 1)
    return (lane >= h * HEAD) & (lane < (h + 1) * HEAD)


def col_sum(rows):
    return jnp.sum(rows, axis=0, keepdims=True)


def fine_mm(left, right, product):
    high = left.astype(BF)
    low = (left - high.astype(FL)).astype(BF)
    return product(high, right) + product(low, right)


def norm_sums(weighted, shift_sum, gain, shift):
    return (weighted - shift * shift_sum) / gain, shift_sum


def loop(count, body, unroll=1):
    def step(i, carry):
        body(i)
        return carry

    lax.fori_loop(0, count, step, 0, unroll=unroll)


def rows_of(i, size):
    return pl.ds(pl.multiple_of(i * size, size), size)


def by_core(core, part, keep_ref, send_ref, rows, at):
    @pl.when(core == part)
    def _():
        keep_ref[at, :] = rows

    @pl.when(core != part)
    def _():
        send_ref[at, :] = rows


def added(left, right):
    return (left.astype(FL) + right.astype(FL)).astype(BF)


def make_queries(normed, spots, at, refs, heads):
    w_ref, wpos_ref, bu, bv, sin_ref, cos_ref, qb_ref, qv_ref = refs
    wide = heads * HEAD
    scale = HEAD ** (-0.5)
    query = mm(normed, w_ref[:, :wide]).astype(BF).astype(FL)
    query_u = (query + bu).astype(BF).astype(FL) * scale
    query_v = (query + bv).astype(BF).astype(FL) * scale
    qv_ref[at, :] = query_v.astype(BF)
    sin = sin_ref[spots, :]
    cos = cos_ref[spots, :]
    half = sin.shape[1]
    for h in range(heads):
        lanes = head_lanes(wide, h)
        qb_ref[h, at, :wide] = jnp.where(lanes, query_u, 0.0).astype(BF)
        coef = mm_t(jnp.where(lanes, query_v, 0.0).astype(BF), wpos_ref[...])
        on_sin, on_cos = coef[:, :half], coef[:, half:]
        qb_ref[h, at, wide : wide + half] = (on_sin * sin + on_cos * cos).astype(BF)
        qb_ref[h, at, wide + half :] = (on_cos * sin - on_sin * cos).astype(BF)


def attend(first, block, mem_len, heads, count, qb_ref, kt_ref, v_ref, probs_ref, ctx_ref, ctx_scr):
    wide = heads * HEAD
    rows = qb_ref.shape[1]
    for part in range(rows // block):
        at = slice(part * block, (part + 1) * block)
        start = first + part * block
        seen = mem_len + start + block

        def one_head(h):
            scores = mm_t(qb_ref[h, at, :], kt_ref[:seen, :])
            query_pos = start + lax.broadcasted_iota(jnp.int32, (block, 1), 0)
            limit = jnp.minimum(query_pos, count - 1)
            key_pos = lax.broadcasted_iota(jnp.int32, (block, seen - mem_len), 1)
            scores = jnp.concatenate(
                [scores[:, :mem_len], jnp.where(key_pos <= limit, scores[:, mem_len:], neg_fill)], axis=1
            )
            expo = jnp.exp(scores - jnp.max(scores, axis=-1, keepdims=True))
            probs = (expo * (1.0 / jnp.sum(expo, axis=-1, keepdims=True))).astype(BF)
            probs_ref[h, at, :seen] = probs
            found = mm(probs, v_ref[:seen, :])
            ctx_scr[...] = jnp.where(head_lanes(wide, h), found, ctx_scr[...])

        loop(heads, one_head, UNROLL[2])
        ctx_ref[at, :] = ctx_scr[...].astype(BF)


def front_kernel(
    block, heads,
    place_ref, x_in, mem_in, g_in, wq_in, wk_in, wv_in, wpos_in, wup_in, wdown_in, wout_in,
    shift_in, gain_in, fgain_in, fshift_in, upb_in, downb_in, bu_in, bv_in, table_in, sin_in, cos_in,
    x_ref, g_ref, w_ref, wpos_ref, wup_ref, wdown_ref, wout_ref, shift_ref, gain_ref, fgain_ref, fshift_ref, upb_ref,
    downb_ref, sin_ref, cos_ref, bias_ref, normed_ref, kt_ref, v_ref,
    mem_ref, bu_ref, bv_ref, sems,
):
    wide = heads * HEAD
    mem_len = mem_in.shape[0]
    seq_len = x_in.shape[0]
    todo = [
        (mem_in, mem_ref), (gain_in, gain_ref), (shift_in, shift_ref), (wk_in, w_ref.at[:, wide : 2 * wide]),
        (wv_in, w_ref.at[:, 2 * wide :]), (x_in, x_ref), (wq_in, w_ref.at[:, :wide]), (bu_in, bu_ref), (bv_in, bv_ref),
        (wpos_in, wpos_ref), (sin_in, sin_ref), (cos_in, cos_ref), (table_in, kt_ref.at[:, wide:]),
        (wout_in, wout_ref), (wup_in, wup_ref), (wdown_in, wdown_ref), (g_in, g_ref), (fgain_in, fgain_ref),
        (fshift_in, fshift_ref), (upb_in, upb_ref), (downb_in, downb_ref),
    ]
    copies = [pltpu.make_async_copy(src, dst, sems.at[i]) for i, (src, dst) in enumerate(todo)]
    for copy in copies:
        copy.start()
    for copy in copies[:5]:
        copy.wait()

    def project(rows_ref, at, to):
        unit, _ = norm_parts(rows_ref[at, :].astype(FL))
        normed = (unit * gain_ref[...] + shift_ref[...]).astype(BF)
        normed_ref[to, :] = normed
        pair = mm(normed, w_ref[:, wide:]).astype(BF)
        kt_ref[to, :wide] = pair[:, :wide]
        v_ref[to, :] = pair[:, wide:]

    def some_memory(i):
        project(mem_ref, rows_of(i, block), rows_of(i, block))

    def some_rows(i):
        project(x_ref, rows_of(i, block), rows_of(i + mem_len // block, block))

    loop(mem_len // block, some_memory, UNROLL[0])
    for copy in copies[5:7]:
        copy.wait()
    loop(seq_len // block, some_rows, UNROLL[0])
    for copy in copies[7:]:
        copy.wait()
    bias_ref[0:1, :] = jnp.concatenate([bu_ref[h : h + 1, :] for h in range(heads)], axis=1)
    bias_ref[1:2, :] = jnp.concatenate([bv_ref[h : h + 1, :] for h in range(heads)], axis=1)


def attend_kernel(
    first, block, heads, mem_len,
    count_ref, normed_ref, kt_ref, v_ref, w_ref, wpos_ref, bias_ref, sin_ref, cos_ref,
    qb_ref, qv_ref, probs_ref, ctx_ref, ctx_scr,
):
    def some_queries(i):
        at = rows_of(i, block)
        spots = rows_of(i + first // block, block)
        make_queries(
            normed_ref[rows_of(i + (mem_len + first) // block, block), :], spots, at,
            (w_ref, wpos_ref, bias_ref[0:1, :], bias_ref[1:2, :], sin_ref, cos_ref, qb_ref, qv_ref), heads,
        )

    loop(qb_ref.shape[1] // block, some_queries, UNROLL[1])
    attend(first, block, mem_len, heads, count_ref[0], qb_ref, kt_ref, v_ref, probs_ref, ctx_ref, ctx_scr)


def relay_kernel(ctx_ref, w_ref, out_ref):
    size, wide = ctx_ref.shape
    out_ref[:size, :] = ctx_ref[...]
    for k in range(w_ref.shape[1] // wide):
        at = size + k * w_ref.shape[0]
        out_ref[at : at + w_ref.shape[0], :] = w_ref[:, k * wide : (k + 1) * wide]


def ffn_rows_kernel(
    first, block, roles, relay,
    place_ref, x_ref, c0_ref, c1_ref, c2_ref, c3_ref, o0_ref, o1_ref, o2_ref, o3_ref, gain_ref, shift_ref, up_ref,
    upb_ref, down_ref, g_ref, *refs,
):
    if relay:
        ctx_in, *refs = refs
        *refs, ctx_out = refs
        ctx_out[...] = ctx_in[...]
    core = place_ref[0]
    wide = c0_ref.shape[1]
    size = c0_ref.shape[0]
    blocks = [o3_ref[at : at + wide, :] for at in range(o3_ref.shape[0] - size, o3_ref.shape[0], wide)]
    o3 = jnp.concatenate(blocks, axis=1)
    for role, hidden_ref, normed_ref, activ_ref, gpre_ref, vec_ref, share_ref in zip(roles, *[iter(refs)] * 6):
        half = core if role == "keep" else 1 - core
        at = rows_of(half, block)
        spots = rows_of(half + first // block, block)
        attended = mm(c0_ref[at, :], o0_ref[...]) + mm(c1_ref[at, :], o1_ref[...])
        attended = attended + (mm(c2_ref[at, :], o2_ref[...]) + mm(c3_ref[at, :], o3))
        hidden = x_ref[spots, :].astype(FL) + attended
        hidden_ref[...] = hidden
        unit, _ = norm_parts(hidden)
        normed = (unit * gain_ref[...] + shift_ref[...]).astype(BF)
        normed_ref[...] = normed
        pre = mm(normed, up_ref[...]) + upb_ref[...]
        cdf = 0.5 + 0.5 * lax.erf(pre * np.float32(0.5**0.5))
        activ_ref[...] = (pre * cdf).astype(BF)
        slope = cdf + pre * jnp.exp(-0.5 * pre * pre) * np.float32((2 * np.pi) ** -0.5)
        grad_pre = (mm_t(g_ref[spots, :], down_ref[...]) * slope).astype(BF)
        gpre_ref[...] = grad_pre
        back = mm_t(grad_pre, up_ref[...])
        share_ref[...] = back.astype(BF)
        vec_ref[0:1, :] = col_sum(back * unit)
        vec_ref[1:2, :] = col_sum(back)


def ffn_weights(first, place_ref, g_ref, down_ref, saved, shares):
    core = place_ref[0]
    block = shares[0].shape[0]
    total = None
    for role, (normed_ref, activ_ref, gpre_ref, vec_ref), share_ref in zip(("send", "keep"), saved, shares):
        half = core if role == "keep" else 1 - core
        grads = g_ref[rows_of(half + first // block, block), :]
        activ = activ_ref[...]
        share_ref[...] = mm(activ, down_ref[...]).astype(BF)
        vecs = jnp.concatenate([vec_ref[...], col_sum(grads.astype(FL))], axis=0)
        new = [t_mm(normed_ref[...], gpre_ref[...]), t_mm(activ, grads), vecs, col_sum(gpre_ref[...].astype(FL))]
        total = new if total is None else [old + part for old, part in zip(total, new)]
    return total


def ffn_late_kernel(first, place_ref, g_ref, down_ref, *refs):
    found = ffn_weights(first, place_ref, g_ref, down_ref, (refs[:4], refs[4:8]), refs[8:10])
    for ref, value in zip(refs[10:], found):
        ref[...] = value


def ffn_early_kernel(first, place_ref, g_ref, down_ref, *refs):
    found = ffn_weights(first, place_ref, g_ref, down_ref, (refs[:4], refs[4:8]), refs[12:14])
    up, down, vec, upb = (value + old[...] for value, old in zip(found, refs[8:12]))
    up_keep, up_send, down_keep, down_send, vec_ref, upb_out = refs[14:]
    halve(place_ref, 0, up.astype(BF), up_keep, up_send)
    halve(place_ref, 1, down.astype(BF), down_keep, down_send)
    vec_ref[...] = vec
    upb_out[...] = upb


def back_rows(
    first, block, heads, mem_len, place_ref, hid_s, hid_k, mine_ref, other_ref, g_ref, fgain_ref, wout_ref, ctx_ref,
    probs_ref, qb_ref, qv_ref, kt_ref, v_ref, wpos_ref, sin_ref, cos_ref,
    gh_ref, dk_ref, dv_ref, dpos_ref, dout_ref, dq_ref, bias_ref, grad_u, grad_v,
):
    core = place_ref[0]
    wide = heads * HEAD
    half = sin_ref.shape[1]
    scale = HEAD ** (-0.5)
    for part in range(2):
        at = slice(part * block, (part + 1) * block)
        spots = slice(first + part * block, first + (part + 1) * block)
        seen = mem_len + first + (part + 1) * block
        unit, inv = norm_parts(jnp.where(core == part, hid_k[...], hid_s[...]))
        summed = jnp.where(core == part, mine_ref[...].astype(FL), other_ref[...].astype(FL))
        grad_hidden = g_ref[spots, :].astype(FL) + norm_back(summed * fgain_ref[...], unit, inv)
        gh_ref[at, :] = grad_hidden
        gh = grad_hidden.astype(BF)
        context = ctx_ref[at, :]
        grad_context = mm_t(gh, wout_ref[...]).astype(BF).astype(FL)
        dout_ref[...] += t_mm(context, gh)
        along_context = grad_context * context.astype(FL)

        def one_head(h):
            lanes = head_lanes(wide, h)
            delta = jnp.sum(jnp.where(lanes, along_context, 0.0), axis=-1, keepdims=True)
            own = jnp.where(lanes, grad_context, 0.0).astype(BF)
            probs = probs_ref[h, at, :seen]
            grad_score = (probs.astype(FL) * (mm_t(own, v_ref[:seen, :]) - delta)).astype(BF)
            dv_ref[:, :seen] += t_mm(own, probs)
            dk_ref[:, :seen] += t_mm(qb_ref[h, at, :wide], grad_score)
            spread = mm(grad_score, kt_ref[:seen, :])
            grad_u[...] = jnp.where(lanes, spread[:, :wide], grad_u[...])
            sin = sin_ref[spots, :]
            cos = cos_ref[spots, :]
            on_cos, on_sin = spread[:, wide : wide + half], spread[:, wide + half :]
            turned = jnp.concatenate(
                [(on_cos * sin - on_sin * cos).astype(BF), (on_cos * cos + on_sin * sin).astype(BF)], axis=1
            )
            grad_v[...] = jnp.where(lanes, mm(turned, wpos_ref[...]), grad_v[...])
            query_v = jnp.where(lanes, qv_ref[at, :].astype(FL), 0.0).astype(BF)
            dpos_ref[...] += t_mm(query_v, turned)

        loop(heads, one_head, 2)
        bias_ref[0:1, :] += col_sum(grad_u[...]) * scale
        bias_ref[1:2, :] += col_sum(grad_v[...]) * scale
        dq_ref[at, :] = ((grad_u[...] + grad_v[...]) * scale).astype(BF)


def back_share(cols, dq_rows, dk_ref, dv_ref, weights):
    pair = [dk_ref[:, cols].T.astype(BF), dv_ref[:, cols].T.astype(BF)]
    return mm_t(jnp.concatenate([dq_rows, *pair], axis=1), weights).astype(BF)


def back_late_kernel(
    first, block, heads, mem_len,
    place_ref, hid_s, hid_k, mine_ref, other_ref, g_ref, fgain_ref, wout_ref, ctx_ref, probs_ref, qb_ref, qv_ref, kt_ref,
    v_ref, wpos_ref, sin_ref, cos_ref, w_ref,
    gh_ref, dk_ref, dv_ref, dpos_ref, dout_ref, dq_ref, bias_ref, share_ref, grad_u, grad_v,
):
    for ref in (dk_ref, dv_ref, dpos_ref, dout_ref, bias_ref):
        ref[...] = jnp.zeros(ref.shape, FL)
    back_rows(
        first, block, heads, mem_len, place_ref, hid_s, hid_k, mine_ref, other_ref, g_ref, fgain_ref, wout_ref, ctx_ref,
        probs_ref, qb_ref, qv_ref, kt_ref, v_ref, wpos_ref, sin_ref, cos_ref,
        gh_ref, dk_ref, dv_ref, dpos_ref, dout_ref, dq_ref, bias_ref, grad_u, grad_v,
    )
    for part in range(2):
        at = slice(part * block, (part + 1) * block)
        cols = slice(mem_len + first + part * block, mem_len + first + (part + 1) * block)
        share_ref[at, :] = back_share(cols, dq_ref[at, :], dk_ref, dv_ref, w_ref[...])


def back_early_kernel(
    first, block, heads, mem_len,
    place_ref, hid_s, hid_k, mine_ref, other_ref, g_ref, fgain_ref, wout_ref, ctx_ref, probs_ref, qb_ref, qv_ref, kt_ref,
    v_ref, wpos_ref, sin_ref, cos_ref, dk_in, dv_in, dpos_in, dout_in, bias_in,
    gh_ref, dk_ref, dv_ref, dpos_ref, dout_ref, dq_ref, bias_ref, grad_u, grad_v,
):
    for ref, old in ((dk_ref, dk_in), (dv_ref, dv_in), (dpos_ref, dpos_in), (dout_ref, dout_in), (bias_ref, bias_in)):
        ref[...] = old[...]
    back_rows(
        first, block, heads, mem_len, place_ref, hid_s, hid_k, mine_ref, other_ref, g_ref, fgain_ref, wout_ref, ctx_ref,
        probs_ref, qb_ref, qv_ref, kt_ref, v_ref, wpos_ref, sin_ref, cos_ref,
        gh_ref, dk_ref, dv_ref, dpos_ref, dout_ref, dq_ref, bias_ref, grad_u, grad_v,
    )


def back_end_kernel(
    first, block, heads, mem_len, n_tensor, size,
    place_ref, w_ref, normed_ref, shift_ref, gain_ref, dk_ref, dv_ref, dpos_ref, dout_ref, dq_ref, bias_ref, dq_in,
    late_ref, fvec_ref, upb_ref, e_send, e_keep, l_send, l_keep, up_keep, up_got, down_keep, down_got,
    keep_ref, send_ref, a_keep, a_send, f_ref,
):
    half = up_keep.shape[0]
    f_ref[:half, :] = added(up_keep[...], up_got[...])
    f_ref[half:, :] = added(down_keep[...], down_got[...])
    wide = heads * HEAD
    core = place_ref[0]
    for part in range(2):
        at = slice(part * block, (part + 1) * block)
        by_core(core, part, keep_ref, send_ref, late_ref[at, :], slice(block, 2 * block))
    keep_ref[2 * block : 3 * block, :] = e_keep[...]
    keep_ref[3 * block :, :] = l_keep[...]
    send_ref[2 * block : 3 * block, :] = e_send[...]
    send_ref[3 * block :, :] = l_send[...]
    normed = normed_ref[...]
    width = normed.shape[1]
    dq_all = jnp.concatenate([dq_ref[...], dq_in[...]], axis=0)
    dk, dv = dk_ref[...].astype(BF), dv_ref[...].astype(BF)
    grads = [t_mm(dq_all, normed[mem_len:]), mm(dk, normed), mm(dv, normed), dpos_ref[...], dout_ref[...]]
    grads = jnp.concatenate(grads, axis=0)
    turned = w_ref[...].astype(FL).T
    shift_sum = fine_mm(col_sum(dq_all.astype(FL)), turned[:wide].astype(BF), mm)
    for i, part in enumerate((dk, dv)):
        shift_sum += col_sum(turned[(i + 1) * wide : (i + 2) * wide] * jnp.sum(part.astype(FL), axis=1, keepdims=True))
    sums = norm_sums(col_sum(turned * grads[: 3 * wide]), shift_sum, gain_ref[...], shift_ref[...])
    for part in range(2):
        at = slice(part * block, (part + 1) * block)
        cols = slice(mem_len + first + part * block, mem_len + first + (part + 1) * block)
        back = back_share(cols, dq_ref[at, :], dk_ref, dv_ref, w_ref[...])
        by_core(core, part, keep_ref, send_ref, back, slice(0, block))
    wider = jnp.zeros((1, width - wide), FL)
    rows = [*sums, fvec_ref[0:2, :], fvec_ref[2:3, :] * (1.0 / n_tensor)]
    rows += [jnp.concatenate([bias_ref[i : i + 1, :], wider], axis=1) for i in range(2)]
    for i in range(upb_ref.shape[1] // width):
        rows.append(upb_ref[:, i * width : (i + 1) * width])
    rows.append(jnp.zeros((small - 7 - upb_ref.shape[1] // width, width), FL))
    rows = jnp.concatenate(rows, axis=0).astype(BF)
    step = size + small
    for d in range(2 * a_keep.shape[0] // step):
        here = max(0, min(size, 5 * wide - d * size))
        piece = [grads[d * size : d * size + here].astype(BF)] if here else []
        piece += [jnp.zeros((size - here, width), BF)] if here < size else []
        piece = jnp.concatenate([*piece, rows], axis=0)
        per_half = a_keep.shape[0] // step
        at = slice(d % per_half * step, (d % per_half + 1) * step)
        by_core(place_ref[1] & 1, d // per_half, a_keep, a_send, piece, at)


def last_kernel(
    wide, heads, n_tensor, place_ref, a_mine, a_got, down_mine, down_got, *refs
):
    totals, refs = refs[:n_tensor], refs[n_tensor:]
    down_out, outs, smalls = refs[0], refs[1:6], refs[6:14]
    down_scr, rows_scr, turned_scr, sems = refs[14:]
    copies = []

    def send(src, dst):
        copies.append(pltpu.make_async_copy(src, dst, sems.at[len(copies)]))
        copies[-1].start()

    join(place_ref, 1, down_mine, down_got, down_scr)
    send(down_scr, down_out)
    join(place_ref, 0, a_mine, a_got, rows_scr)
    send(rows_scr.at[pl.ds(4 * wide, wide), :], outs[4])
    for i in range(4):
        turned_scr[i] = rows_scr[i * wide : (i + 1) * wide, :].T
        send(turned_scr.at[i], outs[i])
    mine = totals[0]
    total = mine[...]
    for other in totals[1:]:
        total = total + other[...]
    for i in range(5):
        smalls[i][...] = total[i : i + 1, :]
    for k in range(2):
        for h in range(heads):
            smalls[5 + k][h : h + 1, :] = mine[5 + k : 6 + k, h * HEAD : (h + 1) * HEAD]
    width = mine.shape[1]
    for i in range(smalls[7].shape[1] // width):
        smalls[7][:, i * width : (i + 1) * width] = mine[7 + i : 8 + i, :]
    for copy in copies:
        copy.wait()


def finish_kernel(
    block, place_ref, x_ref, gain_ref, gh_e, gh_l, hid_es, hid_ek, hid_ls, hid_lk, mine_ref, other_ref, bias_ref, up_ref,
    out_ref, grad_ref, up_out, out_scr, grad_scr, up_scr, sems,
):
    core = place_ref[0]
    copies = []

    def send(src, dst):
        copies.append(pltpu.make_async_copy(src, dst, sems.at[len(copies)]))
        copies[-1].start()

    up_scr[...] = up_ref[...].astype(FL)
    send(up_scr, up_out)
    for first, gh_ref, hid_s, hid_k in ((0, gh_e, hid_es, hid_ek), (1, gh_l, hid_ls, hid_lk)):
        for part in range(2):
            at = slice(part * block, (part + 1) * block)
            spots = pl.ds((2 * first + part) * block, block)

            def summed(group):
                rows = slice(group * block, (group + 1) * block)
                return jnp.where(core == part, mine_ref[rows, :].astype(FL), other_ref[rows, :].astype(FL))

            hidden = jnp.where(core == part, hid_k[...], hid_s[...])
            out_scr[spots, :] = (hidden + summed(first + 2) + bias_ref[...]).astype(BF)
            send(out_scr.at[spots, :], out_ref.at[spots, :])
            unit, inv = norm_parts(x_ref[spots, :].astype(FL))
            grad_scr[spots, :] = (gh_ref[at, :] + norm_back(summed(first) * gain_ref[...], unit, inv)).astype(BF)
            send(grad_scr.at[spots, :], grad_ref.at[spots, :])
    for copy in copies:
        copy.wait()


def halve(place_ref, bit, total, keep_ref, send_ref):
    size = total.shape[0] // 2
    high = (place_ref[1] >> bit) & 1
    by_core(high, 0, keep_ref, send_ref, total[:size], slice(None))
    by_core(high, 1, keep_ref, send_ref, total[size:], slice(None))


def join(place_ref, bit, mine_ref, got_ref, out_ref):
    size = mine_ref.shape[0]
    high = ((place_ref[1] >> bit) & 1) == 1
    mine, got = mine_ref[...].astype(FL), got_ref[...].astype(FL)
    out_ref[:size, :] = jnp.where(high, got, mine).astype(out_ref.dtype)
    out_ref[size:, :] = jnp.where(high, mine, got).astype(out_ref.dtype)


SMEM = pl.BlockSpec(memory_space=pltpu.SMEM)
SPECS = {s: pl.BlockSpec(memory_space=s) for s in (pltpu.VMEM, pltpu.HBM)}


def call(kernel, outs, args, name, flops, scratch=(), space=pltpu.VMEM, after=(), far=0):
    count, extra = len(args), len(after)

    def body(*refs):
        kernel(*refs[:count], *refs[count + extra :])

    specs = [SMEM if a.dtype == jnp.int32 else SPECS[space] for a in args]
    specs += [pl.BlockSpec(memory_space=pl.ANY)] * extra
    if space is pltpu.HBM:
        args = [a if a.dtype == jnp.int32 else pltpu.with_memory_space_constraint(a, space) for a in args]
    return pl.pallas_call(
        body,
        out_shape=[pltpu.HBM(s, d) if i < far else jax.ShapeDtypeStruct(s, d) for i, (s, d) in enumerate(outs)],
        in_specs=specs,
        out_specs=[SPECS[pltpu.HBM]] * far + [SPECS[pltpu.VMEM]] * (len(outs) - far),
        scratch_shapes=scratch,
        compiler_params=pltpu.CompilerParams(vmem_limit_bytes=VMEM_LIMIT),
        cost_estimate=pl.CostEstimate(flops=int(flops), bytes_accessed=1, transcendentals=0),
        name=name,
    )(*args, *after)


def swap(rows, axis, size, bit):
    return lax.ppermute(rows, axis, [(i, i ^ bit) for i in range(size)])


def work_kernel(jobs, place_ref, *refs):
    ins, outs = refs[: 2 * len(jobs)], list(refs[2 * len(jobs) :])
    for i, (kind, bit) in enumerate(jobs):
        mine, got = ins[2 * i : 2 * i + 2]
        if kind == "halve":
            halve(place_ref, bit, added(mine[...], got[...]), outs.pop(0), outs.pop(0))
        elif kind == "join":
            join(place_ref, bit, mine, got, outs.pop(0))
        elif kind == "sum":
            outs.pop(0)[...] = added(mine[...], got[...])
        elif kind == "copy":
            outs.pop(0)[...] = mine[...]
        else:
            total = mine[...].astype(FL) + got[...].astype(FL)
            size = outs[0].shape[0]
            for part in (total[:size], total[size:]):
                out = outs.pop(0)
                out[...] = part.astype(out.dtype)


def work(place, jobs, name, after=(), cost=1):
    outs = []
    for kind, _, mine, _ in jobs:
        size, width = mine.shape
        outs += {
            "halve": [((size // 2, width), BF)] * 2,
            "two": [((size // 2, width), BF)] * 2,
            "join": [((2 * size, width), BF)],
            "sum": [((size, width), BF)],
            "copy": [((size, width), mine.dtype)],
            "split": [((size - small, width), BF), ((small, width), FL)],
        }[kind]
    args = [a for job in jobs for a in job[2:]]
    return list(
        call(functools.partial(work_kernel, [job[:2] for job in jobs]), outs, (place, *args), name, cost, after=after)
    )


class Chain:
    def __init__(self, rows, send, bits, n_dp, end="sum"):
        self.rows, self.send, self.bits, self.n_dp, self.end, self.done = rows, send, bits, n_dp, end, 0
        self.start()

    def bit(self):
        return self.bits[min(self.done, 2 * len(self.bits) - 2 - self.done)]

    def start(self):
        self.got = swap(self.send, "dp", self.n_dp, 1 << self.bit())

    def left(self):
        return 2 * len(self.bits) - 2 - self.done

    def job(self):
        last = len(self.bits) - 1
        if self.done < last - 1:
            kind, bit = "halve", self.bits[self.done + 1]
        elif self.done <= last:
            kind, bit = (self.end if self.done == last else "sum"), 0
        else:
            kind, bit = "join", self.bit()
        return kind, bit, self.rows, self.got

    def take(self, results):
        kind = self.job()[0]
        self.rows = self.send = results.pop(0)
        if kind == "halve":
            self.send = results.pop(0)
        self.done += 1
        if self.left() >= 0:
            self.start()


def cores(rows, n_tensor):
    return swap(rows, "tensor", n_tensor, 1)


def other_chips(rows, n_tensor):
    return swap(rows, "tensor", n_tensor, 2)


def chips(rows, n_tensor):
    return rows, other_chips(rows, n_tensor)


def split_at(*parts):
    (items,) = (p for p in parts if not isinstance(p, int))
    places = [0, *(p for p in parts if isinstance(p, int)), len(items)]
    return [items[start:end] for start, end in zip(places, places[1:])]


def per_device(n_dp, n_tensor, *args):
    (inputs, memory, counts, attn_gain, attn_shift, w_query, w_key, w_value, w_pos, bias_u, bias_v, w_out,
     ffn_gain, ffn_shift, w_up, up_bias, w_down, down_bias, out_grad) = args
    _, seq_len, width = inputs.shape
    mem_len = memory.shape[1]
    total = mem_len + seq_len
    wide = w_query.shape[1]
    heads = wide // HEAD
    ff = w_up.shape[1]
    chunk = seq_len // 2
    block = chunk // 2
    late = chunk
    place = jnp.stack([lax.axis_index("tensor") & 1, lax.axis_index("dp")]).astype(jnp.int32)
    x, mem, g = inputs[0], memory[0], out_grad[0]
    row = lambda v: v.reshape(1, -1)

    freq = 1.0 / 10000.0 ** (np.arange(0, width, 2, dtype=np.float64) / width)
    key_phase = np.arange(total)[:, None] * freq[None, :]
    table = jnp.asarray(np.concatenate([np.cos(key_phase), np.sin(key_phase)], axis=1).astype(BF))
    row_phase = (np.arange(seq_len) + mem_len)[:, None] * freq[None, :]
    sin = jnp.asarray(np.sin(row_phase).astype(np.float32))
    cos = jnp.asarray(np.cos(row_phase).astype(np.float32))

    outs_of = [w_out, cores(w_out, n_tensor), swap(w_out, "tensor", n_tensor, 2)]

    def attend_outs(seen):
        return [((heads, chunk, wide + width), BF), ((chunk, wide), BF), ((heads, chunk, seen), BF), ((chunk, wide), BF)]

    ctx_scr = pltpu.VMEM((block, wide), FL)
    vectors = [row(v) for v in (attn_shift, attn_gain, ffn_gain, ffn_shift, up_bias, down_bias)]
    copied = [
        *[(a.shape, BF) for a in (x, g)], ((width, 3 * wide), BF), *[(a.shape, BF) for a in (w_pos, w_up, w_down, w_out)],
        *[(a.shape, FL) for a in (*vectors, sin, cos)], ((2, wide), FL),
    ]
    found = call(
        functools.partial(front_kernel, block, heads),
        [*copied, ((total, width), BF), ((total, wide + width), BF), ((total, wide), BF)],
        (place, x, mem, g, w_query, w_key, w_value, w_pos, w_up, w_down, w_out, *vectors, bias_u, bias_v, table, sin,
         cos), "front", 1,
        [pltpu.VMEM(mem.shape, BF)] + [pltpu.VMEM(bias_u.shape, FL)] * 2 + [pltpu.SemaphoreType.DMA((21,))], pltpu.HBM,
    )
    x, g, weights, w_pos, w_up, w_down, w_out = found[:7]
    attn_shift, attn_gain, ffn_gain, ffn_shift, up_bias, down_bias, sin, cos, biases, normed, keys, values = found[7:]

    def attend_chunk(first, name, cost, after):
        return call(
            functools.partial(attend_kernel, first, block, heads, mem_len),
            attend_outs(mem_len + first + chunk),
            (counts, normed, keys, values, weights, w_pos, biases, sin, cos), name, cost, [ctx_scr], after=after,
        )

    saved_l = attend_chunk(late, "attend_late", 1, ())
    ctx_l = [saved_l[-1], cores(saved_l[-1], n_tensor), swap(saved_l[-1], "tensor", n_tensor, 2)]
    saved_e = attend_chunk(0, "attend_early", 5e9, outs_of[1:])
    ctx_e = [saved_e[-1], cores(saved_e[-1], n_tensor), swap(saved_e[-1], "tensor", n_tensor, 2)]
    (relay,) = call(
        relay_kernel, [((chunk + width, wide), BF)], (ctx_l[2], outs_of[2]), "relay_late", 1, after=saved_e[-1:]
    )
    relay = cores(relay, n_tensor)
    ctx_l.append(relay)
    outs_of.append(relay)
    half_outs = [
        ((block, width), FL), ((block, width), BF), ((block, ff), BF), ((block, ff), BF), ((2, width), FL),
        ((block, width), BF),
    ]

    def ffn_rows(first, ctx, roles, name, beside=(), after=(), cost=1):
        found = call(
            functools.partial(ffn_rows_kernel, first, block, roles, len(beside)),
            half_outs * len(roles) + [(r.shape, BF) for r in beside],
            (place, x, *ctx, *outs_of, ffn_gain, ffn_shift, w_up, up_bias, w_down, g, *beside), name, cost, after=after,
        )
        return *(found[i : i + 6] for i in range(0, 6 * len(roles), 6)), *found[6 * len(roles) :]

    sum_outs = [((width, ff), FL), ((ff, width), FL), ((3, width), FL), ((1, ff), FL)]
    (send_l,) = ffn_rows(late, ctx_l, ("send",), "ffn_send_late")
    gnt_l = cores(send_l[-1], n_tensor)
    keep_l, relay = ffn_rows(late, ctx_l, ("keep",), "ffn_keep_late", ctx_e[2:3], send_l[-1:], 5e9)
    ctx_e.append(cores(relay, n_tensor))
    (gnt_l,) = work(place, [("sum", 0, keep_l[-1], gnt_l)], "add_late")
    gnt_l = chips(gnt_l, n_tensor)
    shares_l, sums_l = split_at(2, call(
        functools.partial(ffn_late_kernel, late),
        [((block, width), BF)] * 2 + sum_outs, (place, g, w_down, *send_l[1:5], *keep_l[1:5]), "ffn_late", 1,
        after=gnt_l[:1],
    ))
    send_e, keep_e = ffn_rows(0, ctx_e, ("send", "keep"), "ffn_rows_early", after=sums_l[3:4])
    gnt_e = cores(send_e[-1], n_tensor)
    shares_e, halves, vecs = split_at(2, call(
        functools.partial(ffn_early_kernel, 0),
        [((block, width), BF)] * 2 + [((width // 2, ff), BF)] * 2 + [((ff // 2, width), BF)] * 2
        + [((3, width), FL), ((1, ff), FL)],
        (place, g, w_down, *send_e[1:5], *keep_e[1:5], *sums_l), "ffn_early", 1,
    ), 6)
    up_keep, up_send, down_keep, down_send = halves
    up_got = swap(up_send, "dp", n_dp, 1)
    down_got = swap(down_send, "dp", n_dp, 2)
    (gnt_l,) = work(place, [("sum", 0, *gnt_l)], "add_late_chips", (up_keep,), 5e9)
    gnt_l = (gnt_l, cores(gnt_l, n_tensor))
    (gnt_e,) = work(place, [("sum", 0, keep_e[-1], gnt_e)], "add_early", gnt_l[:1])
    gnt_e = chips(gnt_e, n_tensor)
    hidden_l, hidden_e = (send_l[0], keep_l[0]), (send_e[0], keep_e[0])

    sums = [((wide, total), FL), ((wide, total), FL), ((wide, width), FL), ((wide, width), FL), ((chunk, wide), BF)]
    turn_scr = [ctx_scr, ctx_scr]

    def back_args(hidden, gnt, saved):
        qb, qv, probs, ctx = saved
        return (place, *hidden, *gnt, g, ffn_gain, w_out, ctx, probs, qb, qv, keys, values, w_pos, sin, cos, weights)

    gh_l, dk, dv, dpos, dout, dq, bias, part = call(
        functools.partial(back_late_kernel, late, block, heads, mem_len),
        [((chunk, width), FL), *sums, ((2, wide), FL), ((chunk, width), BF)],
        back_args(hidden_l, gnt_l, saved_l), "back_late", 1, turn_scr,
    )
    gnt_e, up_keep, up_send, down_keep, down_send = work(
        place, [("sum", 0, *gnt_e), ("halve", 1, up_keep, up_got), ("halve", 0, down_keep, down_got)], "add_middle", (bias,)
    )
    up_got = swap(up_send, "dp", n_dp, 2)
    down_got = swap(down_send, "dp", n_dp, 1)
    gnt_e = (gnt_e, cores(gnt_e, n_tensor))
    groups = n_dp // 2
    size = max(16, -(-5 * wide // groups // 16) * 16)
    gh_e, dk, dv, dpos, dout, dq_e, bias = call(
        functools.partial(back_early_kernel, 0, block, heads, mem_len),
        [((chunk, width), FL), *sums, ((2, wide), FL)],
        (*back_args(hidden_e, gnt_e, saved_e)[:-1], dk, dv, dpos, dout, bias), "back_early", 1, turn_scr,
    )
    keep, send, a_keep, a_send, f_rows = call(
        functools.partial(back_end_kernel, 0, block, heads, mem_len, n_tensor, size),
        [*[((seq_len, width), BF)] * 2, *[((groups // 2 * (size + small), width), BF)] * 2, ((chunk // 2, width), BF)],
        (place, weights, normed, attn_shift, attn_gain, dk, dv, dpos, dout, dq_e, bias, dq, part, *vecs, *shares_e,
         *shares_l, up_keep, up_got, down_keep, down_got), "back_end", 1,
    )
    bits = list(range((n_dp - 1).bit_length()))
    attn = Chain(a_keep, a_send, bits, n_dp, "split")
    if len(bits) > 3:
        f_rows, f_send = work(place, [("halve", 2, f_rows, jnp.zeros_like(f_rows))], "halve_ffn")
    else:
        f_send = f_rows
    ffn = Chain(f_rows, f_send, bits[2:], n_dp, "two" if len(bits) == 3 else "sum")
    rows = (keep, cores(send, n_tensor))
    count, stage = 0, 0
    while attn.left() > 0:
        jobs = [attn.job()]
        if count == 0:
            pass
        elif stage == 0:
            jobs.append(ffn.job())
        elif stage == 1:
            jobs += [("join", 1, up, up_got), ("join", 0, down, down_got)]
        elif stage == 2:
            jobs += [("join", 0, up, up_got), ("copy", 0, down, down)]
        if attn.left() == 1:
            jobs.append(("copy", 0, totals, totals))
        if count == 0 or attn.left() == 1:
            jobs.append(("sum", 0, *rows))
        results = work(place, jobs, f"step_{count}", cost=STEP_COST if count == 2 else 1)
        if attn.job()[0] == "split":
            totals = results.pop(1)
        if count == 0 or attn.left() == 1:
            rows = results.pop()
            rows = (rows, (other_chips if count == 0 else cores)(rows, n_tensor))
        if attn.left() == 1:
            totals = results.pop()
            totals = [totals] + [swap(totals, "tensor", n_tensor, k) for k in range(1, n_tensor)]
        attn.take(results)
        if count == 0:
            pass
        elif stage == 0 and ffn.left() > 0:
            ffn.take(results)
        elif stage == 0:
            up, down = results if len(results) == 2 else (results[0][: chunk // 4], results[0][chunk // 4 :])
            up_got, down_got = swap(up, "dp", n_dp, 2), swap(down, "dp", n_dp, 1)
            stage = 1
        elif stage == 1:
            up, down = results
            up_got = swap(up, "dp", n_dp, 1)
            stage = 2
        elif stage == 2:
            up, down = results
            down_got = swap(down, "dp", n_dp, 2)
            stage = 3
        count += 1
    output, input_grad, g_up = call(
        functools.partial(finish_kernel, block), [(x.shape, BF)] * 2 + [((width, ff), FL)],
        (place, x, attn_gain, gh_e, gh_l, *hidden_e, *hidden_l, *rows, down_bias, up), "finish", 1,
        [pltpu.VMEM(x.shape, BF)] * 2 + [pltpu.VMEM((width, ff), FL), pltpu.SemaphoreType.DMA((9,))],
        after=(attn.rows,), far=3,
    )
    output_there = pltpu.with_memory_space_constraint(output, pltpu.HBM)
    g_down, g_query, g_key, g_value, g_pos, g_out, *vecs = call(
        functools.partial(last_kernel, wide, heads, n_tensor),
        [((ff, width), FL)] + [((width, wide), FL)] * 4 + [((wide, width), FL)]
        + [((1, width), FL)] * 5 + [((heads, HEAD), FL)] * 2 + [((1, ff), FL)],
        (place, attn.rows, attn.got, down, down_got, *totals), "last", 1,
        [pltpu.VMEM((ff, width), FL), pltpu.VMEM((groups * size, width), FL), pltpu.VMEM((4, width, wide), FL),
         pltpu.SemaphoreType.DMA((6,))],
        after=(output_there,), far=6,
    )
    return (
        output[None],
        input_grad[None],
        vecs[0].reshape(-1),
        vecs[1].reshape(-1),
        g_query,
        g_key,
        g_value,
        g_pos,
        vecs[5],
        vecs[6],
        g_out,
        vecs[2].reshape(-1),
        vecs[3].reshape(-1),
        g_up,
        vecs[7].reshape(-1),
        g_down,
        vecs[4].reshape(-1),
    )


def solution(mesh):
    split, whole = P(None, "tensor"), P()
    return jax.shard_map(
        functools.partial(per_device, mesh.shape["dp"], mesh.shape["tensor"]),
        mesh=mesh,
        in_specs=(
            P("dp", None, None), P("dp", None, None), P("dp"), whole, whole, split, split, split, split,
            P("tensor", None), P("tensor", None), P("tensor", None), whole, whole, split, P("tensor"),
            P("tensor", None), whole, P("dp", None, None),
        ),
        out_specs=(
            P("dp", None, None), P("dp", None, None), whole, whole, split, split, split, split,
            P("tensor", None), P("tensor", None), P("tensor", None), whole, whole, split, P("tensor"),
            P("tensor", None), whole,
        ),
        check_vma=False,
    )
```

```python
import functools

import jax
import jax.numpy as jnp
import numpy as np
from jax import lax
from jax.experimental import pallas as pl
from jax.experimental.pallas import tpu as pltpu
from jax.sharding import PartitionSpec as P

HEAD = 64
BF = jnp.bfloat16
FL = jnp.float32
eps_norm = 1e-05
neg_fill = -1e30
VMEM_LIMIT = 24 * 1024 * 1024
small = 16
UNROLL = [2, 2, 2]
STEP_COST = 5e9


def mm(left, right):
    return lax.dot_general(left, right, (((1,), (0,)), ((), ())), preferred_element_type=FL)


def mm_t(left, right):
    return lax.dot_general(left, right, (((1,), (1,)), ((), ())), preferred_element_type=FL)


def t_mm(left, right):
    return lax.dot_general(left, right, (((0,), (0,)), ((), ())), preferred_element_type=FL)


def norm_parts(rows):
    center = rows - jnp.mean(rows, axis=-1, keepdims=True)
    spread = jnp.mean(center * center, axis=-1, keepdims=True)
    inv = lax.rsqrt(spread + eps_norm)
    return center * inv, inv


def norm_back(scaled, unit, inv):
    flat = jnp.mean(scaled, axis=-1, keepdims=True)
    along = jnp.mean(scaled * unit, axis=-1, keepdims=True)
    return inv * (scaled - flat - unit * along)


def head_lanes(wide, h):
    lane = lax.broadcasted_iota(jnp.int32, (1, wide), 1)
    return (lane >= h * HEAD) & (lane < (h + 1) * HEAD)


def col_sum(rows):
    return jnp.sum(rows, axis=0, keepdims=True)


def fine_mm(left, right, product):
    high = left.astype(BF)
    low = (left - high.astype(FL)).astype(BF)
    return product(high, right) + product(low, right)


def norm_sums(weighted, shift_sum, gain, shift):
    return (weighted - shift * shift_sum) / gain, shift_sum


def loop(count, body, unroll=1):
    def step(i, carry):
        body(i)
        return carry

    lax.fori_loop(0, count, step, 0, unroll=unroll)


def rows_of(i, size):
    return pl.ds(pl.multiple_of(i * size, size), size)


def by_core(core, part, keep_ref, send_ref, rows, at):
    @pl.when(core == part)
    def _():
        keep_ref[at, :] = rows

    @pl.when(core != part)
    def _():
        send_ref[at, :] = rows


def added(left, right):
    return (left.astype(FL) + right.astype(FL)).astype(BF)


def make_queries(normed, spots, at, refs, heads):
    w_ref, wpos_ref, bu, bv, sin_ref, cos_ref, qb_ref, qv_ref = refs
    wide = heads * HEAD
    scale = HEAD ** (-0.5)
    query = mm(normed, w_ref[:, :wide]).astype(BF).astype(FL)
    query_u = (query + bu).astype(BF).astype(FL) * scale
    query_v = (query + bv).astype(BF).astype(FL) * scale
    qv_ref[at, :] = query_v.astype(BF)
    sin = sin_ref[spots, :]
    cos = cos_ref[spots, :]
    half = sin.shape[1]
    for h in range(heads):
        lanes = head_lanes(wide, h)
        qb_ref[h, at, :wide] = jnp.where(lanes, query_u, 0.0).astype(BF)
        coef = mm_t(jnp.where(lanes, query_v, 0.0).astype(BF), wpos_ref[...])
        on_sin, on_cos = coef[:, :half], coef[:, half:]
        qb_ref[h, at, wide : wide + half] = (on_sin * sin + on_cos * cos).astype(BF)
        qb_ref[h, at, wide + half :] = (on_cos * sin - on_sin * cos).astype(BF)


def attend(first, block, mem_len, heads, count, qb_ref, kt_ref, v_ref, probs_ref, ctx_ref, ctx_scr):
    wide = heads * HEAD
    rows = qb_ref.shape[1]
    for part in range(rows // block):
        at = slice(part * block, (part + 1) * block)
        start = first + part * block
        seen = mem_len + start + block

        def one_head(h):
            scores = mm_t(qb_ref[h, at, :], kt_ref[:seen, :])
            query_pos = start + lax.broadcasted_iota(jnp.int32, (block, 1), 0)
            limit = jnp.minimum(query_pos, count - 1)
            key_pos = lax.broadcasted_iota(jnp.int32, (block, seen - mem_len), 1)
            scores = jnp.concatenate(
                [scores[:, :mem_len], jnp.where(key_pos <= limit, scores[:, mem_len:], neg_fill)], axis=1
            )
            expo = jnp.exp(scores - jnp.max(scores, axis=-1, keepdims=True))
            probs = (expo * (1.0 / jnp.sum(expo, axis=-1, keepdims=True))).astype(BF)
            probs_ref[h, at, :seen] = probs
            found = mm(probs, v_ref[:seen, :])
            ctx_scr[...] = jnp.where(head_lanes(wide, h), found, ctx_scr[...])

        loop(heads, one_head, UNROLL[2])
        ctx_ref[at, :] = ctx_scr[...].astype(BF)


def front_kernel(
    block, heads,
    place_ref, x_in, mem_in, g_in, wq_in, wk_in, wv_in, wpos_in, wup_in, wdown_in, wout_in,
    shift_in, gain_in, fgain_in, fshift_in, upb_in, downb_in, bu_in, bv_in, table_in, sin_in, cos_in,
    x_ref, g_ref, w_ref, wpos_ref, wup_ref, wdown_ref, wout_ref, shift_ref, gain_ref, fgain_ref, fshift_ref, upb_ref,
    downb_ref, sin_ref, cos_ref, bias_ref, normed_ref, kt_ref, v_ref,
    mem_ref, bu_ref, bv_ref, sems,
):
    wide = heads * HEAD
    mem_len = mem_in.shape[0]
    seq_len = x_in.shape[0]
    todo = [
        (mem_in, mem_ref), (gain_in, gain_ref), (shift_in, shift_ref), (wk_in, w_ref.at[:, wide : 2 * wide]),
        (wv_in, w_ref.at[:, 2 * wide :]), (x_in, x_ref), (wq_in, w_ref.at[:, :wide]), (bu_in, bu_ref), (bv_in, bv_ref),
        (wpos_in, wpos_ref), (sin_in, sin_ref), (cos_in, cos_ref), (table_in, kt_ref.at[:, wide:]),
        (wout_in, wout_ref), (wup_in, wup_ref), (wdown_in, wdown_ref), (g_in, g_ref), (fgain_in, fgain_ref),
        (fshift_in, fshift_ref), (upb_in, upb_ref), (downb_in, downb_ref),
    ]
    copies = [pltpu.make_async_copy(src, dst, sems.at[i]) for i, (src, dst) in enumerate(todo)]
    for copy in copies:
        copy.start()
    for copy in copies[:5]:
        copy.wait()

    def project(rows_ref, at, to):
        unit, _ = norm_parts(rows_ref[at, :].astype(FL))
        normed = (unit * gain_ref[...] + shift_ref[...]).astype(BF)
        normed_ref[to, :] = normed
        pair = mm(normed, w_ref[:, wide:]).astype(BF)
        kt_ref[to, :wide] = pair[:, :wide]
        v_ref[to, :] = pair[:, wide:]

    def some_memory(i):
        project(mem_ref, rows_of(i, block), rows_of(i, block))

    def some_rows(i):
        project(x_ref, rows_of(i, block), rows_of(i + mem_len // block, block))

    loop(mem_len // block, some_memory, UNROLL[0])
    for copy in copies[5:7]:
        copy.wait()
    loop(seq_len // block, some_rows, UNROLL[0])
    for copy in copies[7:]:
        copy.wait()
    bias_ref[0:1, :] = jnp.concatenate([bu_ref[h : h + 1, :] for h in range(heads)], axis=1)
    bias_ref[1:2, :] = jnp.concatenate([bv_ref[h : h + 1, :] for h in range(heads)], axis=1)


def attend_kernel(
    first, block, heads, mem_len,
    count_ref, normed_ref, kt_ref, v_ref, w_ref, wpos_ref, bias_ref, sin_ref, cos_ref,
    qb_ref, qv_ref, probs_ref, ctx_ref, ctx_scr,
):
    def some_queries(i):
        at = rows_of(i, block)
        spots = rows_of(i + first // block, block)
        make_queries(
            normed_ref[rows_of(i + (mem_len + first) // block, block), :], spots, at,
            (w_ref, wpos_ref, bias_ref[0:1, :], bias_ref[1:2, :], sin_ref, cos_ref, qb_ref, qv_ref), heads,
        )

    loop(qb_ref.shape[1] // block, some_queries, UNROLL[1])
    attend(first, block, mem_len, heads, count_ref[0], qb_ref, kt_ref, v_ref, probs_ref, ctx_ref, ctx_scr)


def relay_kernel(ctx_ref, w_ref, out_ref):
    size, wide = ctx_ref.shape
    out_ref[:size, :] = ctx_ref[...]
    for k in range(w_ref.shape[1] // wide):
        at = size + k * w_ref.shape[0]
        out_ref[at : at + w_ref.shape[0], :] = w_ref[:, k * wide : (k + 1) * wide]


def ffn_rows_kernel(
    first, block, roles, relay,
    place_ref, x_ref, c0_ref, c1_ref, c2_ref, c3_ref, o0_ref, o1_ref, o2_ref, o3_ref, gain_ref, shift_ref, up_ref,
    upb_ref, down_ref, g_ref, *refs,
):
    if relay:
        ctx_in, *refs = refs
        *refs, ctx_out = refs
        ctx_out[...] = ctx_in[...]
    core = place_ref[0]
    wide = c0_ref.shape[1]
    size = c0_ref.shape[0]
    blocks = [o3_ref[at : at + wide, :] for at in range(o3_ref.shape[0] - size, o3_ref.shape[0], wide)]
    o3 = jnp.concatenate(blocks, axis=1)
    for role, hidden_ref, normed_ref, activ_ref, gpre_ref, vec_ref, share_ref in zip(roles, *[iter(refs)] * 6):
        half = core if role == "keep" else 1 - core
        at = rows_of(half, block)
        spots = rows_of(half + first // block, block)
        attended = mm(c0_ref[at, :], o0_ref[...]) + mm(c1_ref[at, :], o1_ref[...])
        attended = attended + (mm(c2_ref[at, :], o2_ref[...]) + mm(c3_ref[at, :], o3))
        hidden = x_ref[spots, :].astype(FL) + attended
        hidden_ref[...] = hidden
        unit, _ = norm_parts(hidden)
        normed = (unit * gain_ref[...] + shift_ref[...]).astype(BF)
        normed_ref[...] = normed
        pre = mm(normed, up_ref[...]) + upb_ref[...]
        cdf = 0.5 + 0.5 * lax.erf(pre * np.float32(0.5**0.5))
        activ_ref[...] = (pre * cdf).astype(BF)
        slope = cdf + pre * jnp.exp(-0.5 * pre * pre) * np.float32((2 * np.pi) ** -0.5)
        grad_pre = (mm_t(g_ref[spots, :], down_ref[...]) * slope).astype(BF)
        gpre_ref[...] = grad_pre
        back = mm_t(grad_pre, up_ref[...])
        share_ref[...] = back.astype(BF)
        vec_ref[0:1, :] = col_sum(back * unit)
        vec_ref[1:2, :] = col_sum(back)


def ffn_weights(first, place_ref, g_ref, down_ref, saved, shares):
    core = place_ref[0]
    block = shares[0].shape[0]
    total = None
    for role, (normed_ref, activ_ref, gpre_ref, vec_ref), share_ref in zip(("send", "keep"), saved, shares):
        half = core if role == "keep" else 1 - core
        grads = g_ref[rows_of(half + first // block, block), :]
        activ = activ_ref[...]
        share_ref[...] = mm(activ, down_ref[...]).astype(BF)
        vecs = jnp.concatenate([vec_ref[...], col_sum(grads.astype(FL))], axis=0)
        new = [t_mm(normed_ref[...], gpre_ref[...]), t_mm(activ, grads), vecs, col_sum(gpre_ref[...].astype(FL))]
        total = new if total is None else [old + part for old, part in zip(total, new)]
    return total


def ffn_late_kernel(first, place_ref, g_ref, down_ref, *refs):
    found = ffn_weights(first, place_ref, g_ref, down_ref, (refs[:4], refs[4:8]), refs[8:10])
    for ref, value in zip(refs[10:], found):
        ref[...] = value


def ffn_early_kernel(first, place_ref, g_ref, down_ref, *refs):
    found = ffn_weights(first, place_ref, g_ref, down_ref, (refs[:4], refs[4:8]), refs[12:14])
    up, down, vec, upb = (value + old[...] for value, old in zip(found, refs[8:12]))
    up_keep, up_send, down_keep, down_send, vec_ref, upb_out = refs[14:]
    halve(place_ref, 0, up.astype(BF), up_keep, up_send)
    halve(place_ref, 1, down.astype(BF), down_keep, down_send)
    vec_ref[...] = vec
    upb_out[...] = upb


def back_rows(
    first, block, heads, mem_len, place_ref, hid_s, hid_k, mine_ref, other_ref, g_ref, fgain_ref, wout_ref, ctx_ref,
    probs_ref, qb_ref, qv_ref, kt_ref, v_ref, wpos_ref, sin_ref, cos_ref,
    gh_ref, dk_ref, dv_ref, dpos_ref, dout_ref, dq_ref, bias_ref, grad_u, grad_v,
):
    core = place_ref[0]
    wide = heads * HEAD
    half = sin_ref.shape[1]
    scale = HEAD ** (-0.5)
    for part in range(2):
        at = slice(part * block, (part + 1) * block)
        spots = slice(first + part * block, first + (part + 1) * block)
        seen = mem_len + first + (part + 1) * block
        unit, inv = norm_parts(jnp.where(core == part, hid_k[...], hid_s[...]))
        summed = jnp.where(core == part, mine_ref[...].astype(FL), other_ref[...].astype(FL))
        grad_hidden = g_ref[spots, :].astype(FL) + norm_back(summed * fgain_ref[...], unit, inv)
        gh_ref[at, :] = grad_hidden
        gh = grad_hidden.astype(BF)
        context = ctx_ref[at, :]
        grad_context = mm_t(gh, wout_ref[...]).astype(BF).astype(FL)
        dout_ref[...] += t_mm(context, gh)
        along_context = grad_context * context.astype(FL)

        def one_head(h):
            lanes = head_lanes(wide, h)
            delta = jnp.sum(jnp.where(lanes, along_context, 0.0), axis=-1, keepdims=True)
            own = jnp.where(lanes, grad_context, 0.0).astype(BF)
            probs = probs_ref[h, at, :seen]
            grad_score = (probs.astype(FL) * (mm_t(own, v_ref[:seen, :]) - delta)).astype(BF)
            dv_ref[:, :seen] += t_mm(own, probs)
            dk_ref[:, :seen] += t_mm(qb_ref[h, at, :wide], grad_score)
            spread = mm(grad_score, kt_ref[:seen, :])
            grad_u[...] = jnp.where(lanes, spread[:, :wide], grad_u[...])
            sin = sin_ref[spots, :]
            cos = cos_ref[spots, :]
            on_cos, on_sin = spread[:, wide : wide + half], spread[:, wide + half :]
            turned = jnp.concatenate(
                [(on_cos * sin - on_sin * cos).astype(BF), (on_cos * cos + on_sin * sin).astype(BF)], axis=1
            )
            grad_v[...] = jnp.where(lanes, mm(turned, wpos_ref[...]), grad_v[...])
            query_v = jnp.where(lanes, qv_ref[at, :].astype(FL), 0.0).astype(BF)
            dpos_ref[...] += t_mm(query_v, turned)

        loop(heads, one_head, 2)
        bias_ref[0:1, :] += col_sum(grad_u[...]) * scale
        bias_ref[1:2, :] += col_sum(grad_v[...]) * scale
        dq_ref[at, :] = ((grad_u[...] + grad_v[...]) * scale).astype(BF)


def back_share(cols, dq_rows, dk_ref, dv_ref, weights):
    pair = [dk_ref[:, cols].T.astype(BF), dv_ref[:, cols].T.astype(BF)]
    return mm_t(jnp.concatenate([dq_rows, *pair], axis=1), weights).astype(BF)


def back_late_kernel(
    first, block, heads, mem_len,
    place_ref, hid_s, hid_k, mine_ref, other_ref, g_ref, fgain_ref, wout_ref, ctx_ref, probs_ref, qb_ref, qv_ref, kt_ref,
    v_ref, wpos_ref, sin_ref, cos_ref, w_ref,
    gh_ref, dk_ref, dv_ref, dpos_ref, dout_ref, dq_ref, bias_ref, share_ref, grad_u, grad_v,
):
    for ref in (dk_ref, dv_ref, dpos_ref, dout_ref, bias_ref):
        ref[...] = jnp.zeros(ref.shape, FL)
    back_rows(
        first, block, heads, mem_len, place_ref, hid_s, hid_k, mine_ref, other_ref, g_ref, fgain_ref, wout_ref, ctx_ref,
        probs_ref, qb_ref, qv_ref, kt_ref, v_ref, wpos_ref, sin_ref, cos_ref,
        gh_ref, dk_ref, dv_ref, dpos_ref, dout_ref, dq_ref, bias_ref, grad_u, grad_v,
    )
    for part in range(2):
        at = slice(part * block, (part + 1) * block)
        cols = slice(mem_len + first + part * block, mem_len + first + (part + 1) * block)
        share_ref[at, :] = back_share(cols, dq_ref[at, :], dk_ref, dv_ref, w_ref[...])


def back_early_kernel(
    first, block, heads, mem_len,
    place_ref, hid_s, hid_k, mine_ref, other_ref, g_ref, fgain_ref, wout_ref, ctx_ref, probs_ref, qb_ref, qv_ref, kt_ref,
    v_ref, wpos_ref, sin_ref, cos_ref, dk_in, dv_in, dpos_in, dout_in, bias_in,
    gh_ref, dk_ref, dv_ref, dpos_ref, dout_ref, dq_ref, bias_ref, grad_u, grad_v,
):
    for ref, old in ((dk_ref, dk_in), (dv_ref, dv_in), (dpos_ref, dpos_in), (dout_ref, dout_in), (bias_ref, bias_in)):
        ref[...] = old[...]
    back_rows(
        first, block, heads, mem_len, place_ref, hid_s, hid_k, mine_ref, other_ref, g_ref, fgain_ref, wout_ref, ctx_ref,
        probs_ref, qb_ref, qv_ref, kt_ref, v_ref, wpos_ref, sin_ref, cos_ref,
        gh_ref, dk_ref, dv_ref, dpos_ref, dout_ref, dq_ref, bias_ref, grad_u, grad_v,
    )


def back_end_kernel(
    first, block, heads, mem_len, n_tensor, size,
    place_ref, w_ref, normed_ref, shift_ref, gain_ref, dk_ref, dv_ref, dpos_ref, dout_ref, dq_ref, bias_ref, dq_in,
    late_ref, fvec_ref, upb_ref, e_send, e_keep, l_send, l_keep, up_keep, up_got, down_keep, down_got,
    keep_ref, send_ref, a_keep, a_send, f_ref,
):
    half = up_keep.shape[0]
    f_ref[:half, :] = added(up_keep[...], up_got[...])
    f_ref[half:, :] = added(down_keep[...], down_got[...])
    wide = heads * HEAD
    core = place_ref[0]
    for part in range(2):
        at = slice(part * block, (part + 1) * block)
        by_core(core, part, keep_ref, send_ref, late_ref[at, :], slice(block, 2 * block))
    keep_ref[2 * block : 3 * block, :] = e_keep[...]
    keep_ref[3 * block :, :] = l_keep[...]
    send_ref[2 * block : 3 * block, :] = e_send[...]
    send_ref[3 * block :, :] = l_send[...]
    normed = normed_ref[...]
    width = normed.shape[1]
    dq_all = jnp.concatenate([dq_ref[...], dq_in[...]], axis=0)
    dk, dv = dk_ref[...].astype(BF), dv_ref[...].astype(BF)
    grads = [t_mm(dq_all, normed[mem_len:]), mm(dk, normed), mm(dv, normed), dpos_ref[...], dout_ref[...]]
    grads = jnp.concatenate(grads, axis=0)
    turned = w_ref[...].astype(FL).T
    shift_sum = fine_mm(col_sum(dq_all.astype(FL)), turned[:wide].astype(BF), mm)
    for i, part in enumerate((dk, dv)):
        shift_sum += col_sum(turned[(i + 1) * wide : (i + 2) * wide] * jnp.sum(part.astype(FL), axis=1, keepdims=True))
    sums = norm_sums(col_sum(turned * grads[: 3 * wide]), shift_sum, gain_ref[...], shift_ref[...])
    for part in range(2):
        at = slice(part * block, (part + 1) * block)
        cols = slice(mem_len + first + part * block, mem_len + first + (part + 1) * block)
        back = back_share(cols, dq_ref[at, :], dk_ref, dv_ref, w_ref[...])
        by_core(core, part, keep_ref, send_ref, back, slice(0, block))
    wider = jnp.zeros((1, width - wide), FL)
    rows = [*sums, fvec_ref[0:2, :], fvec_ref[2:3, :] * (1.0 / n_tensor)]
    rows += [jnp.concatenate([bias_ref[i : i + 1, :], wider], axis=1) for i in range(2)]
    for i in range(upb_ref.shape[1] // width):
        rows.append(upb_ref[:, i * width : (i + 1) * width])
    rows.append(jnp.zeros((small - 7 - upb_ref.shape[1] // width, width), FL))
    rows = jnp.concatenate(rows, axis=0).astype(BF)
    step = size + small
    for d in range(2 * a_keep.shape[0] // step):
        here = max(0, min(size, 5 * wide - d * size))
        piece = [grads[d * size : d * size + here].astype(BF)] if here else []
        piece += [jnp.zeros((size - here, width), BF)] if here < size else []
        piece = jnp.concatenate([*piece, rows], axis=0)
        per_half = a_keep.shape[0] // step
        at = slice(d % per_half * step, (d % per_half + 1) * step)
        by_core(place_ref[1] & 1, d // per_half, a_keep, a_send, piece, at)


def last_kernel(
    wide, heads, n_tensor, place_ref, a_mine, a_got, down_mine, down_got, *refs
):
    totals, refs = refs[:n_tensor], refs[n_tensor:]
    down_out, outs, smalls = refs[0], refs[1:6], refs[6:14]
    down_scr, rows_scr, turned_scr, sems = refs[14:]
    copies = []

    def send(src, dst):
        copies.append(pltpu.make_async_copy(src, dst, sems.at[len(copies)]))
        copies[-1].start()

    join(place_ref, 1, down_mine, down_got, down_scr)
    send(down_scr, down_out)
    join(place_ref, 0, a_mine, a_got, rows_scr)
    send(rows_scr.at[pl.ds(4 * wide, wide), :], outs[4])
    for i in range(4):
        turned_scr[i] = rows_scr[i * wide : (i + 1) * wide, :].T
        send(turned_scr.at[i], outs[i])
    mine = totals[0]
    total = mine[...]
    for other in totals[1:]:
        total = total + other[...]
    for i in range(5):
        smalls[i][...] = total[i : i + 1, :]
    for k in range(2):
        for h in range(heads):
            smalls[5 + k][h : h + 1, :] = mine[5 + k : 6 + k, h * HEAD : (h + 1) * HEAD]
    width = mine.shape[1]
    for i in range(smalls[7].shape[1] // width):
        smalls[7][:, i * width : (i + 1) * width] = mine[7 + i : 8 + i, :]
    for copy in copies:
        copy.wait()


def finish_kernel(
    block, place_ref, x_ref, gain_ref, gh_e, gh_l, hid_es, hid_ek, hid_ls, hid_lk, mine_ref, other_ref, bias_ref, up_ref,
    out_ref, grad_ref, up_out, out_scr, grad_scr, up_scr, sems,
):
    core = place_ref[0]
    copies = []

    def send(src, dst):
        copies.append(pltpu.make_async_copy(src, dst, sems.at[len(copies)]))
        copies[-1].start()

    up_scr[...] = up_ref[...].astype(FL)
    send(up_scr, up_out)
    for first, gh_ref, hid_s, hid_k in ((0, gh_e, hid_es, hid_ek), (1, gh_l, hid_ls, hid_lk)):
        for part in range(2):
            at = slice(part * block, (part + 1) * block)
            spots = pl.ds((2 * first + part) * block, block)

            def summed(group):
                rows = slice(group * block, (group + 1) * block)
                return jnp.where(core == part, mine_ref[rows, :].astype(FL), other_ref[rows, :].astype(FL))

            hidden = jnp.where(core == part, hid_k[...], hid_s[...])
            out_scr[spots, :] = (hidden + summed(first + 2) + bias_ref[...]).astype(BF)
            send(out_scr.at[spots, :], out_ref.at[spots, :])
            unit, inv = norm_parts(x_ref[spots, :].astype(FL))
            grad_scr[spots, :] = (gh_ref[at, :] + norm_back(summed(first) * gain_ref[...], unit, inv)).astype(BF)
            send(grad_scr.at[spots, :], grad_ref.at[spots, :])
    for copy in copies:
        copy.wait()


def halve(place_ref, bit, total, keep_ref, send_ref):
    size = total.shape[0] // 2
    high = (place_ref[1] >> bit) & 1
    by_core(high, 0, keep_ref, send_ref, total[:size], slice(None))
    by_core(high, 1, keep_ref, send_ref, total[size:], slice(None))


def join(place_ref, bit, mine_ref, got_ref, out_ref):
    size = mine_ref.shape[0]
    high = ((place_ref[1] >> bit) & 1) == 1
    mine, got = mine_ref[...].astype(FL), got_ref[...].astype(FL)
    out_ref[:size, :] = jnp.where(high, got, mine).astype(out_ref.dtype)
    out_ref[size:, :] = jnp.where(high, mine, got).astype(out_ref.dtype)


SMEM = pl.BlockSpec(memory_space=pltpu.SMEM)
PLACE = object()
SPECS = {s: pl.BlockSpec(memory_space=s) for s in (pltpu.VMEM, pltpu.HBM)}


def call(kernel, outs, args, name, flops, scratch=(), space=pltpu.VMEM, after=(), far=0):
    placed = args[0] is PLACE
    args = args[1:] if placed else args
    count, extra = len(args), len(after)

    def body(*refs):
        place = [(lax.axis_index("tensor") & 1, lax.axis_index("dp"))] if placed else []
        kernel(*place, *refs[:count], *refs[count + extra :])

    specs = [SMEM if a.dtype == jnp.int32 else SPECS[space] for a in args]
    specs += [pl.BlockSpec(memory_space=pl.ANY)] * extra
    if space is pltpu.HBM:
        args = [a if a.dtype == jnp.int32 else pltpu.with_memory_space_constraint(a, space) for a in args]
    return pl.pallas_call(
        body,
        out_shape=[pltpu.HBM(s, d) if i < far else jax.ShapeDtypeStruct(s, d) for i, (s, d) in enumerate(outs)],
        in_specs=specs,
        out_specs=[SPECS[pltpu.HBM]] * far + [SPECS[pltpu.VMEM]] * (len(outs) - far),
        scratch_shapes=scratch,
        compiler_params=pltpu.CompilerParams(vmem_limit_bytes=VMEM_LIMIT),
        cost_estimate=pl.CostEstimate(flops=int(flops), bytes_accessed=1, transcendentals=0),
        name=name,
    )(*args, *after)


def swap(rows, axis, size, bit):
    return lax.ppermute(rows, axis, [(i, i ^ bit) for i in range(size)])


def work_kernel(jobs, place_ref, *refs):
    ins, outs = refs[: 2 * len(jobs)], list(refs[2 * len(jobs) :])
    for i, (kind, bit) in enumerate(jobs):
        mine, got = ins[2 * i : 2 * i + 2]
        if kind == "halve":
            halve(place_ref, bit, added(mine[...], got[...]), outs.pop(0), outs.pop(0))
        elif kind == "join":
            join(place_ref, bit, mine, got, outs.pop(0))
        elif kind == "sum":
            outs.pop(0)[...] = added(mine[...], got[...])
        elif kind == "copy":
            outs.pop(0)[...] = mine[...]
        else:
            total = mine[...].astype(FL) + got[...].astype(FL)
            size = outs[0].shape[0]
            for part in (total[:size], total[size:]):
                out = outs.pop(0)
                out[...] = part.astype(out.dtype)


def work(place, jobs, name, after=(), cost=1):
    outs = []
    for kind, _, mine, _ in jobs:
        size, width = mine.shape
        outs += {
            "halve": [((size // 2, width), BF)] * 2,
            "two": [((size // 2, width), BF)] * 2,
            "join": [((2 * size, width), BF)],
            "sum": [((size, width), BF)],
            "copy": [((size, width), mine.dtype)],
            "split": [((size - small, width), BF), ((small, width), FL)],
        }[kind]
    args = [a for job in jobs for a in job[2:]]
    return list(
        call(functools.partial(work_kernel, [job[:2] for job in jobs]), outs, (place, *args), name, cost, after=after)
    )


class Chain:
    def __init__(self, rows, send, bits, n_dp, end="sum"):
        self.rows, self.send, self.bits, self.n_dp, self.end, self.done = rows, send, bits, n_dp, end, 0
        self.start()

    def bit(self):
        return self.bits[min(self.done, 2 * len(self.bits) - 2 - self.done)]

    def start(self):
        self.got = swap(self.send, "dp", self.n_dp, 1 << self.bit())

    def left(self):
        return 2 * len(self.bits) - 2 - self.done

    def job(self):
        last = len(self.bits) - 1
        if self.done < last - 1:
            kind, bit = "halve", self.bits[self.done + 1]
        elif self.done <= last:
            kind, bit = (self.end if self.done == last else "sum"), 0
        else:
            kind, bit = "join", self.bit()
        return kind, bit, self.rows, self.got

    def take(self, results):
        kind = self.job()[0]
        self.rows = self.send = results.pop(0)
        if kind == "halve":
            self.send = results.pop(0)
        self.done += 1
        if self.left() >= 0:
            self.start()


def cores(rows, n_tensor):
    return swap(rows, "tensor", n_tensor, 1)


def other_chips(rows, n_tensor):
    return swap(rows, "tensor", n_tensor, 2)


def chips(rows, n_tensor):
    return rows, other_chips(rows, n_tensor)


def split_at(*parts):
    (items,) = (p for p in parts if not isinstance(p, int))
    places = [0, *(p for p in parts if isinstance(p, int)), len(items)]
    return [items[start:end] for start, end in zip(places, places[1:])]


def per_device(n_dp, n_tensor, *args):
    (inputs, memory, counts, attn_gain, attn_shift, w_query, w_key, w_value, w_pos, bias_u, bias_v, w_out,
     ffn_gain, ffn_shift, w_up, up_bias, w_down, down_bias, out_grad) = args
    _, seq_len, width = inputs.shape
    mem_len = memory.shape[1]
    total = mem_len + seq_len
    wide = w_query.shape[1]
    heads = wide // HEAD
    ff = w_up.shape[1]
    chunk = seq_len // 2
    block = chunk // 2
    late = chunk
    place = PLACE
    x, mem, g = inputs[0], memory[0], out_grad[0]
    row = lambda v: v.reshape(1, -1)

    freq = 1.0 / 10000.0 ** (np.arange(0, width, 2, dtype=np.float64) / width)
    key_phase = np.arange(total)[:, None] * freq[None, :]
    table = jnp.asarray(np.concatenate([np.cos(key_phase), np.sin(key_phase)], axis=1).astype(BF))
    row_phase = (np.arange(seq_len) + mem_len)[:, None] * freq[None, :]
    sin = jnp.asarray(np.sin(row_phase).astype(np.float32))
    cos = jnp.asarray(np.cos(row_phase).astype(np.float32))

    outs_of = [w_out, cores(w_out, n_tensor), swap(w_out, "tensor", n_tensor, 2)]

    def attend_outs(seen):
        return [((heads, chunk, wide + width), BF), ((chunk, wide), BF), ((heads, chunk, seen), BF), ((chunk, wide), BF)]

    ctx_scr = pltpu.VMEM((block, wide), FL)
    vectors = [row(v) for v in (attn_shift, attn_gain, ffn_gain, ffn_shift, up_bias, down_bias)]
    copied = [
        *[(a.shape, BF) for a in (x, g)], ((width, 3 * wide), BF), *[(a.shape, BF) for a in (w_pos, w_up, w_down, w_out)],
        *[(a.shape, FL) for a in (*vectors, sin, cos)], ((2, wide), FL),
    ]
    found = call(
        functools.partial(front_kernel, block, heads),
        [*copied, ((total, width), BF), ((total, wide + width), BF), ((total, wide), BF)],
        (place, x, mem, g, w_query, w_key, w_value, w_pos, w_up, w_down, w_out, *vectors, bias_u, bias_v, table, sin,
         cos), "front", 1,
        [pltpu.VMEM(mem.shape, BF)] + [pltpu.VMEM(bias_u.shape, FL)] * 2 + [pltpu.SemaphoreType.DMA((21,))], pltpu.HBM,
    )
    x, g, weights, w_pos, w_up, w_down, w_out = found[:7]
    attn_shift, attn_gain, ffn_gain, ffn_shift, up_bias, down_bias, sin, cos, biases, normed, keys, values = found[7:]

    def attend_chunk(first, name, cost, after):
        return call(
            functools.partial(attend_kernel, first, block, heads, mem_len),
            attend_outs(mem_len + first + chunk),
            (counts, normed, keys, values, weights, w_pos, biases, sin, cos), name, cost, [ctx_scr], after=after,
        )

    saved_l = attend_chunk(late, "attend_late", 1, ())
    ctx_l = [saved_l[-1], cores(saved_l[-1], n_tensor), swap(saved_l[-1], "tensor", n_tensor, 2)]
    saved_e = attend_chunk(0, "attend_early", 5e9, outs_of[1:])
    ctx_e = [saved_e[-1], cores(saved_e[-1], n_tensor), swap(saved_e[-1], "tensor", n_tensor, 2)]
    (relay,) = call(
        relay_kernel, [((chunk + width, wide), BF)], (ctx_l[2], outs_of[2]), "relay_late", 1, after=saved_e[-1:]
    )
    relay = cores(relay, n_tensor)
    ctx_l.append(relay)
    outs_of.append(relay)
    half_outs = [
        ((block, width), FL), ((block, width), BF), ((block, ff), BF), ((block, ff), BF), ((2, width), FL),
        ((block, width), BF),
    ]

    def ffn_rows(first, ctx, roles, name, beside=(), after=(), cost=1):
        found = call(
            functools.partial(ffn_rows_kernel, first, block, roles, len(beside)),
            half_outs * len(roles) + [(r.shape, BF) for r in beside],
            (place, x, *ctx, *outs_of, ffn_gain, ffn_shift, w_up, up_bias, w_down, g, *beside), name, cost, after=after,
        )
        return *(found[i : i + 6] for i in range(0, 6 * len(roles), 6)), *found[6 * len(roles) :]

    sum_outs = [((width, ff), FL), ((ff, width), FL), ((3, width), FL), ((1, ff), FL)]
    (send_l,) = ffn_rows(late, ctx_l, ("send",), "ffn_send_late")
    gnt_l = cores(send_l[-1], n_tensor)
    keep_l, relay = ffn_rows(late, ctx_l, ("keep",), "ffn_keep_late", ctx_e[2:3], send_l[-1:], 5e9)
    ctx_e.append(cores(relay, n_tensor))
    (gnt_l,) = work(place, [("sum", 0, keep_l[-1], gnt_l)], "add_late")
    gnt_l = chips(gnt_l, n_tensor)
    shares_l, sums_l = split_at(2, call(
        functools.partial(ffn_late_kernel, late),
        [((block, width), BF)] * 2 + sum_outs, (place, g, w_down, *send_l[1:5], *keep_l[1:5]), "ffn_late", 1,
        after=gnt_l[:1],
    ))
    send_e, keep_e = ffn_rows(0, ctx_e, ("send", "keep"), "ffn_rows_early", after=sums_l[3:4])
    gnt_e = cores(send_e[-1], n_tensor)
    shares_e, halves, vecs = split_at(2, call(
        functools.partial(ffn_early_kernel, 0),
        [((block, width), BF)] * 2 + [((width // 2, ff), BF)] * 2 + [((ff // 2, width), BF)] * 2
        + [((3, width), FL), ((1, ff), FL)],
        (place, g, w_down, *send_e[1:5], *keep_e[1:5], *sums_l), "ffn_early", 1,
    ), 6)
    up_keep, up_send, down_keep, down_send = halves
    up_got = swap(up_send, "dp", n_dp, 1)
    down_got = swap(down_send, "dp", n_dp, 2)
    (gnt_l,) = work(place, [("sum", 0, *gnt_l)], "add_late_chips", (up_keep,), 5e9)
    gnt_l = (gnt_l, cores(gnt_l, n_tensor))
    (gnt_e,) = work(place, [("sum", 0, keep_e[-1], gnt_e)], "add_early", gnt_l[:1])
    gnt_e = chips(gnt_e, n_tensor)
    hidden_l, hidden_e = (send_l[0], keep_l[0]), (send_e[0], keep_e[0])

    sums = [((wide, total), FL), ((wide, total), FL), ((wide, width), FL), ((wide, width), FL), ((chunk, wide), BF)]
    turn_scr = [ctx_scr, ctx_scr]

    def back_args(hidden, gnt, saved):
        qb, qv, probs, ctx = saved
        return (place, *hidden, *gnt, g, ffn_gain, w_out, ctx, probs, qb, qv, keys, values, w_pos, sin, cos, weights)

    gh_l, dk, dv, dpos, dout, dq, bias, part = call(
        functools.partial(back_late_kernel, late, block, heads, mem_len),
        [((chunk, width), FL), *sums, ((2, wide), FL), ((chunk, width), BF)],
        back_args(hidden_l, gnt_l, saved_l), "back_late", 1, turn_scr,
    )
    gnt_e, up_keep, up_send, down_keep, down_send = work(
        place, [("sum", 0, *gnt_e), ("halve", 1, up_keep, up_got), ("halve", 0, down_keep, down_got)], "add_middle", (bias,)
    )
    up_got = swap(up_send, "dp", n_dp, 2)
    down_got = swap(down_send, "dp", n_dp, 1)
    gnt_e = (gnt_e, cores(gnt_e, n_tensor))
    groups = n_dp // 2
    size = max(16, -(-5 * wide // groups // 16) * 16)
    gh_e, dk, dv, dpos, dout, dq_e, bias = call(
        functools.partial(back_early_kernel, 0, block, heads, mem_len),
        [((chunk, width), FL), *sums, ((2, wide), FL)],
        (*back_args(hidden_e, gnt_e, saved_e)[:-1], dk, dv, dpos, dout, bias), "back_early", 1, turn_scr,
    )
    keep, send, a_keep, a_send, f_rows = call(
        functools.partial(back_end_kernel, 0, block, heads, mem_len, n_tensor, size),
        [*[((seq_len, width), BF)] * 2, *[((groups // 2 * (size + small), width), BF)] * 2, ((chunk // 2, width), BF)],
        (place, weights, normed, attn_shift, attn_gain, dk, dv, dpos, dout, dq_e, bias, dq, part, *vecs, *shares_e,
         *shares_l, up_keep, up_got, down_keep, down_got), "back_end", 1,
    )
    bits = list(range((n_dp - 1).bit_length()))
    attn = Chain(a_keep, a_send, bits, n_dp, "split")
    if len(bits) > 3:
        f_rows, f_send = work(place, [("halve", 2, f_rows, jnp.zeros_like(f_rows))], "halve_ffn")
    else:
        f_send = f_rows
    ffn = Chain(f_rows, f_send, bits[2:], n_dp, "two" if len(bits) == 3 else "sum")
    rows = (keep, cores(send, n_tensor))
    count, stage = 0, 0
    while attn.left() > 0:
        jobs = [attn.job()]
        if count == 0:
            pass
        elif stage == 0:
            jobs.append(ffn.job())
        elif stage == 1:
            jobs += [("join", 1, up, up_got), ("join", 0, down, down_got)]
        elif stage == 2:
            jobs += [("join", 0, up, up_got), ("copy", 0, down, down)]
        if attn.left() == 1:
            jobs.append(("copy", 0, totals, totals))
        if count == 0 or attn.left() == 1:
            jobs.append(("sum", 0, *rows))
        results = work(place, jobs, f"step_{count}", cost=STEP_COST if count == 2 else 1)
        if attn.job()[0] == "split":
            totals = results.pop(1)
        if count == 0 or attn.left() == 1:
            rows = results.pop()
            rows = (rows, (other_chips if count == 0 else cores)(rows, n_tensor))
        if attn.left() == 1:
            totals = results.pop()
            totals = [totals] + [swap(totals, "tensor", n_tensor, k) for k in range(1, n_tensor)]
        attn.take(results)
        if count == 0:
            pass
        elif stage == 0 and ffn.left() > 0:
            ffn.take(results)
        elif stage == 0:
            up, down = results if len(results) == 2 else (results[0][: chunk // 4], results[0][chunk // 4 :])
            up_got, down_got = swap(up, "dp", n_dp, 2), swap(down, "dp", n_dp, 1)
            stage = 1
        elif stage == 1:
            up, down = results
            up_got = swap(up, "dp", n_dp, 1)
            stage = 2
        elif stage == 2:
            up, down = results
            down_got = swap(down, "dp", n_dp, 2)
            stage = 3
        count += 1
    output, input_grad, g_up = call(
        functools.partial(finish_kernel, block), [(x.shape, BF)] * 2 + [((width, ff), FL)],
        (place, x, attn_gain, gh_e, gh_l, *hidden_e, *hidden_l, *rows, down_bias, up), "finish", 1,
        [pltpu.VMEM(x.shape, BF)] * 2 + [pltpu.VMEM((width, ff), FL), pltpu.SemaphoreType.DMA((9,))],
        after=(attn.rows,), far=3,
    )
    output_there = pltpu.with_memory_space_constraint(output, pltpu.HBM)
    g_down, g_query, g_key, g_value, g_pos, g_out, *vecs = call(
        functools.partial(last_kernel, wide, heads, n_tensor),
        [((ff, width), FL)] + [((width, wide), FL)] * 4 + [((wide, width), FL)]
        + [((1, width), FL)] * 5 + [((heads, HEAD), FL)] * 2 + [((1, ff), FL)],
        (place, attn.rows, attn.got, down, down_got, *totals), "last", 1,
        [pltpu.VMEM((ff, width), FL), pltpu.VMEM((groups * size, width), FL), pltpu.VMEM((4, width, wide), FL),
         pltpu.SemaphoreType.DMA((6,))],
        after=(output_there,), far=6,
    )
    return (
        output[None],
        input_grad[None],
        vecs[0].reshape(-1),
        vecs[1].reshape(-1),
        g_query,
        g_key,
        g_value,
        g_pos,
        vecs[5],
        vecs[6],
        g_out,
        vecs[2].reshape(-1),
        vecs[3].reshape(-1),
        g_up,
        vecs[7].reshape(-1),
        g_down,
        vecs[4].reshape(-1),
    )


def solution(mesh):
    split, whole = P(None, "tensor"), P()
    return jax.shard_map(
        functools.partial(per_device, mesh.shape["dp"], mesh.shape["tensor"]),
        mesh=mesh,
        in_specs=(
            P("dp", None, None), P("dp", None, None), P("dp"), whole, whole, split, split, split, split,
            P("tensor", None), P("tensor", None), P("tensor", None), whole, whole, split, P("tensor"),
            P("tensor", None), whole, P("dp", None, None),
        ),
        out_specs=(
            P("dp", None, None), P("dp", None, None), whole, whole, split, split, split, split,
            P("tensor", None), P("tensor", None), P("tensor", None), whole, whole, split, P("tensor"),
            P("tensor", None), whole,
        ),
        check_vma=False,
    )
```

```python
import functools

import jax
import jax.numpy as jnp
import numpy as np
from jax import lax
from jax.experimental import pallas as pl
from jax.experimental.pallas import tpu as pltpu
from jax.sharding import PartitionSpec as P

HEAD = 64
BF = jnp.bfloat16
FL = jnp.float32
eps_norm = 1e-05
neg_fill = -1e30
VMEM_LIMIT = 24 * 1024 * 1024
small = 16
UNROLL = [2, 2, 2]
STEP_COST = 5e9


def mm(left, right):
    return lax.dot_general(left, right, (((1,), (0,)), ((), ())), preferred_element_type=FL)


def mm_t(left, right):
    return lax.dot_general(left, right, (((1,), (1,)), ((), ())), preferred_element_type=FL)


def t_mm(left, right):
    return lax.dot_general(left, right, (((0,), (0,)), ((), ())), preferred_element_type=FL)


def norm_parts(rows):
    center = rows - jnp.mean(rows, axis=-1, keepdims=True)
    spread = jnp.mean(center * center, axis=-1, keepdims=True)
    inv = lax.rsqrt(spread + eps_norm)
    return center * inv, inv


def norm_back(scaled, unit, inv):
    flat = jnp.mean(scaled, axis=-1, keepdims=True)
    along = jnp.mean(scaled * unit, axis=-1, keepdims=True)
    return inv * (scaled - flat - unit * along)


def head_lanes(wide, h):
    lane = lax.broadcasted_iota(jnp.int32, (1, wide), 1)
    return (lane >= h * HEAD) & (lane < (h + 1) * HEAD)


def col_sum(rows):
    return jnp.sum(rows, axis=0, keepdims=True)


def fine_mm(left, right, product):
    high = left.astype(BF)
    low = (left - high.astype(FL)).astype(BF)
    return product(high, right) + product(low, right)


def norm_sums(weighted, shift_sum, gain, shift):
    return (weighted - shift * shift_sum) / gain, shift_sum


def loop(count, body, unroll=1):
    def step(i, carry):
        body(i)
        return carry

    lax.fori_loop(0, count, step, 0, unroll=unroll)


def rows_of(i, size):
    return pl.ds(pl.multiple_of(i * size, size), size)


def by_core(core, part, keep_ref, send_ref, rows, at):
    @pl.when(core == part)
    def _():
        keep_ref[at, :] = rows

    @pl.when(core != part)
    def _():
        send_ref[at, :] = rows


def added(left, right):
    return (left.astype(FL) + right.astype(FL)).astype(BF)


def make_queries(normed, spots, at, refs, heads):
    w_ref, wpos_ref, bu, bv, sin_ref, cos_ref, qb_ref, qv_ref = refs
    wide = heads * HEAD
    scale = HEAD ** (-0.5)
    query = mm(normed, w_ref[:, :wide]).astype(BF).astype(FL)
    query_u = (query + bu).astype(BF).astype(FL) * scale
    query_v = (query + bv).astype(BF).astype(FL) * scale
    qv_ref[at, :] = query_v.astype(BF)
    sin = sin_ref[spots, :]
    cos = cos_ref[spots, :]
    half = sin.shape[1]
    for h in range(heads):
        lanes = head_lanes(wide, h)
        qb_ref[h, at, :wide] = jnp.where(lanes, query_u, 0.0).astype(BF)
        coef = mm_t(jnp.where(lanes, query_v, 0.0).astype(BF), wpos_ref[...])
        on_sin, on_cos = coef[:, :half], coef[:, half:]
        qb_ref[h, at, wide : wide + half] = (on_sin * sin + on_cos * cos).astype(BF)
        qb_ref[h, at, wide + half :] = (on_cos * sin - on_sin * cos).astype(BF)


def attend(first, block, mem_len, heads, count, qb_ref, kt_ref, v_ref, probs_ref, ctx_ref, ctx_scr):
    wide = heads * HEAD
    rows = qb_ref.shape[1]
    for part in range(rows // block):
        at = slice(part * block, (part + 1) * block)
        start = first + part * block
        seen = mem_len + start + block

        def one_head(h):
            scores = mm_t(qb_ref[h, at, :], kt_ref[:seen, :])
            query_pos = start + lax.broadcasted_iota(jnp.int32, (block, 1), 0)
            limit = jnp.minimum(query_pos, count - 1)
            key_pos = lax.broadcasted_iota(jnp.int32, (block, seen - mem_len), 1)
            scores = jnp.concatenate(
                [scores[:, :mem_len], jnp.where(key_pos <= limit, scores[:, mem_len:], neg_fill)], axis=1
            )
            expo = jnp.exp(scores - jnp.max(scores, axis=-1, keepdims=True))
            probs = (expo * (1.0 / jnp.sum(expo, axis=-1, keepdims=True))).astype(BF)
            probs_ref[h, at, :seen] = probs
            found = mm(probs, v_ref[:seen, :])
            ctx_scr[...] = jnp.where(head_lanes(wide, h), found, ctx_scr[...])

        loop(heads, one_head, UNROLL[2])
        ctx_ref[at, :] = ctx_scr[...].astype(BF)


def front_kernel(
    block, heads,
    place_ref, x_in, mem_in, g_in, wq_in, wk_in, wv_in, wpos_in, wup_in, wdown_in, wout_in,
    shift_in, gain_in, fgain_in, fshift_in, upb_in, downb_in, bu_in, bv_in, table_in, sin_in, cos_in,
    x_ref, g_ref, w_ref, wpos_ref, wup_ref, wdown_ref, wout_ref, shift_ref, gain_ref, fgain_ref, fshift_ref, upb_ref,
    downb_ref, sin_ref, cos_ref, bias_ref, normed_ref, kt_ref, v_ref,
    mem_ref, bu_ref, bv_ref, sems,
):
    wide = heads * HEAD
    mem_len = mem_in.shape[0]
    seq_len = x_in.shape[0]
    todo = [
        (mem_in, mem_ref), (gain_in, gain_ref), (shift_in, shift_ref), (wk_in, w_ref.at[:, wide : 2 * wide]),
        (wv_in, w_ref.at[:, 2 * wide :]), (x_in, x_ref), (wq_in, w_ref.at[:, :wide]), (bu_in, bu_ref), (bv_in, bv_ref),
        (wpos_in, wpos_ref), (sin_in, sin_ref), (cos_in, cos_ref), (table_in, kt_ref.at[:, wide:]),
        (wout_in, wout_ref), (wup_in, wup_ref), (wdown_in, wdown_ref), (g_in, g_ref), (fgain_in, fgain_ref),
        (fshift_in, fshift_ref), (upb_in, upb_ref), (downb_in, downb_ref),
    ]
    copies = [pltpu.make_async_copy(src, dst, sems.at[i]) for i, (src, dst) in enumerate(todo)]
    for copy in copies:
        copy.start()
    for copy in copies[:5]:
        copy.wait()

    def project(rows_ref, at, to):
        unit, _ = norm_parts(rows_ref[at, :].astype(FL))
        normed = (unit * gain_ref[...] + shift_ref[...]).astype(BF)
        normed_ref[to, :] = normed
        pair = mm(normed, w_ref[:, wide:]).astype(BF)
        kt_ref[to, :wide] = pair[:, :wide]
        v_ref[to, :] = pair[:, wide:]

    def some_memory(i):
        project(mem_ref, rows_of(i, block), rows_of(i, block))

    def some_rows(i):
        project(x_ref, rows_of(i, block), rows_of(i + mem_len // block, block))

    loop(mem_len // block, some_memory, UNROLL[0])
    for copy in copies[5:7]:
        copy.wait()
    loop(seq_len // block, some_rows, UNROLL[0])
    for copy in copies[7:]:
        copy.wait()
    bias_ref[0:1, :] = jnp.concatenate([bu_ref[h : h + 1, :] for h in range(heads)], axis=1)
    bias_ref[1:2, :] = jnp.concatenate([bv_ref[h : h + 1, :] for h in range(heads)], axis=1)


def attend_kernel(
    first, block, heads, mem_len,
    count_ref, normed_ref, kt_ref, v_ref, w_ref, wpos_ref, bias_ref, sin_ref, cos_ref,
    qb_ref, qv_ref, probs_ref, ctx_ref, ctx_scr,
):
    def some_queries(i):
        at = rows_of(i, block)
        spots = rows_of(i + first // block, block)
        make_queries(
            normed_ref[rows_of(i + (mem_len + first) // block, block), :], spots, at,
            (w_ref, wpos_ref, bias_ref[0:1, :], bias_ref[1:2, :], sin_ref, cos_ref, qb_ref, qv_ref), heads,
        )

    loop(qb_ref.shape[1] // block, some_queries, UNROLL[1])
    attend(first, block, mem_len, heads, count_ref[0], qb_ref, kt_ref, v_ref, probs_ref, ctx_ref, ctx_scr)


def relay_kernel(ctx_ref, w_ref, out_ref):
    size, wide = ctx_ref.shape
    out_ref[:size, :] = ctx_ref[...]
    for k in range(w_ref.shape[1] // wide):
        at = size + k * w_ref.shape[0]
        out_ref[at : at + w_ref.shape[0], :] = w_ref[:, k * wide : (k + 1) * wide]


def ffn_rows_kernel(
    first, block, roles,
    place_ref, x_ref, c0_ref, c1_ref, c2_ref, c3_ref, o0_ref, o1_ref, o2_ref, o3_ref, gain_ref, shift_ref, up_ref,
    upb_ref, down_ref, g_ref, *refs,
):
    core = place_ref[0]
    wide = c0_ref.shape[1]
    size = c0_ref.shape[0]
    blocks = [o3_ref[at : at + wide, :] for at in range(o3_ref.shape[0] - size, o3_ref.shape[0], wide)]
    o3 = jnp.concatenate(blocks, axis=1)
    for role, hidden_ref, normed_ref, activ_ref, gpre_ref, vec_ref, share_ref in zip(roles, *[iter(refs)] * 6):
        half = core if role == "keep" else 1 - core
        at = rows_of(half, block)
        spots = rows_of(half + first // block, block)
        attended = mm(c0_ref[at, :], o0_ref[...]) + mm(c1_ref[at, :], o1_ref[...])
        attended = attended + (mm(c2_ref[at, :], o2_ref[...]) + mm(c3_ref[at, :], o3))
        hidden = x_ref[spots, :].astype(FL) + attended
        hidden_ref[...] = hidden
        unit, _ = norm_parts(hidden)
        normed = (unit * gain_ref[...] + shift_ref[...]).astype(BF)
        normed_ref[...] = normed
        pre = mm(normed, up_ref[...]) + upb_ref[...]
        cdf = 0.5 + 0.5 * lax.erf(pre * np.float32(0.5**0.5))
        activ_ref[...] = (pre * cdf).astype(BF)
        slope = cdf + pre * jnp.exp(-0.5 * pre * pre) * np.float32((2 * np.pi) ** -0.5)
        grad_pre = (mm_t(g_ref[spots, :], down_ref[...]) * slope).astype(BF)
        gpre_ref[...] = grad_pre
        back = mm_t(grad_pre, up_ref[...])
        share_ref[...] = back.astype(BF)
        vec_ref[0:1, :] = col_sum(back * unit)
        vec_ref[1:2, :] = col_sum(back)


def ffn_weights(first, place_ref, g_ref, down_ref, saved, shares):
    core = place_ref[0]
    block = shares[0].shape[0]
    total = None
    for role, (normed_ref, activ_ref, gpre_ref, vec_ref), share_ref in zip(("send", "keep"), saved, shares):
        half = core if role == "keep" else 1 - core
        grads = g_ref[rows_of(half + first // block, block), :]
        activ = activ_ref[...]
        share_ref[...] = mm(activ, down_ref[...]).astype(BF)
        vecs = jnp.concatenate([vec_ref[...], col_sum(grads.astype(FL))], axis=0)
        new = [t_mm(normed_ref[...], gpre_ref[...]), t_mm(activ, grads), vecs, col_sum(gpre_ref[...].astype(FL))]
        total = new if total is None else [old + part for old, part in zip(total, new)]
    return total


def ffn_late_kernel(first, place_ref, g_ref, down_ref, *refs):
    found = ffn_weights(first, place_ref, g_ref, down_ref, (refs[:4], refs[4:8]), refs[8:10])
    for ref, value in zip(refs[10:], found):
        ref[...] = value


def ffn_early_kernel(first, place_ref, g_ref, down_ref, *refs):
    found = ffn_weights(first, place_ref, g_ref, down_ref, (refs[:4], refs[4:8]), refs[12:14])
    up, down, vec, upb = (value + old[...] for value, old in zip(found, refs[8:12]))
    up_keep, up_send, down_keep, down_send, vec_ref, upb_out = refs[14:]
    halve(place_ref, 0, up.astype(BF), up_keep, up_send)
    halve(place_ref, 1, down.astype(BF), down_keep, down_send)
    vec_ref[...] = vec
    upb_out[...] = upb


def back_rows(
    first, block, heads, mem_len, place_ref, hid_s, hid_k, mine_ref, other_ref, g_ref, fgain_ref, wout_ref, ctx_ref,
    probs_ref, qb_ref, qv_ref, kt_ref, v_ref, wpos_ref, sin_ref, cos_ref,
    gh_ref, dk_ref, dv_ref, dpos_ref, dout_ref, dq_ref, bias_ref, grad_u, grad_v,
):
    core = place_ref[0]
    wide = heads * HEAD
    half = sin_ref.shape[1]
    scale = HEAD ** (-0.5)
    for part in range(2):
        at = slice(part * block, (part + 1) * block)
        spots = slice(first + part * block, first + (part + 1) * block)
        seen = mem_len + first + (part + 1) * block
        unit, inv = norm_parts(jnp.where(core == part, hid_k[...], hid_s[...]))
        summed = jnp.where(core == part, mine_ref[...].astype(FL), other_ref[...].astype(FL))
        grad_hidden = g_ref[spots, :].astype(FL) + norm_back(summed * fgain_ref[...], unit, inv)
        gh_ref[at, :] = grad_hidden
        gh = grad_hidden.astype(BF)
        context = ctx_ref[at, :]
        grad_context = mm_t(gh, wout_ref[...]).astype(BF).astype(FL)
        dout_ref[...] += t_mm(context, gh)
        along_context = grad_context * context.astype(FL)

        def one_head(h):
            lanes = head_lanes(wide, h)
            delta = jnp.sum(jnp.where(lanes, along_context, 0.0), axis=-1, keepdims=True)
            own = jnp.where(lanes, grad_context, 0.0).astype(BF)
            probs = probs_ref[h, at, :seen]
            grad_score = (probs.astype(FL) * (mm_t(own, v_ref[:seen, :]) - delta)).astype(BF)
            dv_ref[:, :seen] += t_mm(own, probs)
            dk_ref[:, :seen] += t_mm(qb_ref[h, at, :wide], grad_score)
            spread = mm(grad_score, kt_ref[:seen, :])
            grad_u[...] = jnp.where(lanes, spread[:, :wide], grad_u[...])
            sin = sin_ref[spots, :]
            cos = cos_ref[spots, :]
            on_cos, on_sin = spread[:, wide : wide + half], spread[:, wide + half :]
            turned = jnp.concatenate(
                [(on_cos * sin - on_sin * cos).astype(BF), (on_cos * cos + on_sin * sin).astype(BF)], axis=1
            )
            grad_v[...] = jnp.where(lanes, mm(turned, wpos_ref[...]), grad_v[...])
            query_v = jnp.where(lanes, qv_ref[at, :].astype(FL), 0.0).astype(BF)
            dpos_ref[...] += t_mm(query_v, turned)

        loop(heads, one_head, 2)
        bias_ref[0:1, :] += col_sum(grad_u[...]) * scale
        bias_ref[1:2, :] += col_sum(grad_v[...]) * scale
        dq_ref[at, :] = ((grad_u[...] + grad_v[...]) * scale).astype(BF)


def back_share(cols, dq_rows, dk_ref, dv_ref, weights):
    pair = [dk_ref[:, cols].T.astype(BF), dv_ref[:, cols].T.astype(BF)]
    return mm_t(jnp.concatenate([dq_rows, *pair], axis=1), weights).astype(BF)


def back_late_kernel(
    first, block, heads, mem_len,
    place_ref, hid_s, hid_k, mine_ref, other_ref, g_ref, fgain_ref, wout_ref, ctx_ref, probs_ref, qb_ref, qv_ref, kt_ref,
    v_ref, wpos_ref, sin_ref, cos_ref, w_ref,
    gh_ref, dk_ref, dv_ref, dpos_ref, dout_ref, dq_ref, bias_ref, share_ref, grad_u, grad_v,
):
    for ref in (dk_ref, dv_ref, dpos_ref, dout_ref, bias_ref):
        ref[...] = jnp.zeros(ref.shape, FL)
    back_rows(
        first, block, heads, mem_len, place_ref, hid_s, hid_k, mine_ref, other_ref, g_ref, fgain_ref, wout_ref, ctx_ref,
        probs_ref, qb_ref, qv_ref, kt_ref, v_ref, wpos_ref, sin_ref, cos_ref,
        gh_ref, dk_ref, dv_ref, dpos_ref, dout_ref, dq_ref, bias_ref, grad_u, grad_v,
    )
    for part in range(2):
        at = slice(part * block, (part + 1) * block)
        cols = slice(mem_len + first + part * block, mem_len + first + (part + 1) * block)
        share_ref[at, :] = back_share(cols, dq_ref[at, :], dk_ref, dv_ref, w_ref[...])


def back_early_kernel(
    first, block, heads, mem_len,
    place_ref, hid_s, hid_k, mine_ref, other_ref, g_ref, fgain_ref, wout_ref, ctx_ref, probs_ref, qb_ref, qv_ref, kt_ref,
    v_ref, wpos_ref, sin_ref, cos_ref, dk_in, dv_in, dpos_in, dout_in, bias_in,
    gh_ref, dk_ref, dv_ref, dpos_ref, dout_ref, dq_ref, bias_ref, grad_u, grad_v,
):
    for ref, old in ((dk_ref, dk_in), (dv_ref, dv_in), (dpos_ref, dpos_in), (dout_ref, dout_in), (bias_ref, bias_in)):
        ref[...] = old[...]
    back_rows(
        first, block, heads, mem_len, place_ref, hid_s, hid_k, mine_ref, other_ref, g_ref, fgain_ref, wout_ref, ctx_ref,
        probs_ref, qb_ref, qv_ref, kt_ref, v_ref, wpos_ref, sin_ref, cos_ref,
        gh_ref, dk_ref, dv_ref, dpos_ref, dout_ref, dq_ref, bias_ref, grad_u, grad_v,
    )


def back_end_kernel(
    first, block, heads, mem_len, n_tensor, size,
    place_ref, w_ref, normed_ref, shift_ref, gain_ref, dk_ref, dv_ref, dpos_ref, dout_ref, dq_ref, bias_ref, dq_in,
    late_ref, fvec_ref, upb_ref, e_send, e_keep, l_send, l_keep, up_keep, up_got, down_keep, down_got,
    keep_ref, send_ref, a_keep, a_send, f_ref,
):
    half = up_keep.shape[0]
    f_ref[:half, :] = added(up_keep[...], up_got[...])
    f_ref[half:, :] = added(down_keep[...], down_got[...])
    wide = heads * HEAD
    core = place_ref[0]
    for part in range(2):
        at = slice(part * block, (part + 1) * block)
        by_core(core, part, keep_ref, send_ref, late_ref[at, :], slice(block, 2 * block))
    keep_ref[2 * block : 3 * block, :] = e_keep[...]
    keep_ref[3 * block :, :] = l_keep[...]
    send_ref[2 * block : 3 * block, :] = e_send[...]
    send_ref[3 * block :, :] = l_send[...]
    normed = normed_ref[...]
    width = normed.shape[1]
    dq_all = jnp.concatenate([dq_ref[...], dq_in[...]], axis=0)
    dk, dv = dk_ref[...].astype(BF), dv_ref[...].astype(BF)
    grads = [t_mm(dq_all, normed[mem_len:]), mm(dk, normed), mm(dv, normed), dpos_ref[...], dout_ref[...]]
    grads = jnp.concatenate(grads, axis=0)
    turned = w_ref[...].astype(FL).T
    shift_sum = fine_mm(col_sum(dq_all.astype(FL)), turned[:wide].astype(BF), mm)
    for i, part in enumerate((dk, dv)):
        shift_sum += col_sum(turned[(i + 1) * wide : (i + 2) * wide] * jnp.sum(part.astype(FL), axis=1, keepdims=True))
    sums = norm_sums(col_sum(turned * grads[: 3 * wide]), shift_sum, gain_ref[...], shift_ref[...])
    for part in range(2):
        at = slice(part * block, (part + 1) * block)
        cols = slice(mem_len + first + part * block, mem_len + first + (part + 1) * block)
        back = back_share(cols, dq_ref[at, :], dk_ref, dv_ref, w_ref[...])
        by_core(core, part, keep_ref, send_ref, back, slice(0, block))
    wider = jnp.zeros((1, width - wide), FL)
    rows = [*sums, fvec_ref[0:2, :], fvec_ref[2:3, :] * (1.0 / n_tensor)]
    rows += [jnp.concatenate([bias_ref[i : i + 1, :], wider], axis=1) for i in range(2)]
    for i in range(upb_ref.shape[1] // width):
        rows.append(upb_ref[:, i * width : (i + 1) * width])
    rows.append(jnp.zeros((small - 7 - upb_ref.shape[1] // width, width), FL))
    rows = jnp.concatenate(rows, axis=0).astype(BF)
    step = size + small
    for d in range(2 * a_keep.shape[0] // step):
        here = max(0, min(size, 5 * wide - d * size))
        piece = [grads[d * size : d * size + here].astype(BF)] if here else []
        piece += [jnp.zeros((size - here, width), BF)] if here < size else []
        piece = jnp.concatenate([*piece, rows], axis=0)
        per_half = a_keep.shape[0] // step
        at = slice(d % per_half * step, (d % per_half + 1) * step)
        by_core(place_ref[1] & 1, d // per_half, a_keep, a_send, piece, at)


def last_kernel(
    wide, heads, n_tensor, place_ref, a_mine, a_got, down_mine, down_got, *refs
):
    totals, refs = refs[:n_tensor], refs[n_tensor:]
    down_out, outs, smalls = refs[0], refs[1:6], refs[6:14]
    down_scr, rows_scr, turned_scr, sems = refs[14:]
    copies = []

    def send(src, dst):
        copies.append(pltpu.make_async_copy(src, dst, sems.at[len(copies)]))
        copies[-1].start()

    join(place_ref, 1, down_mine, down_got, down_scr)
    send(down_scr, down_out)
    join(place_ref, 0, a_mine, a_got, rows_scr)
    send(rows_scr.at[pl.ds(4 * wide, wide), :], outs[4])
    for i in range(4):
        turned_scr[i] = rows_scr[i * wide : (i + 1) * wide, :].T
        send(turned_scr.at[i], outs[i])
    mine = totals[0]
    total = mine[...]
    for other in totals[1:]:
        total = total + other[...]
    for i in range(5):
        smalls[i][...] = total[i : i + 1, :]
    for k in range(2):
        for h in range(heads):
            smalls[5 + k][h : h + 1, :] = mine[5 + k : 6 + k, h * HEAD : (h + 1) * HEAD]
    width = mine.shape[1]
    for i in range(smalls[7].shape[1] // width):
        smalls[7][:, i * width : (i + 1) * width] = mine[7 + i : 8 + i, :]
    for copy in copies:
        copy.wait()


def finish_kernel(
    block, place_ref, x_ref, gain_ref, gh_e, gh_l, hid_es, hid_ek, hid_ls, hid_lk, mine_ref, other_ref, bias_ref, up_ref,
    out_ref, grad_ref, up_out, out_scr, grad_scr, up_scr, sems,
):
    core = place_ref[0]
    copies = []

    def send(src, dst):
        copies.append(pltpu.make_async_copy(src, dst, sems.at[len(copies)]))
        copies[-1].start()

    up_scr[...] = up_ref[...].astype(FL)
    send(up_scr, up_out)
    for first, gh_ref, hid_s, hid_k in ((0, gh_e, hid_es, hid_ek), (1, gh_l, hid_ls, hid_lk)):
        for part in range(2):
            at = slice(part * block, (part + 1) * block)
            spots = pl.ds((2 * first + part) * block, block)

            def summed(group):
                rows = slice(group * block, (group + 1) * block)
                return jnp.where(core == part, mine_ref[rows, :].astype(FL), other_ref[rows, :].astype(FL))

            hidden = jnp.where(core == part, hid_k[...], hid_s[...])
            out_scr[spots, :] = (hidden + summed(first + 2) + bias_ref[...]).astype(BF)
            send(out_scr.at[spots, :], out_ref.at[spots, :])
            unit, inv = norm_parts(x_ref[spots, :].astype(FL))
            grad_scr[spots, :] = (gh_ref[at, :] + norm_back(summed(first) * gain_ref[...], unit, inv)).astype(BF)
            send(grad_scr.at[spots, :], grad_ref.at[spots, :])
    for copy in copies:
        copy.wait()


def halve(place_ref, bit, total, keep_ref, send_ref):
    size = total.shape[0] // 2
    high = (place_ref[1] >> bit) & 1
    by_core(high, 0, keep_ref, send_ref, total[:size], slice(None))
    by_core(high, 1, keep_ref, send_ref, total[size:], slice(None))


def join(place_ref, bit, mine_ref, got_ref, out_ref):
    size = mine_ref.shape[0]
    high = ((place_ref[1] >> bit) & 1) == 1
    mine, got = mine_ref[...].astype(FL), got_ref[...].astype(FL)
    out_ref[:size, :] = jnp.where(high, got, mine).astype(out_ref.dtype)
    out_ref[size:, :] = jnp.where(high, mine, got).astype(out_ref.dtype)


SMEM = pl.BlockSpec(memory_space=pltpu.SMEM)
PLACE = object()
SPECS = {s: pl.BlockSpec(memory_space=s) for s in (pltpu.VMEM, pltpu.HBM)}


def call(kernel, outs, args, name, flops, scratch=(), space=pltpu.VMEM, after=(), far=0):
    placed = args[0] is PLACE
    args = args[1:] if placed else args
    count, extra = len(args), len(after)

    def body(*refs):
        place = [(lax.axis_index("tensor") & 1, lax.axis_index("dp"))] if placed else []
        kernel(*place, *refs[:count], *refs[count + extra :])

    specs = [SMEM if a.dtype == jnp.int32 else SPECS[space] for a in args]
    specs += [pl.BlockSpec(memory_space=pl.ANY)] * extra
    if space is pltpu.HBM:
        args = [a if a.dtype == jnp.int32 else pltpu.with_memory_space_constraint(a, space) for a in args]
    return pl.pallas_call(
        body,
        out_shape=[pltpu.HBM(s, d) if i < far else jax.ShapeDtypeStruct(s, d) for i, (s, d) in enumerate(outs)],
        in_specs=specs,
        out_specs=[SPECS[pltpu.HBM]] * far + [SPECS[pltpu.VMEM]] * (len(outs) - far),
        scratch_shapes=scratch,
        compiler_params=pltpu.CompilerParams(vmem_limit_bytes=VMEM_LIMIT),
        cost_estimate=pl.CostEstimate(flops=int(flops), bytes_accessed=1, transcendentals=0),
        name=name,
    )(*args, *after)


def swap(rows, axis, size, bit):
    return lax.ppermute(rows, axis, [(i, i ^ bit) for i in range(size)])


def work_kernel(jobs, place_ref, *refs):
    ins, outs = refs[: 2 * len(jobs)], list(refs[2 * len(jobs) :])
    for i, (kind, bit) in enumerate(jobs):
        mine, got = ins[2 * i : 2 * i + 2]
        if kind == "halve":
            halve(place_ref, bit, added(mine[...], got[...]), outs.pop(0), outs.pop(0))
        elif kind == "join":
            join(place_ref, bit, mine, got, outs.pop(0))
        elif kind == "sum":
            outs.pop(0)[...] = added(mine[...], got[...])
        elif kind == "copy":
            outs.pop(0)[...] = mine[...]
        else:
            total = mine[...].astype(FL) + got[...].astype(FL)
            size = outs[0].shape[0]
            for part in (total[:size], total[size:]):
                out = outs.pop(0)
                out[...] = part.astype(out.dtype)


def work(place, jobs, name, after=(), cost=1):
    outs = []
    for kind, _, mine, _ in jobs:
        size, width = mine.shape
        outs += {
            "halve": [((size // 2, width), BF)] * 2,
            "two": [((size // 2, width), BF)] * 2,
            "join": [((2 * size, width), BF)],
            "sum": [((size, width), BF)],
            "copy": [((size, width), mine.dtype)],
            "split": [((size - small, width), BF), ((small, width), FL)],
        }[kind]
    args = [a for job in jobs for a in job[2:]]
    return list(
        call(functools.partial(work_kernel, [job[:2] for job in jobs]), outs, (place, *args), name, cost, after=after)
    )


class Chain:
    def __init__(self, rows, send, bits, n_dp, end="sum"):
        self.rows, self.send, self.bits, self.n_dp, self.end, self.done = rows, send, bits, n_dp, end, 0
        self.start()

    def bit(self):
        return self.bits[min(self.done, 2 * len(self.bits) - 2 - self.done)]

    def start(self):
        self.got = swap(self.send, "dp", self.n_dp, 1 << self.bit())

    def left(self):
        return 2 * len(self.bits) - 2 - self.done

    def job(self):
        last = len(self.bits) - 1
        if self.done < last - 1:
            kind, bit = "halve", self.bits[self.done + 1]
        elif self.done <= last:
            kind, bit = (self.end if self.done == last else "sum"), 0
        else:
            kind, bit = "join", self.bit()
        return kind, bit, self.rows, self.got

    def take(self, results):
        kind = self.job()[0]
        self.rows = self.send = results.pop(0)
        if kind == "halve":
            self.send = results.pop(0)
        self.done += 1
        if self.left() >= 0:
            self.start()


def cores(rows, n_tensor):
    return swap(rows, "tensor", n_tensor, 1)


def other_chips(rows, n_tensor):
    return swap(rows, "tensor", n_tensor, 2)


def chips(rows, n_tensor):
    return rows, other_chips(rows, n_tensor)


def split_at(*parts):
    (items,) = (p for p in parts if not isinstance(p, int))
    places = [0, *(p for p in parts if isinstance(p, int)), len(items)]
    return [items[start:end] for start, end in zip(places, places[1:])]


def per_device(n_dp, n_tensor, *args):
    (inputs, memory, counts, attn_gain, attn_shift, w_query, w_key, w_value, w_pos, bias_u, bias_v, w_out,
     ffn_gain, ffn_shift, w_up, up_bias, w_down, down_bias, out_grad) = args
    _, seq_len, width = inputs.shape
    mem_len = memory.shape[1]
    total = mem_len + seq_len
    wide = w_query.shape[1]
    heads = wide // HEAD
    ff = w_up.shape[1]
    chunk = seq_len // 2
    block = chunk // 2
    late = chunk
    place = PLACE
    x, mem, g = inputs[0], memory[0], out_grad[0]
    row = lambda v: v.reshape(1, -1)

    freq = 1.0 / 10000.0 ** (np.arange(0, width, 2, dtype=np.float64) / width)
    key_phase = np.arange(total)[:, None] * freq[None, :]
    table = jnp.asarray(np.concatenate([np.cos(key_phase), np.sin(key_phase)], axis=1).astype(BF))
    row_phase = (np.arange(seq_len) + mem_len)[:, None] * freq[None, :]
    sin = jnp.asarray(np.sin(row_phase).astype(np.float32))
    cos = jnp.asarray(np.cos(row_phase).astype(np.float32))

    outs_of = [w_out, cores(w_out, n_tensor), swap(w_out, "tensor", n_tensor, 2)]

    def attend_outs(seen):
        return [((heads, chunk, wide + width), BF), ((chunk, wide), BF), ((heads, chunk, seen), BF), ((chunk, wide), BF)]

    ctx_scr = pltpu.VMEM((block, wide), FL)
    vectors = [row(v) for v in (attn_shift, attn_gain, ffn_gain, ffn_shift, up_bias, down_bias)]
    copied = [
        *[(a.shape, BF) for a in (x, g)], ((width, 3 * wide), BF), *[(a.shape, BF) for a in (w_pos, w_up, w_down, w_out)],
        *[(a.shape, FL) for a in (*vectors, sin, cos)], ((2, wide), FL),
    ]
    found = call(
        functools.partial(front_kernel, block, heads),
        [*copied, ((total, width), BF), ((total, wide + width), BF), ((total, wide), BF)],
        (place, x, mem, g, w_query, w_key, w_value, w_pos, w_up, w_down, w_out, *vectors, bias_u, bias_v, table, sin,
         cos), "front", 1,
        [pltpu.VMEM(mem.shape, BF)] + [pltpu.VMEM(bias_u.shape, FL)] * 2 + [pltpu.SemaphoreType.DMA((21,))], pltpu.HBM,
    )
    x, g, weights, w_pos, w_up, w_down, w_out = found[:7]
    attn_shift, attn_gain, ffn_gain, ffn_shift, up_bias, down_bias, sin, cos, biases, normed, keys, values = found[7:]

    def attend_chunk(first, name, cost, after):
        return call(
            functools.partial(attend_kernel, first, block, heads, mem_len),
            attend_outs(mem_len + first + chunk),
            (counts, normed, keys, values, weights, w_pos, biases, sin, cos), name, cost, [ctx_scr], after=after,
        )

    saved_l = attend_chunk(late, "attend_late", 1, ())
    ctx_l = [saved_l[-1], cores(saved_l[-1], n_tensor), swap(saved_l[-1], "tensor", n_tensor, 2)]
    saved_e = attend_chunk(0, "attend_early", 5e9, outs_of[1:])
    ctx_e = [saved_e[-1], cores(saved_e[-1], n_tensor), swap(saved_e[-1], "tensor", n_tensor, 2)]
    (relay,) = call(
        relay_kernel, [((chunk + width, wide), BF)], (ctx_l[2], outs_of[2]), "relay_late", 1, after=saved_e[-1:]
    )
    relay = cores(relay, n_tensor)
    ctx_l.append(relay)
    outs_of.append(relay)
    half_outs = [
        ((block, width), FL), ((block, width), BF), ((block, ff), BF), ((block, ff), BF), ((2, width), FL),
        ((block, width), BF),
    ]

    def ffn_rows(first, ctx, roles, name, after=()):
        found = call(
            functools.partial(ffn_rows_kernel, first, block, roles), half_outs * len(roles),
            (place, x, *ctx, *outs_of, ffn_gain, ffn_shift, w_up, up_bias, w_down, g), name, 1, after=after,
        )
        return [found[i : i + 6] for i in range(0, 6 * len(roles), 6)]

    sum_outs = [((width, ff), FL), ((ff, width), FL), ((3, width), FL), ((1, ff), FL)]
    (send_l,) = ffn_rows(late, ctx_l, ("send",), "ffn_send_late")
    gnt_l = cores(send_l[-1], n_tensor)
    (keep_l,) = ffn_rows(late, ctx_l, ("keep",), "ffn_keep_late", after=send_l[-1:])
    (relay,) = work(place, [("copy", 0, ctx_e[2], ctx_e[2])], "relay_early", keep_l[-1:], 5e9)
    ctx_e.append(cores(relay, n_tensor))
    (gnt_l,) = work(place, [("sum", 0, keep_l[-1], gnt_l)], "add_late", (relay,))
    gnt_l = chips(gnt_l, n_tensor)
    shares_l, sums_l = split_at(2, call(
        functools.partial(ffn_late_kernel, late),
        [((block, width), BF)] * 2 + sum_outs, (place, g, w_down, *send_l[1:5], *keep_l[1:5]), "ffn_late", 1,
        after=gnt_l[:1],
    ))
    send_e, keep_e = ffn_rows(0, ctx_e, ("send", "keep"), "ffn_rows_early", after=sums_l[3:4])
    gnt_e = cores(send_e[-1], n_tensor)
    shares_e, halves, vecs = split_at(2, call(
        functools.partial(ffn_early_kernel, 0),
        [((block, width), BF)] * 2 + [((width // 2, ff), BF)] * 2 + [((ff // 2, width), BF)] * 2
        + [((3, width), FL), ((1, ff), FL)],
        (place, g, w_down, *send_e[1:5], *keep_e[1:5], *sums_l), "ffn_early", 1,
    ), 6)
    up_keep, up_send, down_keep, down_send = halves
    up_got = swap(up_send, "dp", n_dp, 1)
    down_got = swap(down_send, "dp", n_dp, 2)
    (gnt_l,) = work(place, [("sum", 0, *gnt_l)], "add_late_chips", (up_keep,), 5e9)
    gnt_l = (gnt_l, cores(gnt_l, n_tensor))
    (gnt_e,) = work(place, [("sum", 0, keep_e[-1], gnt_e)], "add_early", gnt_l[:1])
    gnt_e = chips(gnt_e, n_tensor)
    hidden_l, hidden_e = (send_l[0], keep_l[0]), (send_e[0], keep_e[0])

    sums = [((wide, total), FL), ((wide, total), FL), ((wide, width), FL), ((wide, width), FL), ((chunk, wide), BF)]
    turn_scr = [ctx_scr, ctx_scr]

    def back_args(hidden, gnt, saved):
        qb, qv, probs, ctx = saved
        return (place, *hidden, *gnt, g, ffn_gain, w_out, ctx, probs, qb, qv, keys, values, w_pos, sin, cos, weights)

    gh_l, dk, dv, dpos, dout, dq, bias, part = call(
        functools.partial(back_late_kernel, late, block, heads, mem_len),
        [((chunk, width), FL), *sums, ((2, wide), FL), ((chunk, width), BF)],
        back_args(hidden_l, gnt_l, saved_l), "back_late", 1, turn_scr,
    )
    gnt_e, up_keep, up_send, down_keep, down_send = work(
        place, [("sum", 0, *gnt_e), ("halve", 1, up_keep, up_got), ("halve", 0, down_keep, down_got)], "add_middle", (bias,)
    )
    up_got = swap(up_send, "dp", n_dp, 2)
    down_got = swap(down_send, "dp", n_dp, 1)
    gnt_e = (gnt_e, cores(gnt_e, n_tensor))
    groups = n_dp // 2
    size = max(16, -(-5 * wide // groups // 16) * 16)
    gh_e, dk, dv, dpos, dout, dq_e, bias = call(
        functools.partial(back_early_kernel, 0, block, heads, mem_len),
        [((chunk, width), FL), *sums, ((2, wide), FL)],
        (*back_args(hidden_e, gnt_e, saved_e)[:-1], dk, dv, dpos, dout, bias), "back_early", 1, turn_scr,
    )
    keep, send, a_keep, a_send, f_rows = call(
        functools.partial(back_end_kernel, 0, block, heads, mem_len, n_tensor, size),
        [*[((seq_len, width), BF)] * 2, *[((groups // 2 * (size + small), width), BF)] * 2, ((chunk // 2, width), BF)],
        (place, weights, normed, attn_shift, attn_gain, dk, dv, dpos, dout, dq_e, bias, dq, part, *vecs, *shares_e,
         *shares_l, up_keep, up_got, down_keep, down_got), "back_end", 1,
    )
    bits = list(range((n_dp - 1).bit_length()))
    attn = Chain(a_keep, a_send, bits, n_dp, "split")
    if len(bits) > 3:
        f_rows, f_send = work(place, [("halve", 2, f_rows, jnp.zeros_like(f_rows))], "halve_ffn")
    else:
        f_send = f_rows
    ffn = Chain(f_rows, f_send, bits[2:], n_dp, "two" if len(bits) == 3 else "sum")
    rows = (keep, cores(send, n_tensor))
    count, stage = 0, 0
    while attn.left() > 0:
        jobs = [attn.job()]
        if count == 0:
            pass
        elif stage == 0:
            jobs.append(ffn.job())
        elif stage == 1:
            jobs += [("join", 1, up, up_got), ("join", 0, down, down_got)]
        elif stage == 2:
            jobs += [("join", 0, up, up_got), ("copy", 0, down, down)]
        if attn.left() == 1:
            jobs.append(("copy", 0, totals, totals))
        if count == 0 or attn.left() == 1:
            jobs.append(("sum", 0, *rows))
        results = work(place, jobs, f"step_{count}", cost=STEP_COST if count == 2 else 1)
        if attn.job()[0] == "split":
            totals = results.pop(1)
        if count == 0 or attn.left() == 1:
            rows = results.pop()
            rows = (rows, (other_chips if count == 0 else cores)(rows, n_tensor))
        if attn.left() == 1:
            totals = results.pop()
            totals = [totals] + [swap(totals, "tensor", n_tensor, k) for k in range(1, n_tensor)]
        attn.take(results)
        if count == 0:
            pass
        elif stage == 0 and ffn.left() > 0:
            ffn.take(results)
        elif stage == 0:
            up, down = results if len(results) == 2 else (results[0][: chunk // 4], results[0][chunk // 4 :])
            up_got, down_got = swap(up, "dp", n_dp, 2), swap(down, "dp", n_dp, 1)
            stage = 1
        elif stage == 1:
            up, down = results
            up_got = swap(up, "dp", n_dp, 1)
            stage = 2
        elif stage == 2:
            up, down = results
            down_got = swap(down, "dp", n_dp, 2)
            stage = 3
        count += 1
    output, input_grad, g_up = call(
        functools.partial(finish_kernel, block), [(x.shape, BF)] * 2 + [((width, ff), FL)],
        (place, x, attn_gain, gh_e, gh_l, *hidden_e, *hidden_l, *rows, down_bias, up), "finish", 1,
        [pltpu.VMEM(x.shape, BF)] * 2 + [pltpu.VMEM((width, ff), FL), pltpu.SemaphoreType.DMA((9,))],
        after=(attn.rows,), far=3,
    )
    output_there = pltpu.with_memory_space_constraint(output, pltpu.HBM)
    g_down, g_query, g_key, g_value, g_pos, g_out, *vecs = call(
        functools.partial(last_kernel, wide, heads, n_tensor),
        [((ff, width), FL)] + [((width, wide), FL)] * 4 + [((wide, width), FL)]
        + [((1, width), FL)] * 5 + [((heads, HEAD), FL)] * 2 + [((1, ff), FL)],
        (place, attn.rows, attn.got, down, down_got, *totals), "last", 1,
        [pltpu.VMEM((ff, width), FL), pltpu.VMEM((groups * size, width), FL), pltpu.VMEM((4, width, wide), FL),
         pltpu.SemaphoreType.DMA((6,))],
        after=(output_there,), far=6,
    )
    return (
        output[None],
        input_grad[None],
        vecs[0].reshape(-1),
        vecs[1].reshape(-1),
        g_query,
        g_key,
        g_value,
        g_pos,
        vecs[5],
        vecs[6],
        g_out,
        vecs[2].reshape(-1),
        vecs[3].reshape(-1),
        g_up,
        vecs[7].reshape(-1),
        g_down,
        vecs[4].reshape(-1),
    )


def solution(mesh):
    split, whole = P(None, "tensor"), P()
    return jax.shard_map(
        functools.partial(per_device, mesh.shape["dp"], mesh.shape["tensor"]),
        mesh=mesh,
        in_specs=(
            P("dp", None, None), P("dp", None, None), P("dp"), whole, whole, split, split, split, split,
            P("tensor", None), P("tensor", None), P("tensor", None), whole, whole, split, P("tensor"),
            P("tensor", None), whole, P("dp", None, None),
        ),
        out_specs=(
            P("dp", None, None), P("dp", None, None), whole, whole, split, split, split, split,
            P("tensor", None), P("tensor", None), P("tensor", None), whole, whole, split, P("tensor"),
            P("tensor", None), whole,
        ),
        check_vma=False,
    )
```

```python
import functools

import jax
import jax.numpy as jnp
import numpy as np
from jax import lax
from jax.experimental import pallas as pl
from jax.experimental.pallas import tpu as pltpu
from jax.sharding import PartitionSpec as P

HEAD = 64
BF = jnp.bfloat16
FL = jnp.float32
eps_norm = 1e-05
neg_fill = -1e30
VMEM_LIMIT = 24 * 1024 * 1024
small = 16
UNROLL = [2, 2, 2]
STEP_COST = 5e9


def mm(left, right):
    return lax.dot_general(left, right, (((1,), (0,)), ((), ())), preferred_element_type=FL)


def mm_t(left, right):
    return lax.dot_general(left, right, (((1,), (1,)), ((), ())), preferred_element_type=FL)


def t_mm(left, right):
    return lax.dot_general(left, right, (((0,), (0,)), ((), ())), preferred_element_type=FL)


def norm_parts(rows):
    center = rows - jnp.mean(rows, axis=-1, keepdims=True)
    spread = jnp.mean(center * center, axis=-1, keepdims=True)
    inv = lax.rsqrt(spread + eps_norm)
    return center * inv, inv


def norm_back(scaled, unit, inv):
    flat = jnp.mean(scaled, axis=-1, keepdims=True)
    along = jnp.mean(scaled * unit, axis=-1, keepdims=True)
    return inv * (scaled - flat - unit * along)


def head_lanes(wide, h):
    lane = lax.broadcasted_iota(jnp.int32, (1, wide), 1)
    return (lane >= h * HEAD) & (lane < (h + 1) * HEAD)


def col_sum(rows):
    return jnp.sum(rows, axis=0, keepdims=True)


def fine_mm(left, right, product):
    high = left.astype(BF)
    low = (left - high.astype(FL)).astype(BF)
    return product(high, right) + product(low, right)


def norm_sums(weighted, shift_sum, gain, shift):
    return (weighted - shift * shift_sum) / gain, shift_sum


def loop(count, body, unroll=1):
    def step(i, carry):
        body(i)
        return carry

    lax.fori_loop(0, count, step, 0, unroll=unroll)


def rows_of(i, size):
    return pl.ds(pl.multiple_of(i * size, size), size)


def by_core(core, part, keep_ref, send_ref, rows, at):
    @pl.when(core == part)
    def _():
        keep_ref[at, :] = rows

    @pl.when(core != part)
    def _():
        send_ref[at, :] = rows


def added(left, right):
    return (left.astype(FL) + right.astype(FL)).astype(BF)


def make_queries(normed, spots, at, refs, heads):
    w_ref, wpos_ref, bu, bv, sin_ref, cos_ref, qb_ref, qv_ref = refs
    wide = heads * HEAD
    scale = HEAD ** (-0.5)
    query = mm(normed, w_ref[:, :wide]).astype(BF).astype(FL)
    query_u = (query + bu).astype(BF).astype(FL) * scale
    query_v = (query + bv).astype(BF).astype(FL) * scale
    qv_ref[at, :] = query_v.astype(BF)
    sin = sin_ref[spots, :]
    cos = cos_ref[spots, :]
    half = sin.shape[1]
    for h in range(heads):
        lanes = head_lanes(wide, h)
        qb_ref[h, at, :wide] = jnp.where(lanes, query_u, 0.0).astype(BF)
        coef = mm_t(jnp.where(lanes, query_v, 0.0).astype(BF), wpos_ref[...])
        on_sin, on_cos = coef[:, :half], coef[:, half:]
        qb_ref[h, at, wide : wide + half] = (on_sin * sin + on_cos * cos).astype(BF)
        qb_ref[h, at, wide + half :] = (on_cos * sin - on_sin * cos).astype(BF)


def attend(first, block, mem_len, heads, count, qb_ref, kt_ref, v_ref, probs_ref, ctx_ref, ctx_scr):
    wide = heads * HEAD
    rows = qb_ref.shape[1]
    for part in range(rows // block):
        at = slice(part * block, (part + 1) * block)
        start = first + part * block
        seen = mem_len + start + block

        def one_head(h):
            scores = mm_t(qb_ref[h, at, :], kt_ref[:seen, :])
            query_pos = start + lax.broadcasted_iota(jnp.int32, (block, 1), 0)
            limit = jnp.minimum(query_pos, count - 1)
            key_pos = lax.broadcasted_iota(jnp.int32, (block, seen - mem_len), 1)
            scores = jnp.concatenate(
                [scores[:, :mem_len], jnp.where(key_pos <= limit, scores[:, mem_len:], neg_fill)], axis=1
            )
            expo = jnp.exp(scores - jnp.max(scores, axis=-1, keepdims=True))
            probs = (expo * (1.0 / jnp.sum(expo, axis=-1, keepdims=True))).astype(BF)
            probs_ref[h, at, :seen] = probs
            found = mm(probs, v_ref[:seen, :])
            ctx_scr[...] = jnp.where(head_lanes(wide, h), found, ctx_scr[...])

        loop(heads, one_head, UNROLL[2])
        ctx_ref[at, :] = ctx_scr[...].astype(BF)


def front_kernel(
    block, heads,
    place_ref, x_in, mem_in, g_in, wq_in, wk_in, wv_in, wpos_in, wup_in, wdown_in, wout_in,
    shift_in, gain_in, fgain_in, fshift_in, upb_in, downb_in, bu_in, bv_in, table_in, sin_in, cos_in,
    x_ref, g_ref, w_ref, wpos_ref, wup_ref, wdown_ref, wout_ref, shift_ref, gain_ref, fgain_ref, fshift_ref, upb_ref,
    downb_ref, sin_ref, cos_ref, bias_ref, normed_ref, kt_ref, v_ref,
    mem_ref, bu_ref, bv_ref, sems,
):
    wide = heads * HEAD
    mem_len = mem_in.shape[0]
    seq_len = x_in.shape[0]
    todo = [
        (mem_in, mem_ref), (gain_in, gain_ref), (shift_in, shift_ref), (wk_in, w_ref.at[:, wide : 2 * wide]),
        (wv_in, w_ref.at[:, 2 * wide :]), (x_in, x_ref), (wq_in, w_ref.at[:, :wide]), (bu_in, bu_ref), (bv_in, bv_ref),
        (wpos_in, wpos_ref), (sin_in, sin_ref), (cos_in, cos_ref), (table_in, kt_ref.at[:, wide:]),
        (wout_in, wout_ref), (wup_in, wup_ref), (wdown_in, wdown_ref), (g_in, g_ref), (fgain_in, fgain_ref),
        (fshift_in, fshift_ref), (upb_in, upb_ref), (downb_in, downb_ref),
    ]
    copies = [pltpu.make_async_copy(src, dst, sems.at[i]) for i, (src, dst) in enumerate(todo)]
    for copy in copies:
        copy.start()
    for copy in copies[:5]:
        copy.wait()

    def project(rows_ref, at, to):
        unit, _ = norm_parts(rows_ref[at, :].astype(FL))
        normed = (unit * gain_ref[...] + shift_ref[...]).astype(BF)
        normed_ref[to, :] = normed
        pair = mm(normed, w_ref[:, wide:]).astype(BF)
        kt_ref[to, :wide] = pair[:, :wide]
        v_ref[to, :] = pair[:, wide:]

    def some_memory(i):
        project(mem_ref, rows_of(i, block), rows_of(i, block))

    def some_rows(i):
        project(x_ref, rows_of(i, block), rows_of(i + mem_len // block, block))

    loop(mem_len // block, some_memory, UNROLL[0])
    for copy in copies[5:7]:
        copy.wait()
    loop(seq_len // block, some_rows, UNROLL[0])
    for copy in copies[7:]:
        copy.wait()
    bias_ref[0:1, :] = jnp.concatenate([bu_ref[h : h + 1, :] for h in range(heads)], axis=1)
    bias_ref[1:2, :] = jnp.concatenate([bv_ref[h : h + 1, :] for h in range(heads)], axis=1)


def attend_kernel(
    first, block, heads, mem_len,
    count_ref, normed_ref, kt_ref, v_ref, w_ref, wpos_ref, bias_ref, sin_ref, cos_ref,
    qb_ref, qv_ref, probs_ref, ctx_ref, ctx_scr,
):
    def some_queries(i):
        at = rows_of(i, block)
        spots = rows_of(i + first // block, block)
        make_queries(
            normed_ref[rows_of(i + (mem_len + first) // block, block), :], spots, at,
            (w_ref, wpos_ref, bias_ref[0:1, :], bias_ref[1:2, :], sin_ref, cos_ref, qb_ref, qv_ref), heads,
        )

    loop(qb_ref.shape[1] // block, some_queries, UNROLL[1])
    attend(first, block, mem_len, heads, count_ref[0], qb_ref, kt_ref, v_ref, probs_ref, ctx_ref, ctx_scr)


def relay_kernel(ctx_ref, w_ref, out_ref):
    size, wide = ctx_ref.shape
    out_ref[:size, :] = ctx_ref[...]
    for k in range(w_ref.shape[1] // wide):
        at = size + k * w_ref.shape[0]
        out_ref[at : at + w_ref.shape[0], :] = w_ref[:, k * wide : (k + 1) * wide]


def ffn_rows_kernel(
    first, block, roles,
    place_ref, x_ref, c0_ref, c1_ref, c2_ref, c3_ref, o0_ref, o1_ref, o2_ref, o3_ref, gain_ref, shift_ref, up_ref,
    upb_ref, down_ref, g_ref, *refs,
):
    core = place_ref[0]
    wide = c0_ref.shape[1]
    size = c0_ref.shape[0]
    blocks = [o3_ref[at : at + wide, :] for at in range(o3_ref.shape[0] - size, o3_ref.shape[0], wide)]
    o3 = jnp.concatenate(blocks, axis=1)
    for role, hidden_ref, normed_ref, activ_ref, gpre_ref, vec_ref, share_ref in zip(roles, *[iter(refs)] * 6):
        half = core if role == "keep" else 1 - core
        at = rows_of(half, block)
        spots = rows_of(half + first // block, block)
        attended = mm(c0_ref[at, :], o0_ref[...]) + mm(c1_ref[at, :], o1_ref[...])
        attended = attended + (mm(c2_ref[at, :], o2_ref[...]) + mm(c3_ref[at, :], o3))
        hidden = x_ref[spots, :].astype(FL) + attended
        hidden_ref[...] = hidden
        unit, _ = norm_parts(hidden)
        normed = (unit * gain_ref[...] + shift_ref[...]).astype(BF)
        normed_ref[...] = normed
        pre = mm(normed, up_ref[...]) + upb_ref[...]
        cdf = 0.5 + 0.5 * lax.erf(pre * np.float32(0.5**0.5))
        activ_ref[...] = (pre * cdf).astype(BF)
        slope = cdf + pre * jnp.exp(-0.5 * pre * pre) * np.float32((2 * np.pi) ** -0.5)
        grad_pre = (mm_t(g_ref[spots, :], down_ref[...]) * slope).astype(BF)
        gpre_ref[...] = grad_pre
        back = mm_t(grad_pre, up_ref[...])
        share_ref[...] = back.astype(BF)
        vec_ref[0:1, :] = col_sum(back * unit)
        vec_ref[1:2, :] = col_sum(back)


def ffn_weights(first, place_ref, g_ref, down_ref, saved, shares):
    core = place_ref[0]
    block = shares[0].shape[0]
    total = None
    for role, (normed_ref, activ_ref, gpre_ref, vec_ref), share_ref in zip(("send", "keep"), saved, shares):
        half = core if role == "keep" else 1 - core
        grads = g_ref[rows_of(half + first // block, block), :]
        activ = activ_ref[...]
        share_ref[...] = mm(activ, down_ref[...]).astype(BF)
        vecs = jnp.concatenate([vec_ref[...], col_sum(grads.astype(FL))], axis=0)
        new = [t_mm(normed_ref[...], gpre_ref[...]), t_mm(activ, grads), vecs, col_sum(gpre_ref[...].astype(FL))]
        total = new if total is None else [old + part for old, part in zip(total, new)]
    return total


def ffn_late_kernel(first, place_ref, g_ref, down_ref, *refs):
    found = ffn_weights(first, place_ref, g_ref, down_ref, (refs[:4], refs[4:8]), refs[8:10])
    for ref, value in zip(refs[10:], found):
        ref[...] = value


def ffn_early_kernel(first, place_ref, g_ref, down_ref, *refs):
    found = ffn_weights(first, place_ref, g_ref, down_ref, (refs[:4], refs[4:8]), refs[12:14])
    up, down, vec, upb = (value + old[...] for value, old in zip(found, refs[8:12]))
    up_keep, up_send, down_keep, down_send, vec_ref, upb_out = refs[14:]
    halve(place_ref, 0, up.astype(BF), up_keep, up_send)
    halve(place_ref, 1, down.astype(BF), down_keep, down_send)
    vec_ref[...] = vec
    upb_out[...] = upb


def back_rows(
    first, block, heads, mem_len, place_ref, hid_s, hid_k, mine_ref, other_ref, g_ref, fgain_ref, wout_ref, ctx_ref,
    probs_ref, qb_ref, qv_ref, kt_ref, v_ref, wpos_ref, sin_ref, cos_ref,
    gh_ref, dk_ref, dv_ref, dpos_ref, dout_ref, dq_ref, bias_ref, grad_u, grad_v,
):
    core = place_ref[0]
    wide = heads * HEAD
    half = sin_ref.shape[1]
    scale = HEAD ** (-0.5)
    for part in range(2):
        at = slice(part * block, (part + 1) * block)
        spots = slice(first + part * block, first + (part + 1) * block)
        seen = mem_len + first + (part + 1) * block
        unit, inv = norm_parts(jnp.where(core == part, hid_k[...], hid_s[...]))
        summed = jnp.where(core == part, mine_ref[...].astype(FL), other_ref[...].astype(FL))
        grad_hidden = g_ref[spots, :].astype(FL) + norm_back(summed * fgain_ref[...], unit, inv)
        gh_ref[at, :] = grad_hidden
        gh = grad_hidden.astype(BF)
        context = ctx_ref[at, :]
        grad_context = mm_t(gh, wout_ref[...]).astype(BF).astype(FL)
        dout_ref[...] += t_mm(context, gh)
        along_context = grad_context * context.astype(FL)

        def one_head(h):
            lanes = head_lanes(wide, h)
            delta = jnp.sum(jnp.where(lanes, along_context, 0.0), axis=-1, keepdims=True)
            own = jnp.where(lanes, grad_context, 0.0).astype(BF)
            probs = probs_ref[h, at, :seen]
            grad_score = (probs.astype(FL) * (mm_t(own, v_ref[:seen, :]) - delta)).astype(BF)
            dv_ref[:, :seen] += t_mm(own, probs)
            dk_ref[:, :seen] += t_mm(qb_ref[h, at, :wide], grad_score)
            spread = mm(grad_score, kt_ref[:seen, :])
            grad_u[...] = jnp.where(lanes, spread[:, :wide], grad_u[...])
            sin = sin_ref[spots, :]
            cos = cos_ref[spots, :]
            on_cos, on_sin = spread[:, wide : wide + half], spread[:, wide + half :]
            turned = jnp.concatenate(
                [(on_cos * sin - on_sin * cos).astype(BF), (on_cos * cos + on_sin * sin).astype(BF)], axis=1
            )
            grad_v[...] = jnp.where(lanes, mm(turned, wpos_ref[...]), grad_v[...])
            query_v = jnp.where(lanes, qv_ref[at, :].astype(FL), 0.0).astype(BF)
            dpos_ref[...] += t_mm(query_v, turned)

        loop(heads, one_head, 2)
        bias_ref[0:1, :] += col_sum(grad_u[...]) * scale
        bias_ref[1:2, :] += col_sum(grad_v[...]) * scale
        dq_ref[at, :] = ((grad_u[...] + grad_v[...]) * scale).astype(BF)


def back_share(cols, dq_rows, dk_ref, dv_ref, weights):
    pair = [dk_ref[:, cols].T.astype(BF), dv_ref[:, cols].T.astype(BF)]
    return mm_t(jnp.concatenate([dq_rows, *pair], axis=1), weights).astype(BF)


def back_late_kernel(
    first, block, heads, mem_len,
    place_ref, hid_s, hid_k, mine_ref, other_ref, g_ref, fgain_ref, wout_ref, ctx_ref, probs_ref, qb_ref, qv_ref, kt_ref,
    v_ref, wpos_ref, sin_ref, cos_ref, w_ref,
    gh_ref, dk_ref, dv_ref, dpos_ref, dout_ref, dq_ref, bias_ref, share_ref, grad_u, grad_v,
):
    for ref in (dk_ref, dv_ref, dpos_ref, dout_ref, bias_ref):
        ref[...] = jnp.zeros(ref.shape, FL)
    back_rows(
        first, block, heads, mem_len, place_ref, hid_s, hid_k, mine_ref, other_ref, g_ref, fgain_ref, wout_ref, ctx_ref,
        probs_ref, qb_ref, qv_ref, kt_ref, v_ref, wpos_ref, sin_ref, cos_ref,
        gh_ref, dk_ref, dv_ref, dpos_ref, dout_ref, dq_ref, bias_ref, grad_u, grad_v,
    )
    for part in range(2):
        at = slice(part * block, (part + 1) * block)
        cols = slice(mem_len + first + part * block, mem_len + first + (part + 1) * block)
        share_ref[at, :] = back_share(cols, dq_ref[at, :], dk_ref, dv_ref, w_ref[...])


def back_early_kernel(
    first, block, heads, mem_len,
    place_ref, hid_s, hid_k, mine_ref, other_ref, g_ref, fgain_ref, wout_ref, ctx_ref, probs_ref, qb_ref, qv_ref, kt_ref,
    v_ref, wpos_ref, sin_ref, cos_ref, dk_in, dv_in, dpos_in, dout_in, bias_in,
    gh_ref, dk_ref, dv_ref, dpos_ref, dout_ref, dq_ref, bias_ref, grad_u, grad_v,
):
    for ref, old in ((dk_ref, dk_in), (dv_ref, dv_in), (dpos_ref, dpos_in), (dout_ref, dout_in), (bias_ref, bias_in)):
        ref[...] = old[...]
    back_rows(
        first, block, heads, mem_len, place_ref, hid_s, hid_k, mine_ref, other_ref, g_ref, fgain_ref, wout_ref, ctx_ref,
        probs_ref, qb_ref, qv_ref, kt_ref, v_ref, wpos_ref, sin_ref, cos_ref,
        gh_ref, dk_ref, dv_ref, dpos_ref, dout_ref, dq_ref, bias_ref, grad_u, grad_v,
    )


def back_end_kernel(
    first, block, heads, mem_len, n_tensor, size,
    place_ref, w_ref, normed_ref, shift_ref, gain_ref, dk_ref, dv_ref, dpos_ref, dout_ref, dq_ref, bias_ref, dq_in,
    late_ref, fvec_ref, upb_ref, e_send, e_keep, l_send, l_keep, up_keep, up_got, down_keep, down_got,
    keep_ref, send_ref, a_keep, a_send, b_keep, b_send, f_ref,
):
    half = up_keep.shape[0]
    f_ref[:half, :] = added(up_keep[...], up_got[...])
    f_ref[half:, :] = added(down_keep[...], down_got[...])
    wide = heads * HEAD
    core = place_ref[0]
    for part in range(2):
        at = slice(part * block, (part + 1) * block)
        by_core(core, part, keep_ref, send_ref, late_ref[at, :], slice(block, 2 * block))
    keep_ref[2 * block : 3 * block, :] = e_keep[...]
    keep_ref[3 * block :, :] = l_keep[...]
    send_ref[2 * block : 3 * block, :] = e_send[...]
    send_ref[3 * block :, :] = l_send[...]
    normed = normed_ref[...]
    width = normed.shape[1]
    dq_all = jnp.concatenate([dq_ref[...], dq_in[...]], axis=0)
    dk, dv = dk_ref[...].astype(BF), dv_ref[...].astype(BF)
    grads = [t_mm(dq_all, normed[mem_len:]), mm(dk, normed), mm(dv, normed), dpos_ref[...], dout_ref[...]]
    grads = jnp.concatenate(grads, axis=0)
    turned = w_ref[...].astype(FL).T
    shift_sum = fine_mm(col_sum(dq_all.astype(FL)), turned[:wide].astype(BF), mm)
    for i, part in enumerate((dk, dv)):
        shift_sum += col_sum(turned[(i + 1) * wide : (i + 2) * wide] * jnp.sum(part.astype(FL), axis=1, keepdims=True))
    sums = norm_sums(col_sum(turned * grads[: 3 * wide]), shift_sum, gain_ref[...], shift_ref[...])
    for part in range(2):
        at = slice(part * block, (part + 1) * block)
        cols = slice(mem_len + first + part * block, mem_len + first + (part + 1) * block)
        back = back_share(cols, dq_ref[at, :], dk_ref, dv_ref, w_ref[...])
        by_core(core, part, keep_ref, send_ref, back, slice(0, block))
    wider = jnp.zeros((1, width - wide), FL)
    rows = [*sums, fvec_ref[0:2, :], fvec_ref[2:3, :] * (1.0 / n_tensor)]
    rows += [jnp.concatenate([bias_ref[i : i + 1, :], wider], axis=1) for i in range(2)]
    for i in range(upb_ref.shape[1] // width):
        rows.append(upb_ref[:, i * width : (i + 1) * width])
    rows.append(jnp.zeros((small - 7 - upb_ref.shape[1] // width, width), FL))
    rows = jnp.concatenate(rows, axis=0).astype(BF)
    for d in range(4):
        piece = jnp.concatenate([grads[d * size : (d + 1) * size].astype(BF), rows], axis=0)
        at = slice(d % 2 * (size + small), (d % 2 + 1) * (size + small))
        by_core(place_ref[1] & 1, d // 2, a_keep, a_send, piece, at)
        piece = grads[(d + 4) * size : (d + 5) * size].astype(BF)
        by_core((place_ref[1] >> 1) & 1, d // 2, b_keep, b_send, piece, slice(d % 2 * size, (d % 2 + 1) * size))


def last_kernel(wide, heads, n_tensor, place_ref, a_mine, a_got, b_mine, b_got, *refs):
    totals, refs = refs[:n_tensor], refs[n_tensor:]
    outs, smalls = refs[:5], refs[5:13]
    rows_scr, turned_scr, sems = refs[13:]
    copies = []

    def send(src, dst):
        copies.append(pltpu.make_async_copy(src, dst, sems.at[len(copies)]))
        copies[-1].start()

    half = rows_scr.shape[0] // 2
    join(place_ref, 0, a_mine, a_got, rows_scr.at[pl.ds(0, half), :])
    join(place_ref, 1, b_mine, b_got, rows_scr.at[pl.ds(half, half), :])
    send(rows_scr.at[pl.ds(4 * wide, wide), :], outs[4])
    for i in range(4):
        turned_scr[i] = rows_scr[i * wide : (i + 1) * wide, :].T
        send(turned_scr.at[i], outs[i])
    mine = totals[0]
    total = mine[...]
    for other in totals[1:]:
        total = total + other[...]
    for i in range(5):
        smalls[i][...] = total[i : i + 1, :]
    for k in range(2):
        for h in range(heads):
            smalls[5 + k][h : h + 1, :] = mine[5 + k : 6 + k, h * HEAD : (h + 1) * HEAD]
    width = mine.shape[1]
    for i in range(smalls[7].shape[1] // width):
        smalls[7][:, i * width : (i + 1) * width] = mine[7 + i : 8 + i, :]
    for copy in copies:
        copy.wait()


def finish_kernel(
    block, place_ref, x_ref, gain_ref, gh_e, gh_l, hid_es, hid_ek, hid_ls, hid_lk, mine_ref, other_ref, bias_ref, up_ref,
    down_ref, out_ref, grad_ref, up_out, down_out, out_scr, grad_scr, up_scr, down_scr, sems,
):
    core = place_ref[0]
    copies = []

    def send(src, dst):
        copies.append(pltpu.make_async_copy(src, dst, sems.at[len(copies)]))
        copies[-1].start()

    up_scr[...] = up_ref[...].astype(FL)
    send(up_scr, up_out)
    down_scr[...] = down_ref[...].astype(FL)
    send(down_scr, down_out)
    for first, gh_ref, hid_s, hid_k in ((0, gh_e, hid_es, hid_ek), (1, gh_l, hid_ls, hid_lk)):
        for part in range(2):
            at = slice(part * block, (part + 1) * block)
            spots = pl.ds((2 * first + part) * block, block)

            def summed(group):
                rows = slice(group * block, (group + 1) * block)
                return jnp.where(core == part, mine_ref[rows, :].astype(FL), other_ref[rows, :].astype(FL))

            hidden = jnp.where(core == part, hid_k[...], hid_s[...])
            out_scr[spots, :] = (hidden + summed(first + 2) + bias_ref[...]).astype(BF)
            send(out_scr.at[spots, :], out_ref.at[spots, :])
            unit, inv = norm_parts(x_ref[spots, :].astype(FL))
            grad_scr[spots, :] = (gh_ref[at, :] + norm_back(summed(first) * gain_ref[...], unit, inv)).astype(BF)
            send(grad_scr.at[spots, :], grad_ref.at[spots, :])
    for copy in copies:
        copy.wait()


def halve(place_ref, bit, total, keep_ref, send_ref):
    size = total.shape[0] // 2
    high = (place_ref[1] >> bit) & 1
    by_core(high, 0, keep_ref, send_ref, total[:size], slice(None))
    by_core(high, 1, keep_ref, send_ref, total[size:], slice(None))


def join(place_ref, bit, mine_ref, got_ref, out_ref):
    size = mine_ref.shape[0]
    high = ((place_ref[1] >> bit) & 1) == 1
    mine, got = mine_ref[...].astype(FL), got_ref[...].astype(FL)
    out_ref[:size, :] = jnp.where(high, got, mine).astype(out_ref.dtype)
    out_ref[size:, :] = jnp.where(high, mine, got).astype(out_ref.dtype)


SMEM = pl.BlockSpec(memory_space=pltpu.SMEM)
PLACE = object()
SPECS = {s: pl.BlockSpec(memory_space=s) for s in (pltpu.VMEM, pltpu.HBM)}


def call(kernel, outs, args, name, flops, scratch=(), space=pltpu.VMEM, after=(), far=0):
    placed = args[0] is PLACE
    args = args[1:] if placed else args
    count, extra = len(args), len(after)

    def body(*refs):
        place = [(lax.axis_index("tensor") & 1, lax.axis_index("dp"))] if placed else []
        kernel(*place, *refs[:count], *refs[count + extra :])

    specs = [SMEM if a.dtype == jnp.int32 else SPECS[space] for a in args]
    specs += [pl.BlockSpec(memory_space=pl.ANY)] * extra
    if space is pltpu.HBM:
        args = [a if a.dtype == jnp.int32 else pltpu.with_memory_space_constraint(a, space) for a in args]
    return pl.pallas_call(
        body,
        out_shape=[pltpu.HBM(s, d) if i < far else jax.ShapeDtypeStruct(s, d) for i, (s, d) in enumerate(outs)],
        in_specs=specs,
        out_specs=[SPECS[pltpu.HBM]] * far + [SPECS[pltpu.VMEM]] * (len(outs) - far),
        scratch_shapes=scratch,
        compiler_params=pltpu.CompilerParams(vmem_limit_bytes=VMEM_LIMIT),
        cost_estimate=pl.CostEstimate(flops=int(flops), bytes_accessed=1, transcendentals=0),
        name=name,
    )(*args, *after)


def swap(rows, axis, size, bit):
    return lax.ppermute(rows, axis, [(i, i ^ bit) for i in range(size)])


def work_kernel(jobs, place_ref, *refs):
    outs = list(refs)
    ins = [[outs.pop(0) for _ in range(count)] for _, _, count in jobs]
    for (kind, bit, _), (mine, got, *more) in zip(jobs, ins):
        if kind == "halve":
            halve(place_ref, bit, added(mine[...], got[...]), outs.pop(0), outs.pop(0))
        elif kind == "join":
            join(place_ref, bit, mine, got, outs.pop(0))
        elif kind == "sum":
            outs.pop(0)[...] = added(mine[...], got[...])
        elif kind == "copy":
            outs.pop(0)[...] = mine[...]
        elif kind == "pack":
            out = outs.pop(0)
            size = mine.shape[0]
            out[:size, :] = added(mine[...], got[...])
            out[size:, :] = added(more[0][...], more[1][...])
        elif kind == "three":
            total = mine[...].astype(FL) + got[...].astype(FL)
            size = outs[0].shape[0]
            for start, end in ((0, size), (size, size + small), (size + small, 2 * size + small)):
                out = outs.pop(0)
                out[...] = total[start:end].astype(out.dtype)
        else:
            total = mine[...].astype(FL) + got[...].astype(FL)
            size = outs[0].shape[0]
            for part in (total[:size], total[size:]):
                out = outs.pop(0)
                out[...] = part.astype(out.dtype)


def work(place, jobs, name, after=(), cost=1):
    outs = []
    for kind, _, mine, *others in jobs:
        size, width = mine.shape
        outs += {
            "halve": [((size // 2, width), BF)] * 2,
            "two": [((size // 2, width), BF)] * 2,
            "join": [((2 * size, width), BF)],
            "sum": [((size, width), BF)],
            "copy": [((size, width), mine.dtype)],
            "pack": [((size + others[-1].shape[0], width), BF)],
            "three": [(((size - small) // 2, width), BF), ((small, width), FL), (((size - small) // 2, width), BF)],
        }[kind]
    args = [a for job in jobs for a in job[2:]]
    return list(
        call(functools.partial(work_kernel, [(*job[:2], len(job) - 2) for job in jobs]), outs, (place, *args), name, cost, after=after)
    )


class Chain:
    def __init__(self, rows, send, bits, n_dp, end="sum"):
        self.rows, self.send, self.bits, self.n_dp, self.end, self.done = rows, send, bits, n_dp, end, 0
        self.start()

    def bit(self):
        return self.bits[min(self.done, 2 * len(self.bits) - 2 - self.done)]

    def start(self):
        self.got = swap(self.send, "dp", self.n_dp, 1 << self.bit())

    def left(self):
        return 2 * len(self.bits) - 2 - self.done

    def job(self):
        last = len(self.bits) - 1
        if self.done < last - 1:
            kind, bit = "halve", self.bits[self.done + 1]
        elif self.done <= last:
            kind, bit = (self.end if self.done == last else "sum"), 0
        else:
            kind, bit = "join", self.bit()
        return kind, bit, self.rows, self.got

    def take(self, results):
        kind = self.job()[0]
        self.rows = self.send = results.pop(0)
        if kind == "halve":
            self.send = results.pop(0)
        self.done += 1
        if self.left() >= 0:
            self.start()


def cores(rows, n_tensor):
    return swap(rows, "tensor", n_tensor, 1)


def other_chips(rows, n_tensor):
    return swap(rows, "tensor", n_tensor, 2)


def chips(rows, n_tensor):
    return rows, other_chips(rows, n_tensor)


def split_at(*parts):
    (items,) = (p for p in parts if not isinstance(p, int))
    places = [0, *(p for p in parts if isinstance(p, int)), len(items)]
    return [items[start:end] for start, end in zip(places, places[1:])]


def per_device(n_dp, n_tensor, *args):
    (inputs, memory, counts, attn_gain, attn_shift, w_query, w_key, w_value, w_pos, bias_u, bias_v, w_out,
     ffn_gain, ffn_shift, w_up, up_bias, w_down, down_bias, out_grad) = args
    _, seq_len, width = inputs.shape
    mem_len = memory.shape[1]
    total = mem_len + seq_len
    wide = w_query.shape[1]
    heads = wide // HEAD
    ff = w_up.shape[1]
    chunk = seq_len // 2
    block = chunk // 2
    late = chunk
    place = PLACE
    x, mem, g = inputs[0], memory[0], out_grad[0]
    row = lambda v: v.reshape(1, -1)

    freq = 1.0 / 10000.0 ** (np.arange(0, width, 2, dtype=np.float64) / width)
    key_phase = np.arange(total)[:, None] * freq[None, :]
    table = jnp.asarray(np.concatenate([np.cos(key_phase), np.sin(key_phase)], axis=1).astype(BF))
    row_phase = (np.arange(seq_len) + mem_len)[:, None] * freq[None, :]
    sin = jnp.asarray(np.sin(row_phase).astype(np.float32))
    cos = jnp.asarray(np.cos(row_phase).astype(np.float32))

    outs_of = [w_out, cores(w_out, n_tensor), swap(w_out, "tensor", n_tensor, 2)]

    def attend_outs(seen):
        return [((heads, chunk, wide + width), BF), ((chunk, wide), BF), ((heads, chunk, seen), BF), ((chunk, wide), BF)]

    ctx_scr = pltpu.VMEM((block, wide), FL)
    vectors = [row(v) for v in (attn_shift, attn_gain, ffn_gain, ffn_shift, up_bias, down_bias)]
    copied = [
        *[(a.shape, BF) for a in (x, g)], ((width, 3 * wide), BF), *[(a.shape, BF) for a in (w_pos, w_up, w_down, w_out)],
        *[(a.shape, FL) for a in (*vectors, sin, cos)], ((2, wide), FL),
    ]
    found = call(
        functools.partial(front_kernel, block, heads),
        [*copied, ((total, width), BF), ((total, wide + width), BF), ((total, wide), BF)],
        (place, x, mem, g, w_query, w_key, w_value, w_pos, w_up, w_down, w_out, *vectors, bias_u, bias_v, table, sin,
         cos), "front", 1,
        [pltpu.VMEM(mem.shape, BF)] + [pltpu.VMEM(bias_u.shape, FL)] * 2 + [pltpu.SemaphoreType.DMA((21,))], pltpu.HBM,
    )
    x, g, weights, w_pos, w_up, w_down, w_out = found[:7]
    attn_shift, attn_gain, ffn_gain, ffn_shift, up_bias, down_bias, sin, cos, biases, normed, keys, values = found[7:]

    def attend_chunk(first, name, cost, after):
        return call(
            functools.partial(attend_kernel, first, block, heads, mem_len),
            attend_outs(mem_len + first + chunk),
            (counts, normed, keys, values, weights, w_pos, biases, sin, cos), name, cost, [ctx_scr], after=after,
        )

    saved_l = attend_chunk(late, "attend_late", 1, ())
    ctx_l = [saved_l[-1], cores(saved_l[-1], n_tensor), swap(saved_l[-1], "tensor", n_tensor, 2)]
    saved_e = attend_chunk(0, "attend_early", 5e9, outs_of[1:])
    ctx_e = [saved_e[-1], cores(saved_e[-1], n_tensor), swap(saved_e[-1], "tensor", n_tensor, 2)]
    (relay,) = call(
        relay_kernel, [((chunk + width, wide), BF)], (ctx_l[2], outs_of[2]), "relay_late", 1, after=saved_e[-1:]
    )
    relay = cores(relay, n_tensor)
    ctx_l.append(relay)
    outs_of.append(relay)
    half_outs = [
        ((block, width), FL), ((block, width), BF), ((block, ff), BF), ((block, ff), BF), ((2, width), FL),
        ((block, width), BF),
    ]

    def ffn_rows(first, ctx, roles, name, after=()):
        found = call(
            functools.partial(ffn_rows_kernel, first, block, roles), half_outs * len(roles),
            (place, x, *ctx, *outs_of, ffn_gain, ffn_shift, w_up, up_bias, w_down, g), name, 1, after=after,
        )
        return [found[i : i + 6] for i in range(0, 6 * len(roles), 6)]

    sum_outs = [((width, ff), FL), ((ff, width), FL), ((3, width), FL), ((1, ff), FL)]
    (send_l,) = ffn_rows(late, ctx_l, ("send",), "ffn_send_late")
    gnt_l = cores(send_l[-1], n_tensor)
    (keep_l,) = ffn_rows(late, ctx_l, ("keep",), "ffn_keep_late", after=send_l[-1:])
    (relay,) = work(place, [("copy", 0, ctx_e[2], ctx_e[2])], "relay_early", keep_l[-1:], 5e9)
    ctx_e.append(cores(relay, n_tensor))
    (gnt_l,) = work(place, [("sum", 0, keep_l[-1], gnt_l)], "add_late", (relay,))
    gnt_l = chips(gnt_l, n_tensor)
    shares_l, sums_l = split_at(2, call(
        functools.partial(ffn_late_kernel, late),
        [((block, width), BF)] * 2 + sum_outs, (place, g, w_down, *send_l[1:5], *keep_l[1:5]), "ffn_late", 1,
        after=gnt_l[:1],
    ))
    send_e, keep_e = ffn_rows(0, ctx_e, ("send", "keep"), "ffn_rows_early", after=sums_l[3:4])
    gnt_e = cores(send_e[-1], n_tensor)
    shares_e, halves, vecs = split_at(2, call(
        functools.partial(ffn_early_kernel, 0),
        [((block, width), BF)] * 2 + [((width // 2, ff), BF)] * 2 + [((ff // 2, width), BF)] * 2
        + [((3, width), FL), ((1, ff), FL)],
        (place, g, w_down, *send_e[1:5], *keep_e[1:5], *sums_l), "ffn_early", 1,
    ), 6)
    up_keep, up_send, down_keep, down_send = halves
    up_got = swap(up_send, "dp", n_dp, 1)
    down_got = swap(down_send, "dp", n_dp, 2)
    (gnt_l,) = work(place, [("sum", 0, *gnt_l)], "add_late_chips", (up_keep,), 5e9)
    gnt_l = (gnt_l, cores(gnt_l, n_tensor))
    (gnt_e,) = work(place, [("sum", 0, keep_e[-1], gnt_e)], "add_early", gnt_l[:1])
    gnt_e = chips(gnt_e, n_tensor)
    hidden_l, hidden_e = (send_l[0], keep_l[0]), (send_e[0], keep_e[0])

    sums = [((wide, total), FL), ((wide, total), FL), ((wide, width), FL), ((wide, width), FL), ((chunk, wide), BF)]
    turn_scr = [ctx_scr, ctx_scr]

    def back_args(hidden, gnt, saved):
        qb, qv, probs, ctx = saved
        return (place, *hidden, *gnt, g, ffn_gain, w_out, ctx, probs, qb, qv, keys, values, w_pos, sin, cos, weights)

    gh_l, dk, dv, dpos, dout, dq, bias, part = call(
        functools.partial(back_late_kernel, late, block, heads, mem_len),
        [((chunk, width), FL), *sums, ((2, wide), FL), ((chunk, width), BF)],
        back_args(hidden_l, gnt_l, saved_l), "back_late", 1, turn_scr,
    )
    gnt_e, up_keep, up_send, down_keep, down_send = work(
        place, [("sum", 0, *gnt_e), ("halve", 1, up_keep, up_got), ("halve", 0, down_keep, down_got)], "add_middle", (bias,)
    )
    up_got = swap(up_send, "dp", n_dp, 2)
    down_got = swap(down_send, "dp", n_dp, 1)
    gnt_e = (gnt_e, cores(gnt_e, n_tensor))
    size = 5 * wide // 8
    gh_e, dk, dv, dpos, dout, dq_e, bias = call(
        functools.partial(back_early_kernel, 0, block, heads, mem_len),
        [((chunk, width), FL), *sums, ((2, wide), FL)],
        (*back_args(hidden_e, gnt_e, saved_e)[:-1], dk, dv, dpos, dout, bias), "back_early", 1, turn_scr,
    )
    pieces = [((2 * (size + small), width), BF)] * 2 + [((2 * size, width), BF)] * 2
    keep, send, a_keep, a_send, b_keep, b_send, f_rows = call(
        functools.partial(back_end_kernel, 0, block, heads, mem_len, n_tensor, size),
        [*[((seq_len, width), BF)] * 2, *pieces, ((chunk // 2, width), BF)],
        (place, weights, normed, attn_shift, attn_gain, dk, dv, dpos, dout, dq_e, bias, dq, part, *vecs, *shares_e,
         *shares_l, up_keep, up_got, down_keep, down_got), "back_end", 1,
    )

    def pair(rows, bit):
        return swap(rows, "dp", n_dp, 1 << bit)

    bits = list(range((n_dp - 1).bit_length()))
    a_got, b_got = pair(a_send, 0), pair(b_send, 1)
    if len(bits) > 3:
        f_rows, f_send = work(place, [("halve", 2, f_rows, jnp.zeros_like(f_rows))], "halve_ffn")
    else:
        f_send = f_rows
    ffn = Chain(f_rows, f_send, bits[2:], n_dp, "two" if len(bits) == 3 else "sum")
    rows = (keep, cores(send, n_tensor))
    a_keep, a_send, b_keep, b_send, rows = work(
        place, [("halve", 1, a_keep, a_got), ("halve", 0, b_keep, b_got), ("sum", 0, *rows)], "step_0"
    )
    rows = (rows, other_chips(rows, n_tensor))
    while ffn.left() > 0:
        ffn.take(work(place, [ffn.job()], "step_ffn"))
    attn, *halves = work(
        place, [("pack", 0, a_keep, pair(a_send, 1), b_keep, pair(b_send, 0)), ffn.job()], "step_1"
    )
    up, down = halves if len(halves) == 2 else (halves[0][: chunk // 4], halves[0][chunk // 4 :])
    for bit in bits[2:-1]:
        (attn,) = work(place, [("sum", 0, attn, pair(attn, bit))], f"step_1_{bit}")
    a_rows, totals, b_rows, up, down = work(
        place,
        [("three", 0, attn, pair(attn, bits[-1])), ("join", 1, up, pair(up, 1)), ("join", 0, down, pair(down, 0))],
        "step_2", cost=STEP_COST,
    )
    a_rows, b_rows, up, down, totals, summed = work(
        place,
        [("join", 1, a_rows, pair(a_rows, 1)), ("join", 0, b_rows, pair(b_rows, 0)), ("join", 0, up, pair(up, 0)),
         ("join", 1, down, pair(down, 1)), ("copy", 0, totals, totals), ("sum", 0, *rows)],
        "step_3",
    )
    rows = (summed, cores(summed, n_tensor))
    totals = [totals] + [swap(totals, "tensor", n_tensor, k) for k in range(1, n_tensor)]
    output, input_grad, g_up, g_down = call(
        functools.partial(finish_kernel, block), [(x.shape, BF)] * 2 + [((width, ff), FL), ((ff, width), FL)],
        (place, x, attn_gain, gh_e, gh_l, *hidden_e, *hidden_l, *rows, down_bias, up, down), "finish", 1,
        [pltpu.VMEM(x.shape, BF)] * 2 + [pltpu.VMEM((width, ff), FL), pltpu.VMEM((ff, width), FL),
                                         pltpu.SemaphoreType.DMA((10,))],
        after=(a_rows,), far=4,
    )
    output_there = pltpu.with_memory_space_constraint(output, pltpu.HBM)
    g_query, g_key, g_value, g_pos, g_out, *vecs = call(
        functools.partial(last_kernel, wide, heads, n_tensor),
        [((width, wide), FL)] * 4 + [((wide, width), FL)]
        + [((1, width), FL)] * 5 + [((heads, HEAD), FL)] * 2 + [((1, ff), FL)],
        (place, a_rows, pair(a_rows, 0), b_rows, pair(b_rows, 1), *totals), "last", 1,
        [pltpu.VMEM((5 * wide, width), FL), pltpu.VMEM((4, width, wide), FL), pltpu.SemaphoreType.DMA((5,))],
        after=(output_there,), far=5,
    )
    return (
        output[None],
        input_grad[None],
        vecs[0].reshape(-1),
        vecs[1].reshape(-1),
        g_query,
        g_key,
        g_value,
        g_pos,
        vecs[5],
        vecs[6],
        g_out,
        vecs[2].reshape(-1),
        vecs[3].reshape(-1),
        g_up,
        vecs[7].reshape(-1),
        g_down,
        vecs[4].reshape(-1),
    )


def solution(mesh):
    split, whole = P(None, "tensor"), P()
    return jax.shard_map(
        functools.partial(per_device, mesh.shape["dp"], mesh.shape["tensor"]),
        mesh=mesh,
        in_specs=(
            P("dp", None, None), P("dp", None, None), P("dp"), whole, whole, split, split, split, split,
            P("tensor", None), P("tensor", None), P("tensor", None), whole, whole, split, P("tensor"),
            P("tensor", None), whole, P("dp", None, None),
        ),
        out_specs=(
            P("dp", None, None), P("dp", None, None), whole, whole, split, split, split, split,
            P("tensor", None), P("tensor", None), P("tensor", None), whole, whole, split, P("tensor"),
            P("tensor", None), whole,
        ),
        check_vma=False,
    )
```

```python
import functools

import jax
import jax.numpy as jnp
import numpy as np
from jax import lax
from jax.experimental import pallas as pl
from jax.experimental.pallas import tpu as pltpu
from jax.sharding import PartitionSpec as P

HEAD = 64
BF = jnp.bfloat16
FL = jnp.float32
eps_norm = 1e-05
neg_fill = -1e30
VMEM_LIMIT = 24 * 1024 * 1024
small = 16
UNROLL = [2, 2, 2]
STEP_COST = 5e9


def mm(left, right):
    return lax.dot_general(left, right, (((1,), (0,)), ((), ())), preferred_element_type=FL)


def mm_t(left, right):
    return lax.dot_general(left, right, (((1,), (1,)), ((), ())), preferred_element_type=FL)


def t_mm(left, right):
    return lax.dot_general(left, right, (((0,), (0,)), ((), ())), preferred_element_type=FL)


def norm_parts(rows):
    center = rows - jnp.mean(rows, axis=-1, keepdims=True)
    spread = jnp.mean(center * center, axis=-1, keepdims=True)
    inv = lax.rsqrt(spread + eps_norm)
    return center * inv, inv


def norm_back(scaled, unit, inv):
    flat = jnp.mean(scaled, axis=-1, keepdims=True)
    along = jnp.mean(scaled * unit, axis=-1, keepdims=True)
    return inv * (scaled - flat - unit * along)


def head_lanes(wide, h):
    lane = lax.broadcasted_iota(jnp.int32, (1, wide), 1)
    return (lane >= h * HEAD) & (lane < (h + 1) * HEAD)


def col_sum(rows):
    return jnp.sum(rows, axis=0, keepdims=True)


def fine_mm(left, right, product):
    high = left.astype(BF)
    low = (left - high.astype(FL)).astype(BF)
    return product(high, right) + product(low, right)


def norm_sums(weighted, shift_sum, gain, shift):
    return (weighted - shift * shift_sum) / gain, shift_sum


def loop(count, body, unroll=1):
    def step(i, carry):
        body(i)
        return carry

    lax.fori_loop(0, count, step, 0, unroll=unroll)


def rows_of(i, size):
    return pl.ds(pl.multiple_of(i * size, size), size)


def by_core(core, part, keep_ref, send_ref, rows, at):
    @pl.when(core == part)
    def _():
        keep_ref[at, :] = rows

    @pl.when(core != part)
    def _():
        send_ref[at, :] = rows


def added(left, right):
    return (left.astype(FL) + right.astype(FL)).astype(BF)


def make_queries(normed, spots, at, refs, heads):
    w_ref, wpos_ref, bu, bv, sin_ref, cos_ref, qb_ref, qv_ref = refs
    wide = heads * HEAD
    scale = HEAD ** (-0.5)
    query = mm(normed, w_ref[:, :wide]).astype(BF).astype(FL)
    query_u = (query + bu).astype(BF).astype(FL) * scale
    query_v = (query + bv).astype(BF).astype(FL) * scale
    qv_ref[at, :] = query_v.astype(BF)
    sin = sin_ref[spots, :]
    cos = cos_ref[spots, :]
    half = sin.shape[1]
    for h in range(heads):
        lanes = head_lanes(wide, h)
        qb_ref[h, at, :wide] = jnp.where(lanes, query_u, 0.0).astype(BF)
        coef = mm_t(jnp.where(lanes, query_v, 0.0).astype(BF), wpos_ref[...])
        on_sin, on_cos = coef[:, :half], coef[:, half:]
        qb_ref[h, at, wide : wide + half] = (on_sin * sin + on_cos * cos).astype(BF)
        qb_ref[h, at, wide + half :] = (on_cos * sin - on_sin * cos).astype(BF)


def attend(first, block, mem_len, heads, count, qb_ref, kt_ref, v_ref, probs_ref, ctx_ref, ctx_scr):
    wide = heads * HEAD
    rows = qb_ref.shape[1]
    for part in range(rows // block):
        at = slice(part * block, (part + 1) * block)
        start = first + part * block
        seen = mem_len + start + block

        def one_head(h):
            scores = mm_t(qb_ref[h, at, :], kt_ref[:seen, :])
            query_pos = start + lax.broadcasted_iota(jnp.int32, (block, 1), 0)
            limit = jnp.minimum(query_pos, count - 1)
            key_pos = lax.broadcasted_iota(jnp.int32, (block, seen - mem_len), 1)
            scores = jnp.concatenate(
                [scores[:, :mem_len], jnp.where(key_pos <= limit, scores[:, mem_len:], neg_fill)], axis=1
            )
            expo = jnp.exp(scores - jnp.max(scores, axis=-1, keepdims=True))
            probs = (expo * (1.0 / jnp.sum(expo, axis=-1, keepdims=True))).astype(BF)
            probs_ref[h, at, :seen] = probs
            found = mm(probs, v_ref[:seen, :])
            ctx_scr[...] = jnp.where(head_lanes(wide, h), found, ctx_scr[...])

        loop(heads, one_head, UNROLL[2])
        ctx_ref[at, :] = ctx_scr[...].astype(BF)


def front_kernel(
    block, heads,
    place_ref, x_in, mem_in, g_in, wq_in, wk_in, wv_in, wpos_in, wup_in, wdown_in, wout_in,
    shift_in, gain_in, fgain_in, fshift_in, upb_in, downb_in, bu_in, bv_in, table_in, sin_in, cos_in,
    x_ref, g_ref, w_ref, wpos_ref, wup_ref, wdown_ref, wout_ref, shift_ref, gain_ref, fgain_ref, fshift_ref, upb_ref,
    downb_ref, sin_ref, cos_ref, bias_ref, normed_ref, kt_ref, v_ref,
    mem_ref, bu_ref, bv_ref, sems,
):
    wide = heads * HEAD
    mem_len = mem_in.shape[0]
    seq_len = x_in.shape[0]
    todo = [
        (mem_in, mem_ref), (gain_in, gain_ref), (shift_in, shift_ref), (wk_in, w_ref.at[:, wide : 2 * wide]),
        (wv_in, w_ref.at[:, 2 * wide :]), (x_in, x_ref), (wq_in, w_ref.at[:, :wide]), (bu_in, bu_ref), (bv_in, bv_ref),
        (wpos_in, wpos_ref), (sin_in, sin_ref), (cos_in, cos_ref), (table_in, kt_ref.at[:, wide:]),
        (wout_in, wout_ref), (wup_in, wup_ref), (wdown_in, wdown_ref), (g_in, g_ref), (fgain_in, fgain_ref),
        (fshift_in, fshift_ref), (upb_in, upb_ref), (downb_in, downb_ref),
    ]
    copies = [pltpu.make_async_copy(src, dst, sems.at[i]) for i, (src, dst) in enumerate(todo)]
    for copy in copies:
        copy.start()
    for copy in copies[:5]:
        copy.wait()

    def project(rows_ref, at, to):
        unit, _ = norm_parts(rows_ref[at, :].astype(FL))
        normed = (unit * gain_ref[...] + shift_ref[...]).astype(BF)
        normed_ref[to, :] = normed
        pair = mm(normed, w_ref[:, wide:]).astype(BF)
        kt_ref[to, :wide] = pair[:, :wide]
        v_ref[to, :] = pair[:, wide:]

    def some_memory(i):
        project(mem_ref, rows_of(i, block), rows_of(i, block))

    def some_rows(i):
        project(x_ref, rows_of(i, block), rows_of(i + mem_len // block, block))

    loop(mem_len // block, some_memory, UNROLL[0])
    for copy in copies[5:7]:
        copy.wait()
    loop(seq_len // block, some_rows, UNROLL[0])
    for copy in copies[7:]:
        copy.wait()
    bias_ref[0:1, :] = jnp.concatenate([bu_ref[h : h + 1, :] for h in range(heads)], axis=1)
    bias_ref[1:2, :] = jnp.concatenate([bv_ref[h : h + 1, :] for h in range(heads)], axis=1)


def attend_kernel(
    first, block, heads, mem_len,
    count_ref, normed_ref, kt_ref, v_ref, w_ref, wpos_ref, bias_ref, sin_ref, cos_ref,
    qb_ref, qv_ref, probs_ref, ctx_ref, ctx_scr,
):
    def some_queries(i):
        at = rows_of(i, block)
        spots = rows_of(i + first // block, block)
        make_queries(
            normed_ref[rows_of(i + (mem_len + first) // block, block), :], spots, at,
            (w_ref, wpos_ref, bias_ref[0:1, :], bias_ref[1:2, :], sin_ref, cos_ref, qb_ref, qv_ref), heads,
        )

    loop(qb_ref.shape[1] // block, some_queries, UNROLL[1])
    attend(first, block, mem_len, heads, count_ref[0], qb_ref, kt_ref, v_ref, probs_ref, ctx_ref, ctx_scr)


def relay_kernel(ctx_ref, w_ref, out_ref):
    size, wide = ctx_ref.shape
    out_ref[:size, :] = ctx_ref[...]
    for k in range(w_ref.shape[1] // wide):
        at = size + k * w_ref.shape[0]
        out_ref[at : at + w_ref.shape[0], :] = w_ref[:, k * wide : (k + 1) * wide]


def ffn_rows_kernel(
    first, block, roles,
    place_ref, x_ref, c0_ref, c1_ref, c2_ref, c3_ref, o0_ref, o1_ref, o2_ref, o3_ref, gain_ref, shift_ref, up_ref,
    upb_ref, down_ref, g_ref, *refs,
):
    core = place_ref[0]
    wide = c0_ref.shape[1]
    size = c0_ref.shape[0]
    blocks = [o3_ref[at : at + wide, :] for at in range(o3_ref.shape[0] - size, o3_ref.shape[0], wide)]
    o3 = jnp.concatenate(blocks, axis=1)
    for role, hidden_ref, normed_ref, activ_ref, gpre_ref, vec_ref, share_ref in zip(roles, *[iter(refs)] * 6):
        half = core if role == "keep" else 1 - core
        at = rows_of(half, block)
        spots = rows_of(half + first // block, block)
        attended = mm(c0_ref[at, :], o0_ref[...]) + mm(c1_ref[at, :], o1_ref[...])
        attended = attended + (mm(c2_ref[at, :], o2_ref[...]) + mm(c3_ref[at, :], o3))
        hidden = x_ref[spots, :].astype(FL) + attended
        hidden_ref[...] = hidden
        unit, _ = norm_parts(hidden)
        normed = (unit * gain_ref[...] + shift_ref[...]).astype(BF)
        normed_ref[...] = normed
        pre = mm(normed, up_ref[...]) + upb_ref[...]
        cdf = 0.5 + 0.5 * lax.erf(pre * np.float32(0.5**0.5))
        activ_ref[...] = (pre * cdf).astype(BF)
        slope = cdf + pre * jnp.exp(-0.5 * pre * pre) * np.float32((2 * np.pi) ** -0.5)
        grad_pre = (mm_t(g_ref[spots, :], down_ref[...]) * slope).astype(BF)
        gpre_ref[...] = grad_pre
        back = mm_t(grad_pre, up_ref[...])
        share_ref[...] = back.astype(BF)
        vec_ref[0:1, :] = col_sum(back * unit)
        vec_ref[1:2, :] = col_sum(back)


def ffn_weights(first, place_ref, g_ref, down_ref, saved, shares):
    core = place_ref[0]
    block = shares[0].shape[0]
    total = None
    for role, (normed_ref, activ_ref, gpre_ref, vec_ref), share_ref in zip(("send", "keep"), saved, shares):
        half = core if role == "keep" else 1 - core
        grads = g_ref[rows_of(half + first // block, block), :]
        activ = activ_ref[...]
        share_ref[...] = mm(activ, down_ref[...]).astype(BF)
        vecs = jnp.concatenate([vec_ref[...], col_sum(grads.astype(FL))], axis=0)
        new = [t_mm(normed_ref[...], gpre_ref[...]), t_mm(activ, grads), vecs, col_sum(gpre_ref[...].astype(FL))]
        total = new if total is None else [old + part for old, part in zip(total, new)]
    return total


def ffn_late_kernel(first, place_ref, g_ref, down_ref, *refs):
    found = ffn_weights(first, place_ref, g_ref, down_ref, (refs[:4], refs[4:8]), refs[8:10])
    for ref, value in zip(refs[10:], found):
        ref[...] = value


def ffn_early_kernel(first, place_ref, g_ref, down_ref, *refs):
    found = ffn_weights(first, place_ref, g_ref, down_ref, (refs[:4], refs[4:8]), refs[12:14])
    up, down, vec, upb = (value + old[...] for value, old in zip(found, refs[8:12]))
    up_keep, up_send, down_keep, down_send, vec_ref, upb_out = refs[14:]
    halve(place_ref, 0, up.astype(BF), up_keep, up_send)
    halve(place_ref, 1, down.astype(BF), down_keep, down_send)
    vec_ref[...] = vec
    upb_out[...] = upb


def back_rows(
    first, block, heads, mem_len, place_ref, hid_s, hid_k, mine_ref, other_ref, g_ref, fgain_ref, wout_ref, ctx_ref,
    probs_ref, qb_ref, qv_ref, kt_ref, v_ref, wpos_ref, sin_ref, cos_ref,
    gh_ref, dk_ref, dv_ref, dpos_ref, dout_ref, dq_ref, bias_ref, grad_u, grad_v,
):
    core = place_ref[0]
    wide = heads * HEAD
    half = sin_ref.shape[1]
    scale = HEAD ** (-0.5)
    for part in range(2):
        at = slice(part * block, (part + 1) * block)
        spots = slice(first + part * block, first + (part + 1) * block)
        seen = mem_len + first + (part + 1) * block
        unit, inv = norm_parts(jnp.where(core == part, hid_k[...], hid_s[...]))
        summed = jnp.where(core == part, mine_ref[...].astype(FL), other_ref[...].astype(FL))
        grad_hidden = g_ref[spots, :].astype(FL) + norm_back(summed * fgain_ref[...], unit, inv)
        gh_ref[at, :] = grad_hidden
        gh = grad_hidden.astype(BF)
        context = ctx_ref[at, :]
        grad_context = mm_t(gh, wout_ref[...]).astype(BF).astype(FL)
        dout_ref[...] += t_mm(context, gh)
        along_context = grad_context * context.astype(FL)

        def one_head(h):
            lanes = head_lanes(wide, h)
            delta = jnp.sum(jnp.where(lanes, along_context, 0.0), axis=-1, keepdims=True)
            own = jnp.where(lanes, grad_context, 0.0).astype(BF)
            probs = probs_ref[h, at, :seen]
            grad_score = (probs.astype(FL) * (mm_t(own, v_ref[:seen, :]) - delta)).astype(BF)
            dv_ref[:, :seen] += t_mm(own, probs)
            dk_ref[:, :seen] += t_mm(qb_ref[h, at, :wide], grad_score)
            spread = mm(grad_score, kt_ref[:seen, :])
            grad_u[...] = jnp.where(lanes, spread[:, :wide], grad_u[...])
            sin = sin_ref[spots, :]
            cos = cos_ref[spots, :]
            on_cos, on_sin = spread[:, wide : wide + half], spread[:, wide + half :]
            turned = jnp.concatenate(
                [(on_cos * sin - on_sin * cos).astype(BF), (on_cos * cos + on_sin * sin).astype(BF)], axis=1
            )
            grad_v[...] = jnp.where(lanes, mm(turned, wpos_ref[...]), grad_v[...])
            query_v = jnp.where(lanes, qv_ref[at, :].astype(FL), 0.0).astype(BF)
            dpos_ref[...] += t_mm(query_v, turned)

        loop(heads, one_head, 2)
        bias_ref[0:1, :] += col_sum(grad_u[...]) * scale
        bias_ref[1:2, :] += col_sum(grad_v[...]) * scale
        dq_ref[at, :] = ((grad_u[...] + grad_v[...]) * scale).astype(BF)


def back_share(cols, dq_rows, dk_ref, dv_ref, weights):
    pair = [dk_ref[:, cols].T.astype(BF), dv_ref[:, cols].T.astype(BF)]
    return mm_t(jnp.concatenate([dq_rows, *pair], axis=1), weights).astype(BF)


def back_late_kernel(
    first, block, heads, mem_len,
    place_ref, hid_s, hid_k, mine_ref, other_ref, g_ref, fgain_ref, wout_ref, ctx_ref, probs_ref, qb_ref, qv_ref, kt_ref,
    v_ref, wpos_ref, sin_ref, cos_ref, w_ref,
    gh_ref, dk_ref, dv_ref, dpos_ref, dout_ref, dq_ref, bias_ref, share_ref, grad_u, grad_v,
):
    for ref in (dk_ref, dv_ref, dpos_ref, dout_ref, bias_ref):
        ref[...] = jnp.zeros(ref.shape, FL)
    back_rows(
        first, block, heads, mem_len, place_ref, hid_s, hid_k, mine_ref, other_ref, g_ref, fgain_ref, wout_ref, ctx_ref,
        probs_ref, qb_ref, qv_ref, kt_ref, v_ref, wpos_ref, sin_ref, cos_ref,
        gh_ref, dk_ref, dv_ref, dpos_ref, dout_ref, dq_ref, bias_ref, grad_u, grad_v,
    )
    for part in range(2):
        at = slice(part * block, (part + 1) * block)
        cols = slice(mem_len + first + part * block, mem_len + first + (part + 1) * block)
        share_ref[at, :] = back_share(cols, dq_ref[at, :], dk_ref, dv_ref, w_ref[...])


def back_early_kernel(
    first, block, heads, mem_len,
    place_ref, hid_s, hid_k, mine_ref, other_ref, g_ref, fgain_ref, wout_ref, ctx_ref, probs_ref, qb_ref, qv_ref, kt_ref,
    v_ref, wpos_ref, sin_ref, cos_ref, dk_in, dv_in, dpos_in, dout_in, bias_in,
    gh_ref, dk_ref, dv_ref, dpos_ref, dout_ref, dq_ref, bias_ref, grad_u, grad_v,
):
    for ref, old in ((dk_ref, dk_in), (dv_ref, dv_in), (dpos_ref, dpos_in), (dout_ref, dout_in), (bias_ref, bias_in)):
        ref[...] = old[...]
    back_rows(
        first, block, heads, mem_len, place_ref, hid_s, hid_k, mine_ref, other_ref, g_ref, fgain_ref, wout_ref, ctx_ref,
        probs_ref, qb_ref, qv_ref, kt_ref, v_ref, wpos_ref, sin_ref, cos_ref,
        gh_ref, dk_ref, dv_ref, dpos_ref, dout_ref, dq_ref, bias_ref, grad_u, grad_v,
    )


def back_end_kernel(
    first, block, heads, mem_len, n_tensor, size,
    place_ref, w_ref, normed_ref, shift_ref, gain_ref, dk_ref, dv_ref, dpos_ref, dout_ref, dq_ref, bias_ref, dq_in,
    late_ref, fvec_ref, upb_ref, e_send, e_keep, l_send, l_keep, up_keep, up_got, down_keep, down_got,
    keep_ref, send_ref, a_keep, a_send, b_keep, b_send, f_ref,
):
    half = up_keep.shape[0]
    f_ref[:half, :] = added(up_keep[...], up_got[...])
    f_ref[half:, :] = added(down_keep[...], down_got[...])
    wide = heads * HEAD
    core = place_ref[0]
    for part in range(2):
        at = slice(part * block, (part + 1) * block)
        by_core(core, part, keep_ref, send_ref, late_ref[at, :], slice(block, 2 * block))
    keep_ref[2 * block : 3 * block, :] = e_keep[...]
    keep_ref[3 * block :, :] = l_keep[...]
    send_ref[2 * block : 3 * block, :] = e_send[...]
    send_ref[3 * block :, :] = l_send[...]
    normed = normed_ref[...]
    width = normed.shape[1]
    dq_all = jnp.concatenate([dq_ref[...], dq_in[...]], axis=0)
    dk, dv = dk_ref[...].astype(BF), dv_ref[...].astype(BF)
    grads = [t_mm(dq_all, normed[mem_len:]), mm(dk, normed), mm(dv, normed), dpos_ref[...], dout_ref[...]]
    grads = jnp.concatenate(grads, axis=0)
    turned = w_ref[...].astype(FL).T
    shift_sum = fine_mm(col_sum(dq_all.astype(FL)), turned[:wide].astype(BF), mm)
    for i, part in enumerate((dk, dv)):
        shift_sum += col_sum(turned[(i + 1) * wide : (i + 2) * wide] * jnp.sum(part.astype(FL), axis=1, keepdims=True))
    sums = norm_sums(col_sum(turned * grads[: 3 * wide]), shift_sum, gain_ref[...], shift_ref[...])
    for part in range(2):
        at = slice(part * block, (part + 1) * block)
        cols = slice(mem_len + first + part * block, mem_len + first + (part + 1) * block)
        back = back_share(cols, dq_ref[at, :], dk_ref, dv_ref, w_ref[...])
        by_core(core, part, keep_ref, send_ref, back, slice(0, block))
    wider = jnp.zeros((1, width - wide), FL)
    rows = [*sums, fvec_ref[0:2, :], fvec_ref[2:3, :] * (1.0 / n_tensor)]
    rows += [jnp.concatenate([bias_ref[i : i + 1, :], wider], axis=1) for i in range(2)]
    for i in range(upb_ref.shape[1] // width):
        rows.append(upb_ref[:, i * width : (i + 1) * width])
    rows.append(jnp.zeros((small - 7 - upb_ref.shape[1] // width, width), FL))
    rows = jnp.concatenate(rows, axis=0).astype(BF)
    for d in range(4):
        piece = jnp.concatenate([grads[d * size : (d + 1) * size].astype(BF), rows], axis=0)
        at = slice(d % 2 * (size + small), (d % 2 + 1) * (size + small))
        by_core(place_ref[1] & 1, d // 2, a_keep, a_send, piece, at)
        piece = grads[(d + 4) * size : (d + 5) * size].astype(BF)
        by_core((place_ref[1] >> 1) & 1, d // 2, b_keep, b_send, piece, slice(d % 2 * size, (d % 2 + 1) * size))


def last_kernel(wide, heads, place_ref, a_mine, a_got, b_mine, b_got, mine, chip_ref, other_ref, *refs):
    outs, smalls = refs[:5], refs[5:13]
    rows_scr, turned_scr, sems = refs[13:]
    copies = []

    def send(src, dst):
        copies.append(pltpu.make_async_copy(src, dst, sems.at[len(copies)]))
        copies[-1].start()

    half = rows_scr.shape[0] // 2
    join(place_ref, 0, a_mine, a_got, rows_scr.at[pl.ds(0, half), :])
    join(place_ref, 1, b_mine, b_got, rows_scr.at[pl.ds(half, half), :])
    send(rows_scr.at[pl.ds(4 * wide, wide), :], outs[4])
    for i in range(4):
        turned_scr[i] = rows_scr[i * wide : (i + 1) * wide, :].T
        send(turned_scr.at[i], outs[i])
    total = chip_ref[...] + other_ref[...]
    for i in range(5):
        smalls[i][...] = total[i : i + 1, :]
    for k in range(2):
        for h in range(heads):
            smalls[5 + k][h : h + 1, :] = mine[5 + k : 6 + k, h * HEAD : (h + 1) * HEAD]
    width = mine.shape[1]
    for i in range(smalls[7].shape[1] // width):
        smalls[7][:, i * width : (i + 1) * width] = mine[7 + i : 8 + i, :]
    for copy in copies:
        copy.wait()


def finish_kernel(
    block, place_ref, x_ref, gain_ref, gh_e, gh_l, hid_es, hid_ek, hid_ls, hid_lk, mine_ref, other_ref, bias_ref, up_ref,
    down_ref, out_ref, grad_ref, up_out, down_out, out_scr, grad_scr, up_scr, down_scr, sems,
):
    core = place_ref[0]
    copies = []

    def send(src, dst):
        copies.append(pltpu.make_async_copy(src, dst, sems.at[len(copies)]))
        copies[-1].start()

    up_scr[...] = up_ref[...].astype(FL)
    send(up_scr, up_out)
    down_scr[...] = down_ref[...].astype(FL)
    send(down_scr, down_out)
    for first, gh_ref, hid_s, hid_k in ((0, gh_e, hid_es, hid_ek), (1, gh_l, hid_ls, hid_lk)):
        for part in range(2):
            at = slice(part * block, (part + 1) * block)
            spots = pl.ds((2 * first + part) * block, block)

            def summed(group):
                rows = slice(group * block, (group + 1) * block)
                return jnp.where(core == part, mine_ref[rows, :].astype(FL), other_ref[rows, :].astype(FL))

            hidden = jnp.where(core == part, hid_k[...], hid_s[...])
            out_scr[spots, :] = (hidden + summed(first + 2) + bias_ref[...]).astype(BF)
            send(out_scr.at[spots, :], out_ref.at[spots, :])
            unit, inv = norm_parts(x_ref[spots, :].astype(FL))
            grad_scr[spots, :] = (gh_ref[at, :] + norm_back(summed(first) * gain_ref[...], unit, inv)).astype(BF)
            send(grad_scr.at[spots, :], grad_ref.at[spots, :])
    for copy in copies:
        copy.wait()


def halve(place_ref, bit, total, keep_ref, send_ref):
    size = total.shape[0] // 2
    high = (place_ref[1] >> bit) & 1
    by_core(high, 0, keep_ref, send_ref, total[:size], slice(None))
    by_core(high, 1, keep_ref, send_ref, total[size:], slice(None))


def join(place_ref, bit, mine_ref, got_ref, out_ref):
    size = mine_ref.shape[0]
    high = ((place_ref[1] >> bit) & 1) == 1
    mine, got = mine_ref[...].astype(FL), got_ref[...].astype(FL)
    out_ref[:size, :] = jnp.where(high, got, mine).astype(out_ref.dtype)
    out_ref[size:, :] = jnp.where(high, mine, got).astype(out_ref.dtype)


SMEM = pl.BlockSpec(memory_space=pltpu.SMEM)
PLACE = object()
SPECS = {s: pl.BlockSpec(memory_space=s) for s in (pltpu.VMEM, pltpu.HBM)}


def call(kernel, outs, args, name, flops, scratch=(), space=pltpu.VMEM, after=(), far=0):
    placed = args[0] is PLACE
    args = args[1:] if placed else args
    count, extra = len(args), len(after)

    def body(*refs):
        place = [(lax.axis_index("tensor") & 1, lax.axis_index("dp"))] if placed else []
        kernel(*place, *refs[:count], *refs[count + extra :])

    specs = [SMEM if a.dtype == jnp.int32 else SPECS[space] for a in args]
    specs += [pl.BlockSpec(memory_space=pl.ANY)] * extra
    if space is pltpu.HBM:
        args = [a if a.dtype == jnp.int32 else pltpu.with_memory_space_constraint(a, space) for a in args]
    return pl.pallas_call(
        body,
        out_shape=[pltpu.HBM(s, d) if i < far else jax.ShapeDtypeStruct(s, d) for i, (s, d) in enumerate(outs)],
        in_specs=specs,
        out_specs=[SPECS[pltpu.HBM]] * far + [SPECS[pltpu.VMEM]] * (len(outs) - far),
        scratch_shapes=scratch,
        compiler_params=pltpu.CompilerParams(vmem_limit_bytes=VMEM_LIMIT),
        cost_estimate=pl.CostEstimate(flops=int(flops), bytes_accessed=1, transcendentals=0),
        name=name,
    )(*args, *after)


def swap(rows, axis, size, bit):
    return lax.ppermute(rows, axis, [(i, i ^ bit) for i in range(size)])


def work_kernel(jobs, place_ref, *refs):
    outs = list(refs)
    ins = [[outs.pop(0) for _ in range(count)] for _, _, count in jobs]
    for (kind, bit, _), (mine, got, *more) in zip(jobs, ins):
        if kind == "halve":
            halve(place_ref, bit, added(mine[...], got[...]), outs.pop(0), outs.pop(0))
        elif kind == "join":
            join(place_ref, bit, mine, got, outs.pop(0))
        elif kind == "sum":
            outs.pop(0)[...] = added(mine[...], got[...])
        elif kind == "copy":
            outs.pop(0)[...] = mine[...]
        elif kind == "plus":
            total = mine[...] + got[...]
            for other in more:
                total = total + other[...]
            outs.pop(0)[...] = total
        elif kind == "pack":
            out = outs.pop(0)
            size = mine.shape[0]
            out[:size, :] = added(mine[...], got[...])
            out[size:, :] = added(more[0][...], more[1][...])
        elif kind == "three":
            total = mine[...].astype(FL) + got[...].astype(FL)
            size = outs[0].shape[0]
            for start, end in ((0, size), (size, size + small), (size + small, 2 * size + small)):
                out = outs.pop(0)
                out[...] = total[start:end].astype(out.dtype)
        else:
            total = mine[...].astype(FL) + got[...].astype(FL)
            size = outs[0].shape[0]
            for part in (total[:size], total[size:]):
                out = outs.pop(0)
                out[...] = part.astype(out.dtype)


def work(place, jobs, name, after=(), cost=1):
    outs = []
    for kind, _, mine, *others in jobs:
        size, width = mine.shape
        outs += {
            "halve": [((size // 2, width), BF)] * 2,
            "two": [((size // 2, width), BF)] * 2,
            "join": [((2 * size, width), BF)],
            "sum": [((size, width), BF)],
            "copy": [((size, width), mine.dtype)],
            "plus": [((size, width), FL)],
            "pack": [((size + others[-1].shape[0], width), BF)],
            "three": [(((size - small) // 2, width), BF), ((small, width), FL), (((size - small) // 2, width), BF)],
        }[kind]
    args = [a for job in jobs for a in job[2:]]
    return list(
        call(functools.partial(work_kernel, [(*job[:2], len(job) - 2) for job in jobs]), outs, (place, *args), name, cost, after=after)
    )


class Chain:
    def __init__(self, rows, send, bits, n_dp, end="sum"):
        self.rows, self.send, self.bits, self.n_dp, self.end, self.done = rows, send, bits, n_dp, end, 0
        self.start()

    def bit(self):
        return self.bits[min(self.done, 2 * len(self.bits) - 2 - self.done)]

    def start(self):
        self.got = swap(self.send, "dp", self.n_dp, 1 << self.bit())

    def left(self):
        return 2 * len(self.bits) - 2 - self.done

    def job(self):
        last = len(self.bits) - 1
        if self.done < last - 1:
            kind, bit = "halve", self.bits[self.done + 1]
        elif self.done <= last:
            kind, bit = (self.end if self.done == last else "sum"), 0
        else:
            kind, bit = "join", self.bit()
        return kind, bit, self.rows, self.got

    def take(self, results):
        kind = self.job()[0]
        self.rows = self.send = results.pop(0)
        if kind == "halve":
            self.send = results.pop(0)
        self.done += 1
        if self.left() >= 0:
            self.start()


def cores(rows, n_tensor):
    return swap(rows, "tensor", n_tensor, 1)


def other_chips(rows, n_tensor):
    return swap(rows, "tensor", n_tensor, 2)


def chips(rows, n_tensor):
    return rows, other_chips(rows, n_tensor)


def split_at(*parts):
    (items,) = (p for p in parts if not isinstance(p, int))
    places = [0, *(p for p in parts if isinstance(p, int)), len(items)]
    return [items[start:end] for start, end in zip(places, places[1:])]


def per_device(n_dp, n_tensor, *args):
    (inputs, memory, counts, attn_gain, attn_shift, w_query, w_key, w_value, w_pos, bias_u, bias_v, w_out,
     ffn_gain, ffn_shift, w_up, up_bias, w_down, down_bias, out_grad) = args
    _, seq_len, width = inputs.shape
    mem_len = memory.shape[1]
    total = mem_len + seq_len
    wide = w_query.shape[1]
    heads = wide // HEAD
    ff = w_up.shape[1]
    chunk = seq_len // 2
    block = chunk // 2
    late = chunk
    place = PLACE
    x, mem, g = inputs[0], memory[0], out_grad[0]
    row = lambda v: v.reshape(1, -1)

    freq = 1.0 / 10000.0 ** (np.arange(0, width, 2, dtype=np.float64) / width)
    key_phase = np.arange(total)[:, None] * freq[None, :]
    table = jnp.asarray(np.concatenate([np.cos(key_phase), np.sin(key_phase)], axis=1).astype(BF))
    row_phase = (np.arange(seq_len) + mem_len)[:, None] * freq[None, :]
    sin = jnp.asarray(np.sin(row_phase).astype(np.float32))
    cos = jnp.asarray(np.cos(row_phase).astype(np.float32))

    outs_of = [w_out, cores(w_out, n_tensor), swap(w_out, "tensor", n_tensor, 2)]

    def attend_outs(seen):
        return [((heads, chunk, wide + width), BF), ((chunk, wide), BF), ((heads, chunk, seen), BF), ((chunk, wide), BF)]

    ctx_scr = pltpu.VMEM((block, wide), FL)
    vectors = [row(v) for v in (attn_shift, attn_gain, ffn_gain, ffn_shift, up_bias, down_bias)]
    copied = [
        *[(a.shape, BF) for a in (x, g)], ((width, 3 * wide), BF), *[(a.shape, BF) for a in (w_pos, w_up, w_down, w_out)],
        *[(a.shape, FL) for a in (*vectors, sin, cos)], ((2, wide), FL),
    ]
    found = call(
        functools.partial(front_kernel, block, heads),
        [*copied, ((total, width), BF), ((total, wide + width), BF), ((total, wide), BF)],
        (place, x, mem, g, w_query, w_key, w_value, w_pos, w_up, w_down, w_out, *vectors, bias_u, bias_v, table, sin,
         cos), "front", 1,
        [pltpu.VMEM(mem.shape, BF)] + [pltpu.VMEM(bias_u.shape, FL)] * 2 + [pltpu.SemaphoreType.DMA((21,))], pltpu.HBM,
    )
    x, g, weights, w_pos, w_up, w_down, w_out = found[:7]
    attn_shift, attn_gain, ffn_gain, ffn_shift, up_bias, down_bias, sin, cos, biases, normed, keys, values = found[7:]

    def attend_chunk(first, name, cost, after):
        return call(
            functools.partial(attend_kernel, first, block, heads, mem_len),
            attend_outs(mem_len + first + chunk),
            (counts, normed, keys, values, weights, w_pos, biases, sin, cos), name, cost, [ctx_scr], after=after,
        )

    saved_l = attend_chunk(late, "attend_late", 1, ())
    ctx_l = [saved_l[-1], cores(saved_l[-1], n_tensor), swap(saved_l[-1], "tensor", n_tensor, 2)]
    saved_e = attend_chunk(0, "attend_early", 5e9, outs_of[1:])
    ctx_e = [saved_e[-1], cores(saved_e[-1], n_tensor), swap(saved_e[-1], "tensor", n_tensor, 2)]
    (relay,) = call(
        relay_kernel, [((chunk + width, wide), BF)], (ctx_l[2], outs_of[2]), "relay_late", 1, after=saved_e[-1:]
    )
    relay = cores(relay, n_tensor)
    ctx_l.append(relay)
    outs_of.append(relay)
    half_outs = [
        ((block, width), FL), ((block, width), BF), ((block, ff), BF), ((block, ff), BF), ((2, width), FL),
        ((block, width), BF),
    ]

    def ffn_rows(first, ctx, roles, name, after=()):
        found = call(
            functools.partial(ffn_rows_kernel, first, block, roles), half_outs * len(roles),
            (place, x, *ctx, *outs_of, ffn_gain, ffn_shift, w_up, up_bias, w_down, g), name, 1, after=after,
        )
        return [found[i : i + 6] for i in range(0, 6 * len(roles), 6)]

    sum_outs = [((width, ff), FL), ((ff, width), FL), ((3, width), FL), ((1, ff), FL)]
    (send_l,) = ffn_rows(late, ctx_l, ("send",), "ffn_send_late")
    gnt_l = cores(send_l[-1], n_tensor)
    (keep_l,) = ffn_rows(late, ctx_l, ("keep",), "ffn_keep_late", after=send_l[-1:])
    (relay,) = work(place, [("copy", 0, ctx_e[2], ctx_e[2])], "relay_early", keep_l[-1:], 5e9)
    ctx_e.append(cores(relay, n_tensor))
    (gnt_l,) = work(place, [("sum", 0, keep_l[-1], gnt_l)], "add_late", (relay,))
    gnt_l = chips(gnt_l, n_tensor)
    shares_l, sums_l = split_at(2, call(
        functools.partial(ffn_late_kernel, late),
        [((block, width), BF)] * 2 + sum_outs, (place, g, w_down, *send_l[1:5], *keep_l[1:5]), "ffn_late", 1,
        after=gnt_l[:1],
    ))
    send_e, keep_e = ffn_rows(0, ctx_e, ("send", "keep"), "ffn_rows_early", after=sums_l[3:4])
    gnt_e = cores(send_e[-1], n_tensor)
    shares_e, halves, vecs = split_at(2, call(
        functools.partial(ffn_early_kernel, 0),
        [((block, width), BF)] * 2 + [((width // 2, ff), BF)] * 2 + [((ff // 2, width), BF)] * 2
        + [((3, width), FL), ((1, ff), FL)],
        (place, g, w_down, *send_e[1:5], *keep_e[1:5], *sums_l), "ffn_early", 1,
    ), 6)
    up_keep, up_send, down_keep, down_send = halves
    up_got = swap(up_send, "dp", n_dp, 1)
    down_got = swap(down_send, "dp", n_dp, 2)
    (gnt_l,) = work(place, [("sum", 0, *gnt_l)], "add_late_chips", (up_keep,), 5e9)
    gnt_l = (gnt_l, cores(gnt_l, n_tensor))
    (gnt_e,) = work(place, [("sum", 0, keep_e[-1], gnt_e)], "add_early", gnt_l[:1])
    gnt_e = chips(gnt_e, n_tensor)
    hidden_l, hidden_e = (send_l[0], keep_l[0]), (send_e[0], keep_e[0])

    sums = [((wide, total), FL), ((wide, total), FL), ((wide, width), FL), ((wide, width), FL), ((chunk, wide), BF)]
    turn_scr = [ctx_scr, ctx_scr]

    def back_args(hidden, gnt, saved):
        qb, qv, probs, ctx = saved
        return (place, *hidden, *gnt, g, ffn_gain, w_out, ctx, probs, qb, qv, keys, values, w_pos, sin, cos, weights)

    gh_l, dk, dv, dpos, dout, dq, bias, part = call(
        functools.partial(back_late_kernel, late, block, heads, mem_len),
        [((chunk, width), FL), *sums, ((2, wide), FL), ((chunk, width), BF)],
        back_args(hidden_l, gnt_l, saved_l), "back_late", 1, turn_scr,
    )
    gnt_e, up_keep, up_send, down_keep, down_send = work(
        place, [("sum", 0, *gnt_e), ("halve", 1, up_keep, up_got), ("halve", 0, down_keep, down_got)], "add_middle", (bias,)
    )
    up_got = swap(up_send, "dp", n_dp, 2)
    down_got = swap(down_send, "dp", n_dp, 1)
    gnt_e = (gnt_e, cores(gnt_e, n_tensor))
    size = 5 * wide // 8
    gh_e, dk, dv, dpos, dout, dq_e, bias = call(
        functools.partial(back_early_kernel, 0, block, heads, mem_len),
        [((chunk, width), FL), *sums, ((2, wide), FL)],
        (*back_args(hidden_e, gnt_e, saved_e)[:-1], dk, dv, dpos, dout, bias), "back_early", 1, turn_scr,
    )
    pieces = [((2 * (size + small), width), BF)] * 2 + [((2 * size, width), BF)] * 2
    keep, send, a_keep, a_send, b_keep, b_send, f_rows = call(
        functools.partial(back_end_kernel, 0, block, heads, mem_len, n_tensor, size),
        [*[((seq_len, width), BF)] * 2, *pieces, ((chunk // 2, width), BF)],
        (place, weights, normed, attn_shift, attn_gain, dk, dv, dpos, dout, dq_e, bias, dq, part, *vecs, *shares_e,
         *shares_l, up_keep, up_got, down_keep, down_got), "back_end", 1,
    )

    def pair(rows, bit):
        return swap(rows, "dp", n_dp, 1 << bit)

    bits = list(range((n_dp - 1).bit_length()))
    a_got, b_got = pair(a_send, 0), pair(b_send, 1)
    if len(bits) > 3:
        f_rows, f_send = work(place, [("halve", 2, f_rows, jnp.zeros_like(f_rows))], "halve_ffn")
    else:
        f_send = f_rows
    ffn = Chain(f_rows, f_send, bits[2:], n_dp, "two" if len(bits) == 3 else "sum")
    rows = (keep, cores(send, n_tensor))
    a_keep, a_send, b_keep, b_send, rows = work(
        place, [("halve", 1, a_keep, a_got), ("halve", 0, b_keep, b_got), ("sum", 0, *rows)], "step_0"
    )
    rows = (rows, other_chips(rows, n_tensor))
    while ffn.left() > 0:
        ffn.take(work(place, [ffn.job()], "step_ffn"))
    attn, *halves = work(
        place, [("pack", 0, a_keep, pair(a_send, 1), b_keep, pair(b_send, 0)), ffn.job()], "step_1"
    )
    up, down = halves if len(halves) == 2 else (halves[0][: chunk // 4], halves[0][chunk // 4 :])
    for bit in bits[2:-1]:
        (attn,) = work(place, [("sum", 0, attn, pair(attn, bit))], f"step_1_{bit}")
    a_rows, totals, b_rows, up, down = work(
        place,
        [("three", 0, attn, pair(attn, bits[-1])), ("join", 1, up, pair(up, 1)), ("join", 0, down, pair(down, 0))],
        "step_2", cost=STEP_COST,
    )
    a_rows, b_rows, up, down, chip_totals, summed = work(
        place,
        [("join", 1, a_rows, pair(a_rows, 1)), ("join", 0, b_rows, pair(b_rows, 0)), ("join", 0, up, pair(up, 0)),
         ("join", 1, down, pair(down, 1)), ("plus", 0, totals, cores(totals, n_tensor)), ("sum", 0, *rows)],
        "step_3",
    )
    rows = (summed, cores(summed, n_tensor))
    output, input_grad, g_up, g_down = call(
        functools.partial(finish_kernel, block), [(x.shape, BF)] * 2 + [((width, ff), FL), ((ff, width), FL)],
        (place, x, attn_gain, gh_e, gh_l, *hidden_e, *hidden_l, *rows, down_bias, up, down), "finish", 1,
        [pltpu.VMEM(x.shape, BF)] * 2 + [pltpu.VMEM((width, ff), FL), pltpu.VMEM((ff, width), FL),
                                         pltpu.SemaphoreType.DMA((10,))],
        after=(a_rows,), far=4,
    )
    output_there = pltpu.with_memory_space_constraint(output, pltpu.HBM)
    g_query, g_key, g_value, g_pos, g_out, *vecs = call(
        functools.partial(last_kernel, wide, heads),
        [((width, wide), FL)] * 4 + [((wide, width), FL)]
        + [((1, width), FL)] * 5 + [((heads, HEAD), FL)] * 2 + [((1, ff), FL)],
        (place, a_rows, pair(a_rows, 0), b_rows, pair(b_rows, 1), totals, *chips(chip_totals, n_tensor)), "last", 1,
        [pltpu.VMEM((5 * wide, width), FL), pltpu.VMEM((4, width, wide), FL), pltpu.SemaphoreType.DMA((5,))],
        after=(output_there,), far=5,
    )
    return (
        output[None],
        input_grad[None],
        vecs[0].reshape(-1),
        vecs[1].reshape(-1),
        g_query,
        g_key,
        g_value,
        g_pos,
        vecs[5],
        vecs[6],
        g_out,
        vecs[2].reshape(-1),
        vecs[3].reshape(-1),
        g_up,
        vecs[7].reshape(-1),
        g_down,
        vecs[4].reshape(-1),
    )


def solution(mesh):
    split, whole = P(None, "tensor"), P()
    return jax.shard_map(
        functools.partial(per_device, mesh.shape["dp"], mesh.shape["tensor"]),
        mesh=mesh,
        in_specs=(
            P("dp", None, None), P("dp", None, None), P("dp"), whole, whole, split, split, split, split,
            P("tensor", None), P("tensor", None), P("tensor", None), whole, whole, split, P("tensor"),
            P("tensor", None), whole, P("dp", None, None),
        ),
        out_specs=(
            P("dp", None, None), P("dp", None, None), whole, whole, split, split, split, split,
            P("tensor", None), P("tensor", None), P("tensor", None), whole, whole, split, P("tensor"),
            P("tensor", None), whole,
        ),
        check_vma=False,
    )
```
